128 devices in a mesh: seq: 64 (over y, x, z), head: 2 (over core).
Axes of the slice: x: 4, y: 4, z: 4, core: 2. Of those that a mesh axis runs over, the one named last changes fastest.
Arguments:
- query_key: bfloat16 [32768, 1024], P('seq', 'head'), may hold values from -160 to 160
- value: bfloat16 [32768, 1024], P('seq', 'head'), may hold values from -6 to 6
- attended_cotangent: bfloat16 [32768, 1024], P('seq', 'head'), may hold values from -6 to 6
- send_rows: int32 [2, 49152], P(None, 'seq'), may hold values from 0 to 511, as said below
- arrival_count: int32 [2, 4096], P(None, 'seq'), may hold values from 4 to 12, as said below
- receive_slot: int32 [2, 32768], P(None, 'seq'), may hold values from 0 to 511, as said below
Outputs:
- attended: bfloat16 [32768, 1024], P('seq', 'head')
- query_key_gradient: bfloat16 [32768, 1024], P('seq', 'head')
- value_gradient: bfloat16 [32768, 1024], P('seq', 'head')
The draws below stay inside these ranges and needn't reach their ends.
Inputs may be any that keep to these rules, and one draw needn't show every extreme that they name: `send_rows`: for each round and destination device d, the first n slots of the block d * 12 to d * 12 + 11 name the local rows sent to d, n being d's arrival_count for this device; every local row is sent once a round; the other slots name arbitrary local rows. `arrival_count`: the counts of a device, and the counts one source sends, sum to 512 in each round; in each round every source sends exactly 12 rows to one device, and every device sends the same numbers of rows in a drawn order of destinations. `receive_slot`: for each round and device, a permutation of the 512 arriving rows, counted in order of source device and then of slot.
All inputs are finite; a program needn't handle non-finite values.
Results may differ from the reference program's by a relative error of at most 0.006.
The reference program's roundings to bfloat16 on the way count: a program that leaves them out, or rounds other values in their place, can miss the bound.
Values may be sent and summed in bfloat16 or wider, within the bound.
No kernel may reach another device: no remote copies, remote signals or barrier semaphores. Data moves between devices by JAX's collectives and lax.ppermute only.
A program may use at most 128 MiB of HBM per device.

```python
import math
import jax
import jax.numpy as jnp
from jax import lax

D = 1024
HEADS = 8
DH = 128
ROUNDS = 2
GROUP = 256
TOK_DEV = 512
TOKENS = 32768
CAP = 12


def routing_tables(key, hash_round):
    owners = TOKENS // TOK_DEV
    mean_load = TOK_DEV // owners
    key = jax.random.fold_in(key, 100 + hash_round)
    streams = jax.random.split(key, 4)
    offsets = jax.random.permutation(streams[0], owners).astype(jnp.int32)
    swing = jax.random.randint(streams[1], (owners // 2,), 0, mean_load // 2 + 1).astype(jnp.int32)
    swing = swing.at[0].set(mean_load // 2)
    loads = jnp.concatenate([mean_load + swing, mean_load - swing]).astype(jnp.int32)
    sources = jnp.arange(owners, dtype=jnp.int32)
    targets = (sources[:, None] + offsets[None, :]) % owners
    counts = jnp.zeros((owners, owners), jnp.int32).at[sources[:, None], targets].set(jnp.broadcast_to(loads[None, :], (owners, owners)))
    starts = (jnp.cumsum(counts, axis=1) - counts).astype(jnp.int32)
    shuffled = jax.vmap(lambda stream: jax.random.permutation(stream, TOK_DEV))(jax.random.split(streams[2], owners)).astype(jnp.int32)
    positions = (starts[:, :, None] + jnp.arange(CAP, dtype=jnp.int32)[None, None, :]) % TOK_DEV
    rows_sent = jnp.take_along_axis(shuffled, positions.reshape(owners, owners * CAP), axis=1)
    arrivals = jax.vmap(lambda stream: jax.random.permutation(stream, TOK_DEV))(jax.random.split(streams[3], owners)).astype(jnp.int32)
    return (rows_sent.reshape(-1), counts.T.reshape(-1), arrivals.reshape(-1))


def all_tables(key):
    tables = [routing_tables(key, hash_round) for hash_round in range(ROUNDS)]
    return [jnp.stack([table[member] for table in tables]).astype(jnp.int32) for member in range(3)]


def draw_send_rows(key, part):
    return all_tables(key)[0]


def draw_arrival_count(key, part):
    return all_tables(key)[1]


def draw_receive_slot(key, part):
    return all_tables(key)[2]


def draw_query_key(key, part):
    key = jax.random.fold_in(key, 7)
    streams = jax.random.split(key, 3)
    base = jnp.clip(jax.random.normal(streams[0], (TOKENS, D), jnp.float32), -4.0, 4.0)
    row_scale = jnp.exp(jax.random.uniform(streams[1], (TOKENS, 1), jnp.float32, math.log(0.4), math.log(4.0)))
    col_scale = jnp.exp(jax.random.uniform(streams[2], (1, D), jnp.float32, math.log(0.5), math.log(5.0)))
    return (base * row_scale * col_scale).astype(jnp.bfloat16)


def levels(rng, extent, cuts, smallest, largest):
    factor_of = 1.0
    for position, parts in cuts:
        draws = jax.random.uniform(jax.random.fold_in(jax.random.fold_in(rng, 6), position), (parts,), jnp.float32, smallest / len(cuts), largest / len(cuts))
        factor_of = factor_of * jnp.repeat(jnp.exp(draws), extent[position] // parts).reshape((-1,) + (1,) * (len(extent) - 1 - position))
    return factor_of


def scatter_about(key, dims, deviation, most, cuts=(), kind=jnp.bfloat16):
    values = deviation * jax.random.normal(key, dims, jnp.float32)
    if cuts:
        values = values * levels(key, dims, cuts, -0.22, 0.18)
    return jnp.clip(values, -most, most).astype(kind)


def setup_inputs(seed: int = 0) -> dict:
    streams_of = jax.random.split(jax.random.key(seed), 7)
    return {
        "query_key": draw_query_key(jax.random.fold_in(streams_of[6], 71), 0),
        "value": scatter_about(streams_of[1], (TOKENS, D), 1.0, 6.0, ((0, 64), (1, 2))),
        "attended_cotangent": scatter_about(streams_of[2], (TOKENS, D), 1.0, 6.0, ((0, 64), (1, 2))),
        "send_rows": draw_send_rows(jax.random.fold_in(streams_of[6], 71), 0),
        "arrival_count": draw_arrival_count(jax.random.fold_in(streams_of[6], 71), 0),
        "receive_slot": draw_receive_slot(jax.random.fold_in(streams_of[6], 71), 0),
    }


NEG_SELF = -100000.0
EPS_KEY = 1e-06

def widened(values):
    return lax.optimization_barrier(values).astype(jnp.float32)

def unit_rows(raw_rows):
    wide_rows = raw_rows.astype(jnp.float32)
    inverse = lax.rsqrt(lax.optimization_barrier(jnp.sum(wide_rows * wide_rows, -1, keepdims=True)) + EPS_KEY)
    return (wide_rows * inverse, inverse)

def grouped(sorted_rows):
    return sorted_rows.reshape(-1, GROUP, sorted_rows.shape[-1])

def token_order(send_rows, arrival_count, receive_slot):
    owners = TOKENS // TOK_DEV
    counts = arrival_count.reshape(ROUNDS, owners, owners)
    inclusive = jnp.cumsum(counts, axis=2).astype(jnp.int32)
    exclusive = (inclusive - counts).astype(jnp.int32)
    target = jnp.arange(TOKENS, dtype=jnp.int32) // TOK_DEV
    bounds = inclusive[:, target, :]
    source = lax.optimization_barrier(jnp.sum((bounds <= receive_slot[:, :, None]).astype(jnp.int32), axis=2)).astype(jnp.int32)
    start = jnp.take_along_axis(exclusive[:, target, :], source[:, :, None], axis=2)[:, :, 0]
    within = (receive_slot - start).astype(jnp.int32)
    flat_slot = (source * (owners * CAP) + target[None, :] * CAP + within).astype(jnp.int32)
    local_row = jnp.take_along_axis(send_rows, flat_slot, axis=1)
    return (source * TOK_DEV + local_row).astype(jnp.int32)

def attention_pieces(query, value):
    unit, inverse = unit_rows(query)
    key_own = grouped(widened(unit.astype(jnp.bfloat16)))
    key_prior = jnp.roll(key_own, 1, axis=0)
    query_wide = grouped(query.astype(jnp.float32))
    value_own = grouped(value.astype(jnp.float32))
    value_prior = jnp.roll(value_own, 1, axis=0)
    self_mask = jnp.eye(GROUP, dtype=bool)[None]
    scores_own = jnp.where(self_mask, NEG_SELF, jnp.einsum('nqd,nkd->nqk', query_wide, key_own))
    scores_prior = jnp.einsum('nqd,nkd->nqk', query_wide, key_prior)
    return (unit, inverse, query_wide, key_own, key_prior, value_own, value_prior, scores_own, scores_prior)

def forward_head(query, value):
    unit, inverse, query_wide, key_own, key_prior, value_own, value_prior, scores_own, scores_prior = attention_pieces(query, value)
    row_top = jnp.maximum(scores_own.max(-1), scores_prior.max(-1))
    log_total = row_top + jnp.log(lax.optimization_barrier(jnp.sum(jnp.exp(scores_own - row_top[..., None]), -1)) + lax.optimization_barrier(jnp.sum(jnp.exp(scores_prior - row_top[..., None]), -1)))
    weights_own = widened(jnp.exp(scores_own - log_total[..., None]).astype(jnp.bfloat16))
    weights_prior = widened(jnp.exp(scores_prior - log_total[..., None]).astype(jnp.bfloat16))
    partial_value = jnp.einsum('nqk,nkd->nqd', weights_own, value_own) + jnp.einsum('nqk,nkd->nqd', weights_prior, value_prior)
    return (partial_value.reshape(-1, DH), log_total.reshape(-1))

def backward_head(query, value, upstream, total_lse, delta):
    unit, inverse, query_wide, key_own, key_prior, value_own, value_prior, scores_own, scores_prior = attention_pieces(query, value)
    upstream_wide = grouped(upstream.astype(jnp.float32))
    lse_rows = total_lse.reshape(-1, GROUP, 1)
    delta_rows = delta.reshape(-1, GROUP, 1)
    probs_own = jnp.exp(scores_own - lse_rows)
    probs_prior = jnp.exp(scores_prior - lse_rows)
    value_own_slope = jnp.einsum('nqk,nqd->nkd', widened(probs_own.astype(jnp.bfloat16)), upstream_wide)
    value_prior_slope = jnp.einsum('nqk,nqd->nkd', widened(probs_prior.astype(jnp.bfloat16)), upstream_wide)
    dots_own = jnp.einsum('nqd,nkd->nqk', upstream_wide, value_own)
    dots_prior = jnp.einsum('nqd,nkd->nqk', upstream_wide, value_prior)
    slopes_own = widened((probs_own * (dots_own - delta_rows)).astype(jnp.bfloat16))
    slopes_prior = widened((probs_prior * (dots_prior - delta_rows)).astype(jnp.bfloat16))
    query_slope = jnp.einsum('nqk,nkd->nqd', slopes_own, key_own) + jnp.einsum('nqk,nkd->nqd', slopes_prior, key_prior)
    unit_slope = jnp.einsum('nqk,nqd->nkd', slopes_own, query_wide) + jnp.roll(jnp.einsum('nqk,nqd->nkd', slopes_prior, query_wide), -1, axis=0)
    value_slope = value_own_slope + jnp.roll(value_prior_slope, -1, axis=0)
    unit_slope = unit_slope.reshape(-1, DH)
    key_slope = inverse * (unit_slope - unit * lax.optimization_barrier(jnp.sum(unit * unit_slope, -1, keepdims=True)))
    return (query_slope.reshape(-1, DH) + key_slope, value_slope.reshape(-1, DH))

def reference(query_key, value, attended_cotangent, send_rows, arrival_count, receive_slot):
    order = token_order(send_rows, arrival_count, receive_slot)
    round_out = []
    round_lse = []
    for hash_round in range(ROUNDS):
        token_rows = order[hash_round]
        head_out = []
        head_lse = []
        for head_index in range(HEADS):
            columns = slice(head_index * DH, (head_index + 1) * DH)
            partial_value, log_total = forward_head(query_key[token_rows, columns], value[token_rows, columns])
            head_out.append(partial_value)
            head_lse.append(log_total)
        sorted_out = jnp.stack(head_out, 1)
        sorted_lse = jnp.stack(head_lse, 1)
        round_out.append(jnp.zeros_like(sorted_out).at[token_rows].set(sorted_out))
        round_lse.append(jnp.zeros_like(sorted_lse).at[token_rows].set(sorted_lse))
    stacked_lse = jnp.stack(round_lse)
    stacked_out = jnp.stack(round_out)
    round_top = lax.optimization_barrier(jnp.max(stacked_lse, axis=0))
    total_lse = round_top + jnp.log(lax.optimization_barrier(jnp.sum(jnp.exp(stacked_lse - round_top), axis=0)))
    shares = jnp.exp(stacked_lse - total_lse)
    combined = lax.optimization_barrier(jnp.sum(shares[..., None] * stacked_out, axis=0))
    attended = combined.reshape(TOKENS, D).astype(jnp.bfloat16)
    upstream = attended_cotangent.reshape(TOKENS, HEADS, DH).astype(jnp.float32)
    delta = lax.optimization_barrier(jnp.sum(upstream * combined, -1))
    key_total = jnp.zeros((TOKENS, HEADS, DH), jnp.float32)
    value_total = jnp.zeros((TOKENS, HEADS, DH), jnp.float32)
    for hash_round in range(ROUNDS):
        token_rows = order[hash_round]
        head_key = []
        head_value = []
        for head_index in range(HEADS):
            columns = slice(head_index * DH, (head_index + 1) * DH)
            key_part, value_part = backward_head(query_key[token_rows, columns], value[token_rows, columns], attended_cotangent[token_rows, columns], total_lse[token_rows, head_index], delta[token_rows, head_index])
            head_key.append(key_part)
            head_value.append(value_part)
        key_total = key_total.at[token_rows].add(jnp.stack(head_key, 1))
        value_total = value_total.at[token_rows].add(jnp.stack(head_value, 1))
    return (attended, key_total.reshape(TOKENS, D).astype(jnp.bfloat16), value_total.reshape(TOKENS, D).astype(jnp.bfloat16))
```

```python
import functools

import jax
import jax.numpy as jnp
from jax import lax
from jax.experimental import pallas as pl
from jax.experimental.pallas import tpu as pltpu
from jax.sharding import PartitionSpec as P

DH = 128
GROUP = 256
NEG_SELF = -100000.0
EPS_KEY = 1e-06
LANES = 128
STAT = 8
PIECES = 3
MIB = 1 << 20


def dot(left, right, left_axis=1, right_axis=0):
    return lax.dot_general(
        left,
        right,
        (((left_axis,), (right_axis,)), ((), ())),
        preferred_element_type=jnp.float32,
    )


def params(mib=40):
    return pltpu.CompilerParams(vmem_limit_bytes=mib * MIB)


def cost(flops, moved, exps=0):
    return pl.CostEstimate(flops=int(flops), bytes_accessed=int(moved), transcendentals=int(exps))


def shifted(block, axis, distance):
    devices = range(lax.axis_size(axis))
    route = [((i - distance) % len(devices), i) for i in devices]
    return lax.ppermute(block, axis, route)


def exchange(block):
    return lax.all_to_all(block, "seq", split_axis=0, concat_axis=0, tiled=True)


def match(left, right):
    return jnp.where(left == right, 1.0, 0.0).astype(jnp.bfloat16)


def iota(shape, axis):
    return lax.broadcasted_iota(jnp.int32, shape, axis)


def pieces_of(wide):
    first = wide.astype(jnp.bfloat16)
    rest = wide - first.astype(jnp.float32)
    second = rest.astype(jnp.bfloat16)
    third = (rest - second.astype(jnp.float32)).astype(jnp.bfloat16)
    return first, second, third


def unit_rows(raw_rows):
    wide = raw_rows.astype(jnp.float32)
    inverse = lax.rsqrt(jnp.sum(wide * wide, -1, keepdims=True) + EPS_KEY)
    return wide * inverse, inverse


def pack_body(index_ref, *refs):
    sources, out_ref = refs[:-1], refs[-1]
    tokens, width = sources[0].shape
    chosen = match(index_ref[...], iota((out_ref.shape[0], tokens), 1))
    for place, source in enumerate(sources):
        out_ref[:, place * width : (place + 1) * width] = dot(chosen, source[...]).astype(
            jnp.bfloat16
        )


def pack(index_col, *sources):
    slots = index_col.shape[0]
    tokens, width = sources[0].shape
    block = slots // 6
    total = width * len(sources)
    return pl.pallas_call(
        pack_body,
        grid=(6,),
        in_specs=[pl.BlockSpec((block, 1), lambda i: (i, 0))]
        + [pl.BlockSpec((tokens, width), lambda i: (0, 0)) for _ in sources],
        out_specs=pl.BlockSpec((block, total), lambda i: (i, 0)),
        out_shape=jax.ShapeDtypeStruct((slots, total), jnp.bfloat16),
        compiler_params=params(),
        cost_estimate=cost(2 * slots * tokens * total, 2 * (slots + tokens) * total),
        name="pack_rows",
    )(index_col, *sources)


def sort_body(place_col_ref, arrival_row_ref, arrived_ref, sorted_ref, tail_ref, head_ref, chosen):
    step = pl.program_id(0)

    @pl.when(step == 0)
    def _():
        chosen[...] = match(place_col_ref[...], arrival_row_ref[...])

    rows = dot(chosen[...], arrived_ref[...]).astype(jnp.bfloat16)
    sorted_ref[...] = rows
    half = rows.shape[0] // 2
    tail_ref[:GROUP, :] = rows[half - GROUP : half]
    tail_ref[GROUP:, :] = rows[2 * half - GROUP :]

    @pl.when(step < 2)
    def _():
        head_ref[:GROUP, :] = rows[:GROUP]
        head_ref[GROUP:, :] = rows[half : half + GROUP]


def sort_rows(place_col, arrival_row, arrived):
    slots, width = arrived.shape
    rows = place_col.shape[0]
    wide = width // 4
    return pl.pallas_call(
        sort_body,
        grid=(4,),
        in_specs=[
            pl.BlockSpec((rows, 1), lambda i: (0, 0)),
            pl.BlockSpec((1, slots), lambda i: (0, 0)),
            pl.BlockSpec((slots, wide), lambda i: (0, i)),
        ],
        out_specs=[
            pl.BlockSpec((rows, wide), lambda i: (0, i)),
            pl.BlockSpec((2 * GROUP, wide), lambda i: (0, i)),
            pl.BlockSpec((2 * GROUP, wide), lambda i: (0, jnp.minimum(i, 1))),
        ],
        out_shape=[
            jax.ShapeDtypeStruct((rows, width), jnp.bfloat16),
            jax.ShapeDtypeStruct((2 * GROUP, width), jnp.bfloat16),
            jax.ShapeDtypeStruct((2 * GROUP, width // 2), jnp.bfloat16),
        ],
        scratch_shapes=[pltpu.VMEM((rows, slots), jnp.bfloat16)],
        compiler_params=params(),
        cost_estimate=cost(2 * slots * rows * width, 2 * (slots + 2 * rows) * width),
        name="sort_rows",
    )(place_col, arrival_row, arrived)


def forward_tile(query, keys, values):
    scores = dot(query, keys, 1, 1)
    own = iota((GROUP, 2 * GROUP), 1) == iota((GROUP, 2 * GROUP), 0) + GROUP
    scores = jnp.where(own, NEG_SELF, scores)
    top = jnp.max(scores, -1, keepdims=True)
    raised = jnp.exp(scores - top)
    total = jnp.sum(raised, -1, keepdims=True)
    weights = (raised * (1.0 / total)).astype(jnp.bfloat16)
    return dot(weights, values), top + jnp.log(total)


def forward_body(with_edge, *refs):
    if with_edge:
        query_ref, value_ref, tail_query_ref, tail_value_ref, out_ref, lse_ref = refs
    else:
        query_ref, value_ref, out_ref, lse_ref = refs
    pair = pl.program_id(1)
    lane = iota((GROUP, LANES), 1) % STAT

    for local in range(2):
        columns = slice(local * DH, (local + 1) * DH)
        if with_edge:
            raw = jnp.concatenate([tail_query_ref[:, columns], query_ref[:GROUP, columns]])
            values = jnp.concatenate([tail_value_ref[:, columns], value_ref[:GROUP, columns]])
            query = query_ref[:GROUP, columns]
        else:
            raw = query_ref[:, columns]
            values = value_ref[:, columns]
            query = query_ref[GROUP:, columns]
        keys = unit_rows(raw)[0].astype(jnp.bfloat16)
        partial, lse = forward_tile(query, keys, values)
        out_ref[:, columns] = partial
        at_head = lane == pair * 2 + local
        if local == 0:
            before = jnp.where(pair == 0, jnp.zeros((GROUP, LANES), jnp.float32), lse_ref[...])
        else:
            before = lse_ref[...]
        lse_ref[...] = jnp.where(at_head, lse, before)


def forward(rows_sorted, tail=None):
    with_edge = tail is not None
    rows, width = rows_sorted.shape
    per_round = rows // 2
    wide = 2 * DH
    in_specs = [
        pl.BlockSpec((per_round, wide), lambda r, p: (r, p)),
        pl.BlockSpec((per_round, wide), lambda r, p: (r, p + 2)),
    ]
    arguments = [rows_sorted, rows_sorted]
    if with_edge:
        in_specs += [
            pl.BlockSpec((GROUP, wide), lambda r, p: (r, p)),
            pl.BlockSpec((GROUP, wide), lambda r, p: (r, p + 2)),
        ]
        arguments += [tail, tail]
    return pl.pallas_call(
        functools.partial(forward_body, with_edge),
        grid=(2, 2),
        in_specs=in_specs,
        out_specs=[
            pl.BlockSpec((GROUP, wide), lambda r, p: (r, p)),
            pl.BlockSpec((GROUP, LANES), lambda r, p: (r, 0)),
        ],
        out_shape=[
            jax.ShapeDtypeStruct((2 * GROUP, width // 2), jnp.float32),
            jax.ShapeDtypeStruct((2 * GROUP, LANES), jnp.float32),
        ],
        compiler_params=params(),
        cost_estimate=cost(8 * 4 * GROUP * 2 * GROUP * DH, 4 * rows * width, 8 * GROUP * 512),
        name="forward_edge" if with_edge else "forward_own",
    )(*arguments)


def stats_body(
    place_col_ref,
    place_row_ref,
    arrival_row_ref,
    arrival_col_ref,
    arrived_ref,
    out_first_ref,
    out_second_ref,
    lse_first_ref,
    lse_second_ref,
    sorted_ref,
    head_ref,
    stats_ref,
):
    rows = place_col_ref.shape[0]
    per_round = rows // 2
    chosen = match(place_col_ref[...], arrival_row_ref[...])
    cotangent = dot(chosen, arrived_ref[...]).astype(jnp.bfloat16)
    sorted_ref[...] = cotangent
    lane = iota((GROUP, LANES), 1)
    parts = []
    for hash_round in range(2):
        kept = slice(hash_round * GROUP, (hash_round + 1) * GROUP)
        head_ref[kept, :] = cotangent[hash_round * per_round : hash_round * per_round + GROUP]
        for group, (out_ref, lse_ref) in enumerate(
            ((out_first_ref, lse_first_ref), (out_second_ref, lse_second_ref))
        ):
            start = hash_round * per_round + group * GROUP
            wide = cotangent[start : start + GROUP].astype(jnp.float32)
            product = wide * out_ref[kept, :]
            stat = lse_ref[kept, :]
            for head in range(4):
                own = jnp.sum(product[:, head * DH : (head + 1) * DH], -1, keepdims=True)
                stat = jnp.where(lane % STAT == 4 + head, own, stat)
            first, second, third = pieces_of(stat)
            piece = lane // (PIECES * STAT)
            parts.append(
                jnp.where(
                    piece == 0,
                    first.astype(jnp.float32),
                    jnp.where(
                        piece == 1,
                        second.astype(jnp.float32),
                        jnp.where(piece == 2, third.astype(jnp.float32), 0.0),
                    ),
                ).astype(jnp.bfloat16)
            )
    stats = jnp.concatenate(parts)
    third_slots = arrival_col_ref.shape[0] // 3
    lane_third = (iota((third_slots, LANES), 1) % (3 * STAT)) // STAT
    result = jnp.zeros((third_slots, LANES), jnp.float32)
    for third in range(3):
        back = match(
            arrival_col_ref[third * third_slots : (third + 1) * third_slots], place_row_ref[...]
        )
        result = jnp.where(lane_third == third, dot(back, stats), result)
    stats_ref[...] = result


def stats_out(place_col, place_row, arrival_row, arrival_col3, arrived, outs, lses):
    slots, width = arrived.shape
    rows = place_col.shape[0]
    return pl.pallas_call(
        stats_body,
        out_shape=[
            jax.ShapeDtypeStruct((rows, width), jnp.bfloat16),
            jax.ShapeDtypeStruct((2 * GROUP, width), jnp.bfloat16),
            jax.ShapeDtypeStruct((slots // 3, LANES), jnp.float32),
        ],
        compiler_params=params(),
        cost_estimate=cost(2 * slots * rows * (width + LANES), 4 * slots * width),
        name="cotangent_and_stats",
    )(place_col, place_row, arrival_row, arrival_col3, arrived, *outs, *lses)


def gather_stats(codes_row, per_slot_codes, stats):
    third_slots = stats.shape[0]
    narrow = stats.astype(jnp.bfloat16)
    total = None
    for third in range(3):
        chosen = match(per_slot_codes[third * third_slots : (third + 1) * third_slots], codes_row)
        found = dot(narrow, chosen, 0, 0)
        for piece in range(PIECES):
            at = piece * PIECES * STAT + third * STAT
            part = found[at : at + STAT]
            total = part if total is None else total + part
    return total


def total_body(tokens, slot_code_ref, arrived_ref, out_ref):
    slots = slot_code_ref.shape[0]
    found = gather_stats(iota((1, 2 * tokens), 1), slot_code_ref[...], arrived_ref[...])
    lse_first, lse_second = found[:4, :tokens], found[:4, tokens:]
    delta_first, delta_second = found[4:, :tokens], found[4:, tokens:]
    top = jnp.maximum(lse_first, lse_second)
    total = top + jnp.log(jnp.exp(lse_first - top) + jnp.exp(lse_second - top))
    delta = delta_first * jnp.exp(lse_first - total) + delta_second * jnp.exp(lse_second - total)
    stat = jnp.concatenate([total, delta])
    first, second, third_piece = [member.astype(jnp.float32) for member in pieces_of(stat)]
    spare = jnp.zeros((LANES - 9 * STAT, tokens), jnp.float32)
    table = jnp.concatenate(
        [first] * 3 + [second] * 3 + [third_piece] * 3 + [spare]
    ).astype(jnp.bfloat16)
    third_slots = slots // 3
    lane_third = (iota((third_slots, LANES), 1) % (3 * STAT)) // STAT
    result = jnp.zeros((third_slots, LANES), jnp.float32)
    for third in range(3):
        code = slot_code_ref[third * third_slots : (third + 1) * third_slots]
        row = jnp.where(code >= tokens, code - tokens, code)
        chosen = match(row, iota((third_slots, tokens), 1))
        result = jnp.where(lane_third == third, dot(chosen, table, 1, 1), result)
    owners = third_slots // STAT
    by_owner = result.reshape(owners, STAT, LANES)
    out_ref[:, :STAT, :] = by_owner
    out_ref[: owners - 1, STAT:, :] = by_owner[1:]
    out_ref[owners - 1 :, STAT:, :] = by_owner[:1]


def total_stats(slot_code, arrived, tokens):
    owners = arrived.shape[0] // STAT
    return pl.pallas_call(
        functools.partial(total_body, tokens),
        out_shape=jax.ShapeDtypeStruct((owners, 2 * STAT, LANES), jnp.float32),
        compiler_params=params(),
        cost_estimate=cost(2 * 1536 * 1536 * LANES, 1 << 20),
        name="total_stats",
    )(slot_code, arrived)


def backward_tile(query, upstream, keys, values, masked, total_row, delta_row):
    scores = dot(keys, query, 1, 1)
    if masked is not None:
        scores = jnp.where(masked, NEG_SELF, scores)
    probs = jnp.exp(scores - total_row)
    dots = dot(values, upstream, 1, 1)
    slopes = (probs * (dots - delta_row)).astype(jnp.bfloat16)
    return probs.astype(jnp.bfloat16), slopes


def backward_body(
    place_row_ref,
    next_row_ref,
    arrival_col_ref,
    arrival_col3_ref,
    next_col3_ref,
    stats_ref,
    query_ref,
    value_ref,
    cotangent_ref,
    tail_query_ref,
    tail_value_ref,
    next_query_ref,
    next_cotangent_ref,
    out_first_ref,
    out_second_ref,
    lse_first_ref,
    lse_second_ref,
    payload_ref,
    back,
    totals,
    next_totals,
    total_cols,
    shaped,
):
    pair = pl.program_id(0)
    hash_round = pl.program_id(1)
    rows = place_row_ref.shape[1]
    per_round = rows // 2

    @pl.when((pair == 0) & (hash_round == 0))
    def _():
        back[...] = match(arrival_col_ref[...], place_row_ref[...])
        own_stats = stats_ref[:, :STAT, :].reshape(-1, LANES)
        next_stats = stats_ref[:, STAT:, :].reshape(-1, LANES)
        found = gather_stats(place_row_ref[...], arrival_col3_ref[...], own_stats)
        edge = gather_stats(next_row_ref[...], next_col3_ref[...], next_stats)
        for each in range(2):
            totals[each] = found[:, each * per_round : (each + 1) * per_round]
            next_totals[each] = edge[:, each * GROUP : (each + 1) * GROUP]
        padded = jnp.concatenate([found, jnp.zeros((LANES - STAT, rows), jnp.float32)])
        total_cols[...] = padded.T.reshape(2, per_round, LANES)

    own = iota((2 * GROUP, GROUP), 0) == iota((2 * GROUP, GROUP), 1) + GROUP
    stat = totals[hash_round]
    edge_stat = next_totals[hash_round]
    columns_of_stat = total_cols[hash_round]
    sublane = iota((STAT, 1), 0)
    lane = iota((1, LANES), 1)

    def row_of(table, index):
        return jnp.sum(jnp.where(sublane == index, table, 0.0), 0, keepdims=True)

    def col_of(table, index):
        return jnp.sum(jnp.where(lane == index, table, 0.0), 1, keepdims=True)

    for local in range(2):
        columns = slice(local * DH, (local + 1) * DH)
        head = pair * 2 + local
        total_row, delta_row = row_of(stat, head), row_of(stat, head + 4)
        edge_total, edge_delta = row_of(edge_stat, head), row_of(edge_stat, head + 4)
        raw = query_ref[:, columns]
        values = value_ref[:, columns]
        upstream = cotangent_ref[:, columns]
        units, inverse = unit_rows(raw)
        keys = units.astype(jnp.bfloat16)
        tail_keys = unit_rows(tail_query_ref[:, columns])[0].astype(jnp.bfloat16)

        keys_first = jnp.concatenate([tail_keys, keys[:GROUP]])
        values_first = jnp.concatenate([tail_value_ref[:, columns], values[:GROUP]])
        probs, slopes = backward_tile(
            raw[:GROUP],
            upstream[:GROUP],
            keys_first,
            values_first,
            own,
            total_row[:, :GROUP],
            delta_row[:, :GROUP],
        )
        query_first = dot(slopes, keys_first, 0, 0)
        unit_first = dot(slopes[GROUP:], raw[:GROUP])
        value_first = dot(probs[GROUP:], upstream[:GROUP])

        probs, slopes = backward_tile(
            raw[GROUP:],
            upstream[GROUP:],
            keys,
            values,
            own,
            total_row[:, GROUP:],
            delta_row[:, GROUP:],
        )
        query_second = dot(slopes, keys, 0, 0)
        unit_both = dot(slopes, raw[GROUP:])
        value_both = dot(probs, upstream[GROUP:])

        next_query = next_query_ref[:, columns]
        next_upstream = next_cotangent_ref[:, columns]
        probs, slopes = backward_tile(
            next_query,
            next_upstream,
            keys[GROUP:],
            values[GROUP:],
            None,
            edge_total,
            edge_delta,
        )
        unit_last = dot(slopes, next_query)
        value_last = dot(probs, next_upstream)

        for group, (query_slope, unit_slope, value_slope, out_ref, lse_ref) in enumerate(
            (
                (
                    query_first,
                    unit_first + unit_both[:GROUP],
                    value_first + value_both[:GROUP],
                    out_first_ref,
                    lse_first_ref,
                ),
                (
                    query_second,
                    unit_both[GROUP:] + unit_last,
                    value_both[GROUP:] + value_last,
                    out_second_ref,
                    lse_second_ref,
                ),
            )
        ):
            kept = slice(group * GROUP, (group + 1) * GROUP)
            unit = units[kept]
            key_slope = inverse[kept] * (
                unit_slope - unit * jnp.sum(unit * unit_slope, -1, keepdims=True)
            )
            share = jnp.exp(col_of(lse_ref[...] - columns_of_stat[kept], head))
            wide = 2 * DH
            shaped[kept, columns] = (out_ref[:, columns] * share).astype(jnp.bfloat16)
            shaped[kept, wide + local * DH : wide + (local + 1) * DH] = (
                query_slope + key_slope
            ).astype(jnp.bfloat16)
            shaped[kept, 2 * wide + local * DH : 2 * wide + (local + 1) * DH] = (
                value_slope.astype(jnp.bfloat16)
            )

    @pl.when(hash_round == 0)
    def _():
        payload_ref[...] = dot(back[:, :per_round], shaped[...]).astype(jnp.bfloat16)

    @pl.when(hash_round == 1)
    def _():
        payload_ref[...] += dot(back[:, per_round:], shaped[...]).astype(jnp.bfloat16)


def backward(index, stats, rows_sorted, cotangent, tail, next_query, next_cotangent, outs, lses):
    rows, width = rows_sorted.shape
    per_round = rows // 2
    slots = index["arrival_col"].shape[0]
    wide = 2 * DH

    def whole(array):
        return pl.BlockSpec(array.shape, lambda p, r: (0,) * array.ndim)

    small = [
        index["place_row"],
        index["next_row"],
        index["arrival_col"],
        index["arrival_col3"],
        index["next_col3"],
        stats,
    ]
    group_spec = pl.BlockSpec((GROUP, wide), lambda p, r: (r, p))
    lse_spec = pl.BlockSpec((GROUP, LANES), lambda p, r: (r, 0))
    return pl.pallas_call(
        backward_body,
        grid=(2, 2),
        in_specs=[whole(array) for array in small]
        + [
            pl.BlockSpec((per_round, wide), lambda p, r: (r, p)),
            pl.BlockSpec((per_round, wide), lambda p, r: (r, p + 2)),
            pl.BlockSpec((per_round, wide), lambda p, r: (r, p)),
            group_spec,
            pl.BlockSpec((GROUP, wide), lambda p, r: (r, p + 2)),
            group_spec,
            group_spec,
            group_spec,
            group_spec,
            lse_spec,
            lse_spec,
        ],
        out_specs=pl.BlockSpec((slots, 3 * wide), lambda p, r: (0, p)),
        out_shape=jax.ShapeDtypeStruct((slots, 6 * wide), jnp.bfloat16),
        scratch_shapes=[
            pltpu.VMEM((slots, rows), jnp.bfloat16),
            pltpu.VMEM((2, STAT, per_round), jnp.float32),
            pltpu.VMEM((2, STAT, GROUP), jnp.float32),
            pltpu.VMEM((2, per_round, LANES), jnp.float32),
            pltpu.VMEM((per_round, 3 * wide), jnp.bfloat16),
        ],
        compiler_params=params(),
        cost_estimate=cost(8e9, 1.5e7, 3e6),
        name="backward",
    )(
        *small,
        rows_sorted,
        rows_sorted,
        cotangent,
        tail,
        tail,
        next_query,
        next_cotangent,
        *outs,
        *lses,
    )


def combine_body(index_row_ref, arrived_ref, *out_refs):
    tokens, wide = out_refs[0].shape
    chosen = match(iota((tokens, 1), 0), index_row_ref[...])
    found = dot(chosen, arrived_ref[...])
    for place, out_ref in enumerate(out_refs):
        out_ref[...] = found[:, place * wide : (place + 1) * wide].astype(jnp.bfloat16)


def combine(index_row, arrived, tokens):
    slots, width = arrived.shape
    wide = width // 6
    return pl.pallas_call(
        combine_body,
        grid=(2,),
        in_specs=[
            pl.BlockSpec((1, slots), lambda i: (0, 0)),
            pl.BlockSpec((slots, 3 * wide), lambda i: (0, i)),
        ],
        out_specs=[pl.BlockSpec((tokens, wide), lambda i: (0, i))] * 3,
        out_shape=[jax.ShapeDtypeStruct((tokens, 2 * wide), jnp.bfloat16)] * 3,
        compiler_params=params(),
        cost_estimate=cost(2 * slots * tokens * width, 2 * (slots + tokens) * width),
        name="combine_rows",
    )(index_row, arrived)


def per_device(query_key, value, attended_cotangent, send_rows, arrival_count, receive_slot):
    tokens, row_width = query_key.shape
    rounds = send_rows.shape[0]
    owners = lax.axis_size("seq")
    capacity = send_rows.shape[1] // owners
    per_owner = rounds * capacity
    slots = owners * per_owner

    code = (tokens * jnp.arange(rounds, dtype=jnp.int32))[:, None]

    def by_owner(table):
        return table.reshape(rounds, owners, capacity).transpose(1, 0, 2).reshape(owners, per_owner)

    def by_third(table):
        return table.reshape(owners, 3, STAT).transpose(1, 0, 2).reshape(slots, 1)

    send = by_owner(send_rows)
    send_code = by_owner(send_rows + code)
    running = jnp.cumsum(arrival_count, axis=1)
    within = jnp.arange(capacity, dtype=jnp.int32)
    arrival = (running - arrival_count + code)[:, :, None] + within
    arrival = by_owner(jnp.where(within < arrival_count[:, :, None], arrival, -1))
    place = receive_slot + code
    next_arrival = shifted(arrival, "seq", -1)
    next_place = shifted(place[:, :GROUP], "seq", -1)

    index = {
        "place_row": place.reshape(1, -1),
        "place_col": place.reshape(-1, 1),
        "arrival_row": arrival.reshape(1, slots),
        "arrival_col": arrival.reshape(slots, 1),
        "arrival_col3": by_third(arrival),
        "next_row": next_place.reshape(1, -1),
        "next_col3": by_third(next_arrival),
    }

    def sent(packed):
        return exchange(packed.reshape(owners, per_owner, -1)).reshape(slots, -1)

    send_col = send.reshape(slots, 1)
    arrived = sent(pack(send_col, query_key, value))
    rows_sorted, tail, head_query = sort_rows(index["place_col"], index["arrival_row"], arrived)
    arrived_cotangent = sent(pack(send_col, attended_cotangent))
    prior_tail = shifted(tail, "seq", 1)
    next_query = shifted(head_query, "seq", -1)
    out_second, lse_second = forward(rows_sorted)
    out_first, lse_first = forward(rows_sorted, prior_tail)
    outs, lses = (out_first, out_second), (lse_first, lse_second)
    cotangent, head_cotangent, stats = stats_out(
        index["place_col"],
        index["place_row"],
        index["arrival_row"],
        index["arrival_col3"],
        arrived_cotangent,
        outs,
        lses,
    )
    next_cotangent = shifted(head_cotangent, "seq", -1)
    home_stats = exchange(stats.reshape(owners, STAT, LANES)).reshape(-1, LANES)
    totals = exchange(total_stats(by_third(send_code), home_stats, tokens))
    payload = backward(
        index,
        totals,
        rows_sorted,
        cotangent,
        prior_tail,
        next_query,
        next_cotangent,
        outs,
        lses,
    )
    return tuple(combine(send.reshape(1, slots), sent(payload), tokens))


def solution(mesh):
    in_specs = (
        P("seq", "head"),
        P("seq", "head"),
        P("seq", "head"),
        P(None, "seq"),
        P(None, "seq"),
        P(None, "seq"),
    )
    out_specs = (P("seq", "head"), P("seq", "head"), P("seq", "head"))
    return jax.shard_map(
        per_device, mesh=mesh, in_specs=in_specs, out_specs=out_specs, check_vma=False
    )
```

```python
import functools

import jax
import jax.numpy as jnp
from jax import lax
from jax.experimental import pallas as pl
from jax.experimental.pallas import tpu as pltpu
from jax.sharding import PartitionSpec as P

DH = 128
GROUP = 256
NEG_SELF = -100000.0
EPS_KEY = 1e-06
LANES = 128
STAT = 8
PIECES = 3
MIB = 1 << 20


def dot(left, right, left_axis=1, right_axis=0):
    return lax.dot_general(
        left,
        right,
        (((left_axis,), (right_axis,)), ((), ())),
        preferred_element_type=jnp.float32,
    )


def params(mib=62):
    return pltpu.CompilerParams(vmem_limit_bytes=mib * MIB)


def cost(flops, moved, exps=0):
    return pl.CostEstimate(flops=int(flops), bytes_accessed=int(moved), transcendentals=int(exps))


def routed(block, route_of):
    owners, halves = lax.axis_size("seq"), lax.axis_size("head")
    route = [
        (i * halves + half, route_of(i, half, owners) * halves + half)
        for i in range(owners)
        for half in range(halves)
    ]
    return lax.ppermute(block, ("seq", "head"), route)


def to_next(block):
    return routed(block, lambda i, half, n: (i + (1 if half == 0 else -1)) % n)


def to_prior(block):
    return routed(block, lambda i, half, n: (i - (1 if half == 0 else -1)) % n)


def to_place(block):
    return routed(block, lambda i, half, n: i if half == 0 else n - 1 - i)


def exchange(block):
    return lax.all_to_all(block, "seq", split_axis=0, concat_axis=0, tiled=True)


def match(left, right):
    return jnp.where(left == right, 1.0, 0.0).astype(jnp.bfloat16)


ARRIVAL, ARRIVAL3, NEXT3, PLACE, NEXT_PLACE, SEND, SEND3, HALF = 0, 16, 32, 48, 56, 64, 80, 96
SLOT_ROWS, PLACE_ROWS, NEXT_ROWS = 12, 8, 4


def table_row(table_ref, start, count):
    return jnp.concatenate([table_ref[start + i : start + i + 1, :] for i in range(count)], axis=1)


def table_cols(table_ref, start, count):
    turned = table_ref[...].T
    return [turned[:, start + i : start + i + 1] for i in range(count)]


def match_cols(cols, row):
    return jnp.concatenate([match(col, row) for col in cols])


def iota(shape, axis):
    return lax.broadcasted_iota(jnp.int32, shape, axis)


def pieces_of(wide):
    first = wide.astype(jnp.bfloat16)
    rest = wide - first.astype(jnp.float32)
    second = rest.astype(jnp.bfloat16)
    third = (rest - second.astype(jnp.float32)).astype(jnp.bfloat16)
    return first, second, third


def unit_rows(raw_rows):
    wide = raw_rows.astype(jnp.float32)
    inverse = lax.rsqrt(jnp.sum(wide * wide, -1, keepdims=True) + EPS_KEY)
    return wide * inverse, inverse


def pack_body(index_ref, *refs):
    sources, out_ref = refs[:-1], refs[-1]
    tokens, width = sources[0].shape
    turned = index_ref[...].T
    cols = [turned[:, i : i + 1] for i in range(out_ref.shape[0] // LANES)]
    chosen = match_cols(cols, iota((LANES, tokens), 1))
    for place, source in enumerate(sources):
        out_ref[:, place * width : (place + 1) * width] = dot(chosen, source[...]).astype(
            jnp.bfloat16
        )


def pack(index, *sources):
    steps = index.shape[0] // STAT
    slots = SLOT_ROWS * LANES
    tokens, width = sources[0].shape
    block = slots // steps
    total = width * len(sources)
    return pl.pallas_call(
        pack_body,
        grid=(steps,),
        in_specs=[pl.BlockSpec((STAT, LANES), lambda i: (i, 0))]
        + [pl.BlockSpec((tokens, width), lambda i: (0, 0)) for _ in sources],
        out_specs=pl.BlockSpec((block, total), lambda i: (i, 0)),
        out_shape=jax.ShapeDtypeStruct((slots, total), jnp.bfloat16),
        compiler_params=params(),
        cost_estimate=cost(2 * slots * tokens * total, 2 * (slots + tokens) * total),
        name="pack_rows",
    )(index, *sources)


def sort_body(table_ref, arrived_ref, sorted_ref, tail_ref, head_ref, chosen):
    step = pl.program_id(0)

    @pl.when(step == 0)
    def _():
        chosen[...] = match_cols(
            table_cols(table_ref, PLACE, PLACE_ROWS), table_row(table_ref, ARRIVAL, SLOT_ROWS)
        )

    rows = dot(chosen[...], arrived_ref[...]).astype(jnp.bfloat16)
    sorted_ref[...] = rows
    half = rows.shape[0] // 2
    tail_ref[:GROUP, :] = rows[half - GROUP : half]
    tail_ref[GROUP:, :] = rows[2 * half - GROUP :]

    @pl.when(step < 2)
    def _():
        head_ref[:GROUP, :] = rows[:GROUP]
        head_ref[GROUP:, :] = rows[half : half + GROUP]


def sort_rows(table, arrived):
    slots, width = arrived.shape
    rows = PLACE_ROWS * LANES
    wide = width // 4
    return pl.pallas_call(
        sort_body,
        grid=(4,),
        in_specs=[
            pl.BlockSpec((LANES, LANES), lambda i: (0, 0)),
            pl.BlockSpec((slots, wide), lambda i: (0, i)),
        ],
        out_specs=[
            pl.BlockSpec((rows, wide), lambda i: (0, i)),
            pl.BlockSpec((2 * GROUP, wide), lambda i: (0, i)),
            pl.BlockSpec((2 * GROUP, wide), lambda i: (0, jnp.minimum(i, 1))),
        ],
        out_shape=[
            jax.ShapeDtypeStruct((rows, width), jnp.bfloat16),
            jax.ShapeDtypeStruct((2 * GROUP, width), jnp.bfloat16),
            jax.ShapeDtypeStruct((2 * GROUP, width // 2), jnp.bfloat16),
        ],
        scratch_shapes=[pltpu.VMEM((rows, slots), jnp.bfloat16)],
        compiler_params=params(),
        cost_estimate=cost(2 * slots * rows * width, 2 * (slots + 2 * rows) * width),
        name="sort_rows",
    )(table, arrived)


def forward_tile(query, keys, values):
    scores = dot(query, keys, 1, 1)
    own = iota((GROUP, 2 * GROUP), 1) == iota((GROUP, 2 * GROUP), 0) + GROUP
    scores = jnp.where(own, NEG_SELF, scores)
    top = jnp.max(scores, -1, keepdims=True)
    raised = jnp.exp(scores - top)
    total = jnp.sum(raised, -1, keepdims=True)
    weights = (raised * (1.0 / total)).astype(jnp.bfloat16)
    return dot(weights, values), top + jnp.log(total)


def forward_body(with_edge, *refs):
    if with_edge:
        query_ref, value_ref, tail_query_ref, tail_value_ref, out_ref, lse_ref = refs
    else:
        query_ref, value_ref, out_ref, lse_ref = refs
    pair = pl.program_id(1)
    lane = iota((GROUP, LANES), 1) % STAT

    for local in range(2):
        columns = slice(local * DH, (local + 1) * DH)
        if with_edge:
            raw = jnp.concatenate([tail_query_ref[:, columns], query_ref[:GROUP, columns]])
            values = jnp.concatenate([tail_value_ref[:, columns], value_ref[:GROUP, columns]])
            query = query_ref[:GROUP, columns]
        else:
            raw = query_ref[:, columns]
            values = value_ref[:, columns]
            query = query_ref[GROUP:, columns]
        keys = unit_rows(raw)[0].astype(jnp.bfloat16)
        partial, lse = forward_tile(query, keys, values)
        out_ref[:, columns] = partial
        at_head = lane == pair * 2 + local
        if local == 0:
            before = jnp.where(pair == 0, jnp.zeros((GROUP, LANES), jnp.float32), lse_ref[...])
        else:
            before = lse_ref[...]
        lse_ref[...] = jnp.where(at_head, lse, before)


def forward(rows_sorted, tail=None):
    with_edge = tail is not None
    rows, width = rows_sorted.shape
    per_round = rows // 2
    wide = 2 * DH
    in_specs = [
        pl.BlockSpec((per_round, wide), lambda r, p: (r, p)),
        pl.BlockSpec((per_round, wide), lambda r, p: (r, p + 2)),
    ]
    arguments = [rows_sorted, rows_sorted]
    if with_edge:
        in_specs += [
            pl.BlockSpec((GROUP, wide), lambda r, p: (r, p)),
            pl.BlockSpec((GROUP, wide), lambda r, p: (r, p + 2)),
        ]
        arguments += [tail, tail]
    return pl.pallas_call(
        functools.partial(forward_body, with_edge),
        grid=(2, 2),
        in_specs=in_specs,
        out_specs=[
            pl.BlockSpec((GROUP, wide), lambda r, p: (r, p)),
            pl.BlockSpec((GROUP, LANES), lambda r, p: (r, 0)),
        ],
        out_shape=[
            jax.ShapeDtypeStruct((2 * GROUP, width // 2), jnp.float32),
            jax.ShapeDtypeStruct((2 * GROUP, LANES), jnp.float32),
        ],
        compiler_params=params(),
        cost_estimate=cost(8 * 4 * GROUP * 2 * GROUP * DH, 4 * rows * width, 8 * GROUP * 512),
        name="forward_edge" if with_edge else "forward_own",
    )(*arguments)


def stats_body(
    table_ref,
    arrived_ref,
    out_first_ref,
    out_second_ref,
    lse_first_ref,
    lse_second_ref,
    sorted_ref,
    head_ref,
    stats_ref,
):
    rows = sorted_ref.shape[0]
    per_round = rows // 2
    place_row = table_row(table_ref, PLACE, PLACE_ROWS)
    chosen = match_cols(
        table_cols(table_ref, PLACE, PLACE_ROWS), table_row(table_ref, ARRIVAL, SLOT_ROWS)
    )
    cotangent = dot(chosen, arrived_ref[...]).astype(jnp.bfloat16)
    sorted_ref[...] = cotangent
    lane = iota((GROUP, LANES), 1)
    parts = []
    for hash_round in range(2):
        kept = slice(hash_round * GROUP, (hash_round + 1) * GROUP)
        head_ref[kept, :] = cotangent[hash_round * per_round : hash_round * per_round + GROUP]
        for group, (out_ref, lse_ref) in enumerate(
            ((out_first_ref, lse_first_ref), (out_second_ref, lse_second_ref))
        ):
            start = hash_round * per_round + group * GROUP
            wide = cotangent[start : start + GROUP].astype(jnp.float32)
            product = wide * out_ref[kept, :]
            stat = lse_ref[kept, :]
            for head in range(4):
                own = jnp.sum(product[:, head * DH : (head + 1) * DH], -1, keepdims=True)
                stat = jnp.where(lane % STAT == 4 + head, own, stat)
            first, second, third = pieces_of(stat)
            piece = lane // (PIECES * STAT)
            parts.append(
                jnp.where(
                    piece == 0,
                    first.astype(jnp.float32),
                    jnp.where(
                        piece == 1,
                        second.astype(jnp.float32),
                        jnp.where(piece == 2, third.astype(jnp.float32), 0.0),
                    ),
                ).astype(jnp.bfloat16)
            )
    stats = jnp.concatenate(parts)
    third_slots = stats_ref.shape[0]
    arrival_cols = table_cols(table_ref, ARRIVAL3, SLOT_ROWS)
    lane_third = (iota((third_slots, LANES), 1) % (3 * STAT)) // STAT
    result = jnp.zeros((third_slots, LANES), jnp.float32)
    for third in range(3):
        back = match_cols(arrival_cols[4 * third : 4 * third + 4], place_row)
        result = jnp.where(lane_third == third, dot(back, stats), result)
    stats_ref[...] = result


def stats_out(table, arrived, outs, lses):
    slots, width = arrived.shape
    rows = PLACE_ROWS * LANES
    return pl.pallas_call(
        stats_body,
        out_shape=[
            jax.ShapeDtypeStruct((rows, width), jnp.bfloat16),
            jax.ShapeDtypeStruct((2 * GROUP, width), jnp.bfloat16),
            jax.ShapeDtypeStruct((slots // 3, LANES), jnp.float32),
        ],
        compiler_params=params(),
        cost_estimate=cost(2 * slots * rows * (width + LANES), 4 * slots * width),
        name="cotangent_and_stats",
    )(table, arrived, *outs, *lses)


def gather_stats(codes_row, slot_cols, stats):
    narrow = stats.astype(jnp.bfloat16)
    total = None
    for third in range(3):
        chosen = match_cols(slot_cols[4 * third : 4 * third + 4], codes_row)
        found = dot(narrow, chosen, 0, 0)
        for piece in range(PIECES):
            at = piece * PIECES * STAT + third * STAT
            part = found[at : at + STAT]
            total = part if total is None else total + part
    return total


def total_body(tokens, table_ref, arrived_ref, out_ref):
    slot_cols = table_cols(table_ref, SEND3, SLOT_ROWS)
    found = gather_stats(iota((1, 2 * tokens), 1), slot_cols, arrived_ref[...])
    lse_first, lse_second = found[:4, :tokens], found[:4, tokens:]
    delta_first, delta_second = found[4:, :tokens], found[4:, tokens:]
    top = jnp.maximum(lse_first, lse_second)
    total = top + jnp.log(jnp.exp(lse_first - top) + jnp.exp(lse_second - top))
    delta = delta_first * jnp.exp(lse_first - total) + delta_second * jnp.exp(lse_second - total)
    stat = jnp.concatenate([total, delta])
    first, second, third_piece = [member.astype(jnp.float32) for member in pieces_of(stat)]
    spare = jnp.zeros((LANES - 9 * STAT, tokens), jnp.float32)
    table = jnp.concatenate(
        [first] * 3 + [second] * 3 + [third_piece] * 3 + [spare]
    ).astype(jnp.bfloat16)
    third_slots = arrived_ref.shape[0]
    lane_third = (iota((third_slots, LANES), 1) % (3 * STAT)) // STAT
    result = jnp.zeros((third_slots, LANES), jnp.float32)
    for third in range(3):
        codes = slot_cols[4 * third : 4 * third + 4]
        cols = [jnp.where(code >= tokens, code - tokens, code) for code in codes]
        chosen = match_cols(cols, iota((LANES, tokens), 1))
        result = jnp.where(lane_third == third, dot(chosen, table, 1, 1), result)
    owners = third_slots // STAT
    by_owner = result.reshape(owners, STAT, LANES)
    out_ref[:, :STAT, :] = by_owner
    above = jnp.concatenate([by_owner[1:], by_owner[:1]])
    below = jnp.concatenate([by_owner[owners - 1 :], by_owner[: owners - 1]])
    half = table_ref[HALF : HALF + 1, :]
    out_ref[:, STAT:, :] = jnp.where(half[None] == 0, above, below)


def total_stats(table, arrived, tokens):
    owners = arrived.shape[0] // STAT
    return pl.pallas_call(
        functools.partial(total_body, tokens),
        out_shape=jax.ShapeDtypeStruct((owners, 2 * STAT, LANES), jnp.float32),
        compiler_params=params(),
        cost_estimate=cost(2 * 1536 * 1536 * LANES, 1 << 20),
        name="total_stats",
    )(table, arrived)


def backward_tile(query, upstream, keys, values, masked, total_row, delta_row):
    scores = dot(keys, query, 1, 1)
    if masked is not None:
        scores = jnp.where(masked, NEG_SELF, scores)
    probs = jnp.exp(scores - total_row)
    dots = dot(values, upstream, 1, 1)
    slopes = (probs * (dots - delta_row)).astype(jnp.bfloat16)
    return probs.astype(jnp.bfloat16), slopes


def backward_body(
    table_ref,
    stats_ref,
    query_ref,
    value_ref,
    cotangent_ref,
    tail_query_ref,
    tail_value_ref,
    next_query_ref,
    next_cotangent_ref,
    out_first_ref,
    out_second_ref,
    lse_first_ref,
    lse_second_ref,
    payload_ref,
    back,
    totals,
    next_totals,
    total_cols,
    shaped,
):
    pair = pl.program_id(0)
    hash_round = pl.program_id(1)
    rows = PLACE_ROWS * LANES
    per_round = rows // 2

    @pl.when((pair == 0) & (hash_round == 0))
    def _():
        place_row = table_row(table_ref, PLACE, PLACE_ROWS)
        next_row = table_row(table_ref, NEXT_PLACE, NEXT_ROWS)
        back[...] = match_cols(table_cols(table_ref, ARRIVAL, SLOT_ROWS), place_row)
        own_stats = stats_ref[:, :STAT, :].reshape(-1, LANES)
        next_stats = stats_ref[:, STAT:, :].reshape(-1, LANES)
        found = gather_stats(place_row, table_cols(table_ref, ARRIVAL3, SLOT_ROWS), own_stats)
        edge = gather_stats(next_row, table_cols(table_ref, NEXT3, SLOT_ROWS), next_stats)
        for each in range(2):
            totals[each] = found[:, each * per_round : (each + 1) * per_round]
            next_totals[each] = edge[:, each * GROUP : (each + 1) * GROUP]
        padded = jnp.concatenate([found, jnp.zeros((LANES - STAT, rows), jnp.float32)])
        total_cols[...] = padded.T.reshape(2, per_round, LANES)

    own = iota((2 * GROUP, GROUP), 0) == iota((2 * GROUP, GROUP), 1) + GROUP
    stat = totals[hash_round]
    edge_stat = next_totals[hash_round]
    columns_of_stat = total_cols[hash_round]
    sublane = iota((STAT, 1), 0)
    lane = iota((1, LANES), 1)

    def row_of(table, index):
        return jnp.sum(jnp.where(sublane == index, table, 0.0), 0, keepdims=True)

    def col_of(table, index):
        return jnp.sum(jnp.where(lane == index, table, 0.0), 1, keepdims=True)

    for local in range(2):
        columns = slice(local * DH, (local + 1) * DH)
        head = pair * 2 + local
        total_row, delta_row = row_of(stat, head), row_of(stat, head + 4)
        edge_total, edge_delta = row_of(edge_stat, head), row_of(edge_stat, head + 4)
        raw = query_ref[:, columns]
        values = value_ref[:, columns]
        upstream = cotangent_ref[:, columns]
        units, inverse = unit_rows(raw)
        keys = units.astype(jnp.bfloat16)
        tail_keys = unit_rows(tail_query_ref[:, columns])[0].astype(jnp.bfloat16)

        keys_first = jnp.concatenate([tail_keys, keys[:GROUP]])
        values_first = jnp.concatenate([tail_value_ref[:, columns], values[:GROUP]])
        probs, slopes = backward_tile(
            raw[:GROUP],
            upstream[:GROUP],
            keys_first,
            values_first,
            own,
            total_row[:, :GROUP],
            delta_row[:, :GROUP],
        )
        query_first = dot(slopes, keys_first, 0, 0)
        unit_first = dot(slopes[GROUP:], raw[:GROUP])
        value_first = dot(probs[GROUP:], upstream[:GROUP])

        probs, slopes = backward_tile(
            raw[GROUP:],
            upstream[GROUP:],
            keys,
            values,
            own,
            total_row[:, GROUP:],
            delta_row[:, GROUP:],
        )
        query_second = dot(slopes, keys, 0, 0)
        unit_both = dot(slopes, raw[GROUP:])
        value_both = dot(probs, upstream[GROUP:])

        next_query = next_query_ref[:, columns]
        next_upstream = next_cotangent_ref[:, columns]
        probs, slopes = backward_tile(
            next_query,
            next_upstream,
            keys[GROUP:],
            values[GROUP:],
            None,
            edge_total,
            edge_delta,
        )
        unit_last = dot(slopes, next_query)
        value_last = dot(probs, next_upstream)

        for group, (query_slope, unit_slope, value_slope, out_ref, lse_ref) in enumerate(
            (
                (
                    query_first,
                    unit_first + unit_both[:GROUP],
                    value_first + value_both[:GROUP],
                    out_first_ref,
                    lse_first_ref,
                ),
                (
                    query_second,
                    unit_both[GROUP:] + unit_last,
                    value_both[GROUP:] + value_last,
                    out_second_ref,
                    lse_second_ref,
                ),
            )
        ):
            kept = slice(group * GROUP, (group + 1) * GROUP)
            unit = units[kept]
            key_slope = inverse[kept] * (
                unit_slope - unit * jnp.sum(unit * unit_slope, -1, keepdims=True)
            )
            share = jnp.exp(col_of(lse_ref[...] - columns_of_stat[kept], head))
            wide = 2 * DH
            shaped[kept, columns] = (out_ref[:, columns] * share).astype(jnp.bfloat16)
            shaped[kept, wide + local * DH : wide + (local + 1) * DH] = (
                query_slope + key_slope
            ).astype(jnp.bfloat16)
            shaped[kept, 2 * wide + local * DH : 2 * wide + (local + 1) * DH] = (
                value_slope.astype(jnp.bfloat16)
            )

    @pl.when(hash_round == 0)
    def _():
        payload_ref[...] = dot(back[:, :per_round], shaped[...]).astype(jnp.bfloat16)

    @pl.when(hash_round == 1)
    def _():
        payload_ref[...] += dot(back[:, per_round:], shaped[...]).astype(jnp.bfloat16)


def backward(table, stats, rows_sorted, cotangent, tail, next_query, next_cotangent, outs, lses):
    rows, width = rows_sorted.shape
    per_round = rows // 2
    slots = SLOT_ROWS * LANES
    wide = 2 * DH

    def whole(array):
        return pl.BlockSpec(array.shape, lambda p, r: (0,) * array.ndim)

    small = [table, stats]
    group_spec = pl.BlockSpec((GROUP, wide), lambda p, r: (r, p))
    lse_spec = pl.BlockSpec((GROUP, LANES), lambda p, r: (r, 0))
    return pl.pallas_call(
        backward_body,
        grid=(2, 2),
        in_specs=[whole(array) for array in small]
        + [
            pl.BlockSpec((per_round, wide), lambda p, r: (r, p)),
            pl.BlockSpec((per_round, wide), lambda p, r: (r, p + 2)),
            pl.BlockSpec((per_round, wide), lambda p, r: (r, p)),
            group_spec,
            pl.BlockSpec((GROUP, wide), lambda p, r: (r, p + 2)),
            group_spec,
            group_spec,
            group_spec,
            group_spec,
            lse_spec,
            lse_spec,
        ],
        out_specs=pl.BlockSpec((slots, 3 * wide), lambda p, r: (0, p)),
        out_shape=jax.ShapeDtypeStruct((slots, 6 * wide), jnp.bfloat16),
        scratch_shapes=[
            pltpu.VMEM((slots, rows), jnp.bfloat16),
            pltpu.VMEM((2, STAT, per_round), jnp.float32),
            pltpu.VMEM((2, STAT, GROUP), jnp.float32),
            pltpu.VMEM((2, per_round, LANES), jnp.float32),
            pltpu.VMEM((per_round, 3 * wide), jnp.bfloat16),
        ],
        compiler_params=params(),
        cost_estimate=cost(8e9, 1.5e7, 3e6),
        name="backward",
    )(
        *small,
        rows_sorted,
        rows_sorted,
        cotangent,
        tail,
        tail,
        next_query,
        next_cotangent,
        *outs,
        *lses,
    )


def combine_body(table_ref, arrived_ref, *out_refs):
    tokens, wide = out_refs[0].shape
    chosen = match(iota((tokens, 1), 0), table_row(table_ref, SEND, SLOT_ROWS))
    found = dot(chosen, arrived_ref[...])
    for place, out_ref in enumerate(out_refs):
        out_ref[...] = found[:, place * wide : (place + 1) * wide].astype(jnp.bfloat16)


def combine(table, arrived, tokens):
    slots, width = arrived.shape
    wide = width // 6
    return pl.pallas_call(
        combine_body,
        grid=(2,),
        in_specs=[
            pl.BlockSpec((LANES, LANES), lambda i: (0, 0)),
            pl.BlockSpec((slots, 3 * wide), lambda i: (0, i)),
        ],
        out_specs=[pl.BlockSpec((tokens, wide), lambda i: (0, i))] * 3,
        out_shape=[jax.ShapeDtypeStruct((tokens, 2 * wide), jnp.bfloat16)] * 3,
        compiler_params=params(),
        cost_estimate=cost(2 * slots * tokens * width, 2 * (slots + tokens) * width),
        name="combine_rows",
    )(table, arrived)


def per_device(query_key, value, attended_cotangent, send_rows, arrival_count, receive_slot):
    tokens, row_width = query_key.shape
    rounds = send_rows.shape[0]
    owners = lax.axis_size("seq")
    capacity = send_rows.shape[1] // owners
    per_owner = rounds * capacity
    slots = owners * per_owner

    code = (tokens * jnp.arange(rounds, dtype=jnp.int32))[:, None]
    half = lax.axis_index("head")

    def by_owner(table):
        return table.reshape(rounds, owners, capacity).transpose(1, 0, 2).reshape(owners, per_owner)

    def by_third(codes):
        return codes.reshape(owners, 3, STAT).transpose(1, 0, 2)

    def rows_of(codes, count):
        rows = codes.reshape(-1, LANES)
        return jnp.pad(rows, ((0, count - rows.shape[0]), (0, 0)), constant_values=-1)

    def sent(packed):
        return exchange(packed.reshape(owners, per_owner, -1)).reshape(slots, -1)

    blocks = send_rows.reshape(rounds, owners, capacity)
    send_rows = jnp.where(half == 0, blocks, blocks[:, ::-1]).reshape(rounds, -1)
    send = by_owner(send_rows)
    send_blocks = send.reshape(6, 2, LANES)
    send_blocks = jnp.pad(send_blocks, ((0, 0), (0, STAT - 2), (0, 0))).reshape(-1, LANES)
    packed = pack(send_blocks, query_key, value)
    packed_cotangent = pack(send_blocks, attended_cotangent)

    arrival_count = to_place(arrival_count)
    receive_slot = to_place(receive_slot)
    running = jnp.cumsum(arrival_count, axis=1)
    within = jnp.arange(capacity, dtype=jnp.int32)
    arrival = (running - arrival_count + code)[:, :, None] + within
    arrival = by_owner(jnp.where(within < arrival_count[:, :, None], arrival, -1))
    place = receive_slot + code
    next_arrival = to_prior(arrival)
    next_place = to_prior(place[:, :GROUP])
    table = jnp.concatenate(
        [
            rows_of(arrival, ARRIVAL3 - ARRIVAL),
            rows_of(by_third(arrival), NEXT3 - ARRIVAL3),
            rows_of(by_third(next_arrival), PLACE - NEXT3),
            rows_of(place, NEXT_PLACE - PLACE),
            rows_of(next_place, SEND - NEXT_PLACE),
            rows_of(send, SEND3 - SEND),
            rows_of(by_third(by_owner(send_rows + code)), HALF - SEND3),
            jnp.full((LANES - HALF, LANES), half, jnp.int32),
        ]
    )

    arrived, table = lax.optimization_barrier((sent(packed), table))
    rows_sorted, tail, head_query = sort_rows(table, arrived)
    prior_tail = to_next(tail)
    arrived_cotangent = sent(packed_cotangent)
    next_query = to_prior(head_query)
    out_second, lse_second = forward(rows_sorted)
    out_first, lse_first = forward(rows_sorted, prior_tail)
    outs, lses = (out_first, out_second), (lse_first, lse_second)
    cotangent, head_cotangent, stats = stats_out(table, arrived_cotangent, outs, lses)
    next_cotangent = to_prior(head_cotangent)
    home_stats = exchange(stats.reshape(owners, STAT, LANES)).reshape(-1, LANES)
    totals = exchange(total_stats(table, home_stats, tokens))
    payload = backward(
        table,
        totals,
        rows_sorted,
        cotangent,
        prior_tail,
        next_query,
        next_cotangent,
        outs,
        lses,
    )
    return tuple(combine(table, sent(payload), tokens))


def solution(mesh):
    in_specs = (
        P("seq", "head"),
        P("seq", "head"),
        P("seq", "head"),
        P(None, "seq"),
        P(None, "seq"),
        P(None, "seq"),
    )
    out_specs = (P("seq", "head"), P("seq", "head"), P("seq", "head"))
    return jax.shard_map(
        per_device, mesh=mesh, in_specs=in_specs, out_specs=out_specs, check_vma=False
    )
```

```python
import functools

import jax
import jax.numpy as jnp
from jax import lax
from jax.experimental import pallas as pl
from jax.experimental.pallas import tpu as pltpu
from jax.sharding import PartitionSpec as P

DH = 128
GROUP = 256
NEG_SELF = -100000.0
EPS_KEY = 1e-06
LANES = 128
STAT = 8
PIECES = 3
MIB = 1 << 20


def dot(left, right, left_axis=1, right_axis=0):
    return lax.dot_general(
        left,
        right,
        (((left_axis,), (right_axis,)), ((), ())),
        preferred_element_type=jnp.float32,
    )


def params(mib=62):
    return pltpu.CompilerParams(vmem_limit_bytes=mib * MIB)


def cost(flops, moved, exps=0):
    return pl.CostEstimate(flops=int(flops), bytes_accessed=int(moved), transcendentals=int(exps))


def routed(block, route_of):
    owners, halves = lax.axis_size("seq"), lax.axis_size("head")
    route = [
        (i * halves + half, route_of(i, half, owners) * halves + half)
        for i in range(owners)
        for half in range(halves)
    ]
    return lax.ppermute(block, ("seq", "head"), route)


def to_next(block):
    return routed(block, lambda i, half, n: (i + (1 if half == 0 else -1)) % n)


def to_prior(block):
    return routed(block, lambda i, half, n: (i - (1 if half == 0 else -1)) % n)


def to_place_prior(block):
    return routed(block, lambda i, half, n: (i - 1) % n if half == 0 else n - 1 - (i - 1) % n)


def to_place(block):
    return routed(block, lambda i, half, n: i if half == 0 else n - 1 - i)


def exchange(block):
    return lax.all_to_all(block, "seq", split_axis=0, concat_axis=0, tiled=True)


def match(left, right):
    return jnp.where(left == right, 1.0, 0.0).astype(jnp.bfloat16)


ARRIVAL, ARRIVAL3, NEXT3, PLACE, NEXT_PLACE, SEND, SEND3, HALF = 0, 16, 32, 48, 56, 64, 80, 96
SLOT_ROWS, PLACE_ROWS, NEXT_ROWS = 12, 8, 4


def table_row(table_ref, start, count):
    return jnp.concatenate([table_ref[start + i : start + i + 1, :] for i in range(count)], axis=1)


def table_cols(table_ref, start, count):
    turned = table_ref[...].T
    return [turned[:, start + i : start + i + 1] for i in range(count)]


def match_cols(cols, row):
    return jnp.concatenate([match(col, row) for col in cols])


def iota(shape, axis):
    return lax.broadcasted_iota(jnp.int32, shape, axis)


def pieces_of(wide):
    first = wide.astype(jnp.bfloat16)
    rest = wide - first.astype(jnp.float32)
    second = rest.astype(jnp.bfloat16)
    third = (rest - second.astype(jnp.float32)).astype(jnp.bfloat16)
    return first, second, third


def unit_rows(raw_rows):
    wide = raw_rows.astype(jnp.float32)
    inverse = lax.rsqrt(jnp.sum(wide * wide, -1, keepdims=True) + EPS_KEY)
    return wide * inverse, inverse


def pack_body(index_ref, *refs):
    sources, out_ref = refs[:-1], refs[-1]
    tokens, width = sources[0].shape
    turned = index_ref[...].T
    cols = [turned[:, i : i + 1] for i in range(out_ref.shape[0] // LANES)]
    chosen = match_cols(cols, iota((LANES, tokens), 1))
    for place, source in enumerate(sources):
        out_ref[:, place * width : (place + 1) * width] = dot(chosen, source[...]).astype(
            jnp.bfloat16
        )


def pack(index, *sources):
    steps = index.shape[0] // STAT
    slots = SLOT_ROWS * LANES
    tokens, width = sources[0].shape
    block = slots // steps
    total = width * len(sources)
    return pl.pallas_call(
        pack_body,
        grid=(steps,),
        in_specs=[pl.BlockSpec((STAT, LANES), lambda i: (i, 0))]
        + [pl.BlockSpec((tokens, width), lambda i: (0, 0)) for _ in sources],
        out_specs=pl.BlockSpec((block, total), lambda i: (i, 0)),
        out_shape=jax.ShapeDtypeStruct((slots, total), jnp.bfloat16),
        compiler_params=params(),
        cost_estimate=cost(2 * slots * tokens * total, 2 * (slots + tokens) * total),
        name="pack_rows",
    )(index, *sources)


def place_cols(table_ref, group):
    cols = table_cols(table_ref, PLACE, PLACE_ROWS)
    each = GROUP // LANES
    first, second = group * each, PLACE_ROWS // 2 + group * each
    return cols[first : first + each], cols[second : second + each]


def tail_body(table_ref, arrived_ref, tail_ref, chosen):
    @pl.when(pl.program_id(0) == 0)
    def _():
        first, second = place_cols(table_ref, 1)
        chosen[...] = match_cols(first + second, table_row(table_ref, ARRIVAL, SLOT_ROWS))

    tail_ref[...] = dot(chosen[...], arrived_ref[...]).astype(jnp.bfloat16)


def sort_tail(table, arrived, width):
    slots = arrived.shape[0]
    wide = width // 4
    return pl.pallas_call(
        tail_body,
        grid=(4,),
        in_specs=[
            pl.BlockSpec((LANES, LANES), lambda i: (0, 0)),
            pl.BlockSpec((slots, wide), lambda i: (0, i)),
        ],
        out_specs=pl.BlockSpec((2 * GROUP, wide), lambda i: (0, i)),
        out_shape=jax.ShapeDtypeStruct((2 * GROUP, width), jnp.bfloat16),
        scratch_shapes=[pltpu.VMEM((2 * GROUP, slots), jnp.bfloat16)],
        compiler_params=params(),
        cost_estimate=cost(4 * slots * GROUP * width, 2 * (slots + 2 * GROUP) * width),
        name="sort_tail",
    )(table, arrived)


def forward_tile(query, keys, values):
    scores = dot(query, keys, 1, 1)
    own = iota((GROUP, 2 * GROUP), 1) == iota((GROUP, 2 * GROUP), 0) + GROUP
    scores = jnp.where(own, NEG_SELF, scores)
    top = jnp.max(scores, -1, keepdims=True)
    raised = jnp.exp(scores - top)
    total = jnp.sum(raised, -1, keepdims=True)
    weights = (raised * (1.0 / total)).astype(jnp.bfloat16)
    return dot(weights, values), top + jnp.log(total)


def forward_pair(pair, query, raw, values, cotangent, out_ref):
    lane = iota((GROUP, LANES), 1) % STAT
    stat = jnp.zeros((GROUP, LANES), jnp.float32)
    for local in range(2):
        columns = slice(local * DH, (local + 1) * DH)
        keys = unit_rows(raw[:, columns])[0].astype(jnp.bfloat16)
        partial, lse = forward_tile(query[:, columns], keys, values[:, columns])
        out_ref[:, columns] = partial
        delta = jnp.sum(partial * cotangent[:, columns].astype(jnp.float32), -1, keepdims=True)
        head = pair * 2 + local
        stat = jnp.where(lane == head, lse, jnp.where(lane == head + 4, delta, stat))
    return stat


def own_body(
    table_ref,
    arrived_query_ref,
    arrived_value_ref,
    arrived_cotangent_ref,
    tail_query_ref,
    tail_value_ref,
    head_query_ref,
    head_value_ref,
    head_cotangent_ref,
    tail_cotangent_ref,
    out_ref,
    stat_ref,
    chosen,
):
    pair = pl.program_id(0)
    hash_round = pl.program_id(1)

    @pl.when((pair == 0) & (hash_round == 0))
    def _():
        row = table_row(table_ref, ARRIVAL, SLOT_ROWS)
        heads, tails = place_cols(table_ref, 0), place_cols(table_ref, 1)
        for each in range(2):
            chosen[each] = match_cols(heads[each] + tails[each], row)

    select_head = chosen[hash_round, :GROUP]
    query = dot(select_head, arrived_query_ref[...]).astype(jnp.bfloat16)
    value = dot(select_head, arrived_value_ref[...]).astype(jnp.bfloat16)
    cotangent = dot(chosen[hash_round], arrived_cotangent_ref[...]).astype(jnp.bfloat16)
    head_query_ref[...] = query
    head_value_ref[...] = value
    head_cotangent_ref[...] = cotangent[:GROUP]
    tail_cotangent_ref[...] = cotangent[GROUP:]
    stat_ref[...] = forward_pair(
        pair,
        tail_query_ref[...],
        jnp.concatenate([query, tail_query_ref[...]]),
        jnp.concatenate([value, tail_value_ref[...]]),
        cotangent[GROUP:],
        out_ref,
    )


def group_spec(offset=0):
    return pl.BlockSpec((GROUP, 2 * DH), lambda p, r: (r, p + offset))


def stat_spec():
    return pl.BlockSpec((GROUP, LANES), lambda p, r: (r, p))


def forward_own(table, arrived, tail):
    slots, width = arrived.shape
    wide = width // 6
    rows = 2 * GROUP
    array = jax.ShapeDtypeStruct((rows, width // 3), jnp.bfloat16)
    return pl.pallas_call(
        own_body,
        grid=(2, 2),
        in_specs=[pl.BlockSpec((LANES, LANES), lambda p, r: (0, 0))]
        + [pl.BlockSpec((slots, wide), lambda p, r, k=k: (0, p + 2 * k)) for k in range(3)]
        + [group_spec(), group_spec(2)],
        out_specs=[group_spec()] * 5 + [stat_spec()],
        out_shape=[array] * 4
        + [
            jax.ShapeDtypeStruct((rows, width // 3), jnp.float32),
            jax.ShapeDtypeStruct((rows, 2 * LANES), jnp.float32),
        ],
        scratch_shapes=[pltpu.VMEM((2, 2 * GROUP, slots), jnp.bfloat16)],
        compiler_params=params(),
        cost_estimate=cost(5e9, 1e7, 8 * GROUP * 512),
        name="forward_own",
    )(table, arrived, arrived, arrived, tail, tail)


def edge_body(
    table_ref,
    query_ref,
    value_ref,
    cotangent_ref,
    prior_query_ref,
    prior_value_ref,
    second_stat_ref,
    out_ref,
    stat_ref,
    stats_ref,
    both,
):
    pair = pl.program_id(0)
    hash_round = pl.program_id(1)
    stat = forward_pair(
        pair,
        query_ref[...],
        jnp.concatenate([prior_query_ref[...], query_ref[...]]),
        jnp.concatenate([prior_value_ref[...], value_ref[...]]),
        cotangent_ref[...],
        out_ref,
    )
    stat_ref[...] = stat

    @pl.when(pair == 0)
    def _():
        both[hash_round, :GROUP] = stat
        both[hash_round, GROUP:] = second_stat_ref[...]

    @pl.when(pair == 1)
    def _():
        both[hash_round, :GROUP] += stat
        both[hash_round, GROUP:] += second_stat_ref[...]

    @pl.when((pair == 1) & (hash_round == 1))
    def _():
        rows = 4 * GROUP
        piece = iota((rows, LANES), 1) // (PIECES * STAT)
        first, second, third = pieces_of(both[...].reshape(rows, LANES))
        nothing = jnp.zeros((rows, LANES), jnp.bfloat16)
        stats = jnp.where(
            piece == 0,
            first,
            jnp.where(piece == 1, second, jnp.where(piece == 2, third, nothing)),
        )
        place_row = table_row(table_ref, PLACE, PLACE_ROWS)
        third_slots = stats_ref.shape[0]
        arrival_cols = table_cols(table_ref, ARRIVAL3, SLOT_ROWS)
        lane_third = (iota((third_slots, LANES), 1) % (3 * STAT)) // STAT
        result = jnp.zeros((third_slots, LANES), jnp.float32)
        for third in range(3):
            back = match_cols(arrival_cols[4 * third : 4 * third + 4], place_row)
            result = jnp.where(lane_third == third, dot(back, stats), result)
        stats_ref[...] = result


def forward_edge(table, query, value, cotangent, prior_tail, second_stat):
    rows, width = query.shape
    third_slots = SLOT_ROWS * LANES // 3
    return pl.pallas_call(
        edge_body,
        grid=(2, 2),
        in_specs=[pl.BlockSpec((LANES, LANES), lambda p, r: (0, 0))]
        + [group_spec()] * 4
        + [group_spec(2), stat_spec()],
        out_specs=[
            group_spec(),
            stat_spec(),
            pl.BlockSpec((third_slots, LANES), lambda p, r: (0, 0)),
        ],
        out_shape=[
            jax.ShapeDtypeStruct((rows, width), jnp.float32),
            jax.ShapeDtypeStruct((rows, 2 * LANES), jnp.float32),
            jax.ShapeDtypeStruct((third_slots, LANES), jnp.float32),
        ],
        scratch_shapes=[pltpu.VMEM((2, 2 * GROUP, LANES), jnp.float32)],
        compiler_params=params(),
        cost_estimate=cost(2e9, 4e6, 8 * GROUP * 512),
        name="forward_edge",
    )(table, query, value, cotangent, prior_tail, prior_tail, second_stat)


def gather_stats(codes_row, slot_cols, stats):
    narrow = stats.astype(jnp.bfloat16)
    total = None
    for third in range(3):
        chosen = match_cols(slot_cols[4 * third : 4 * third + 4], codes_row)
        found = dot(narrow, chosen, 0, 0)
        for piece in range(PIECES):
            at = piece * PIECES * STAT + third * STAT
            part = found[at : at + STAT]
            total = part if total is None else total + part
    return total


def total_body(tokens, table_ref, arrived_ref, out_ref):
    slot_cols = table_cols(table_ref, SEND3, SLOT_ROWS)
    found = gather_stats(iota((1, 2 * tokens), 1), slot_cols, arrived_ref[...])
    lse_first, lse_second = found[:4, :tokens], found[:4, tokens:]
    delta_first, delta_second = found[4:, :tokens], found[4:, tokens:]
    top = jnp.maximum(lse_first, lse_second)
    total = top + jnp.log(jnp.exp(lse_first - top) + jnp.exp(lse_second - top))
    delta = delta_first * jnp.exp(lse_first - total) + delta_second * jnp.exp(lse_second - total)
    stat = jnp.concatenate([total, delta])
    first, second, third_piece = [member.astype(jnp.float32) for member in pieces_of(stat)]
    spare = jnp.zeros((LANES - 9 * STAT, tokens), jnp.float32)
    table = jnp.concatenate(
        [first] * 3 + [second] * 3 + [third_piece] * 3 + [spare]
    ).astype(jnp.bfloat16)
    third_slots = arrived_ref.shape[0]
    lane_third = (iota((third_slots, LANES), 1) % (3 * STAT)) // STAT
    result = jnp.zeros((third_slots, LANES), jnp.float32)
    for third in range(3):
        codes = slot_cols[4 * third : 4 * third + 4]
        cols = [jnp.where(code >= tokens, code - tokens, code) for code in codes]
        chosen = match_cols(cols, iota((LANES, tokens), 1))
        result = jnp.where(lane_third == third, dot(chosen, table, 1, 1), result)
    owners = third_slots // STAT
    by_owner = result.reshape(owners, STAT, LANES)
    out_ref[:, :STAT, :] = by_owner
    above = jnp.concatenate([by_owner[1:], by_owner[:1]])
    below = jnp.concatenate([by_owner[owners - 1 :], by_owner[: owners - 1]])
    half = table_ref[HALF : HALF + 1, :]
    out_ref[:, STAT:, :] = jnp.where(half[None] == 0, above, below)


def total_stats(table, arrived, tokens):
    owners = arrived.shape[0] // STAT
    return pl.pallas_call(
        functools.partial(total_body, tokens),
        out_shape=jax.ShapeDtypeStruct((owners, 2 * STAT, LANES), jnp.float32),
        compiler_params=params(),
        cost_estimate=cost(2 * 1536 * 1536 * LANES, 1 << 20),
        name="total_stats",
    )(table, arrived)


def backward_tile(query, upstream, keys, values, masked, total_row, delta_row):
    scores = dot(keys, query, 1, 1)
    if masked is not None:
        scores = jnp.where(masked, NEG_SELF, scores)
    probs = jnp.exp(scores - total_row)
    dots = dot(values, upstream, 1, 1)
    slopes = (probs * (dots - delta_row)).astype(jnp.bfloat16)
    return probs.astype(jnp.bfloat16), slopes


def backward_body(
    table_ref,
    stats_ref,
    head_query_ref,
    tail_query_ref,
    head_value_ref,
    tail_value_ref,
    head_cotangent_ref,
    tail_cotangent_ref,
    prior_query_ref,
    prior_value_ref,
    next_query_ref,
    next_cotangent_ref,
    out_first_ref,
    out_second_ref,
    lse_first_ref,
    lse_second_ref,
    payload_ref,
    back,
    totals,
    next_totals,
    total_cols,
    shaped,
):
    pair = pl.program_id(0)
    hash_round = pl.program_id(1)
    rows = PLACE_ROWS * LANES
    per_round = rows // 2

    @pl.when((pair == 0) & (hash_round == 0))
    def _():
        place_row = table_row(table_ref, PLACE, PLACE_ROWS)
        next_row = table_row(table_ref, NEXT_PLACE, NEXT_ROWS)
        back[...] = match_cols(table_cols(table_ref, ARRIVAL, SLOT_ROWS), place_row)
        own_stats = stats_ref[:, :STAT, :].reshape(-1, LANES)
        next_stats = stats_ref[:, STAT:, :].reshape(-1, LANES)
        found = gather_stats(place_row, table_cols(table_ref, ARRIVAL3, SLOT_ROWS), own_stats)
        edge = gather_stats(next_row, table_cols(table_ref, NEXT3, SLOT_ROWS), next_stats)
        for each in range(2):
            totals[each] = found[:, each * per_round : (each + 1) * per_round]
            next_totals[each] = edge[:, each * GROUP : (each + 1) * GROUP]
        padded = jnp.concatenate([found, jnp.zeros((LANES - STAT, rows), jnp.float32)])
        total_cols[...] = padded.T.reshape(2, per_round, LANES)

    own = iota((2 * GROUP, GROUP), 0) == iota((2 * GROUP, GROUP), 1) + GROUP
    stat = totals[hash_round]
    edge_stat = next_totals[hash_round]
    columns_of_stat = total_cols[hash_round]
    sublane = iota((STAT, 1), 0)
    lane = iota((1, LANES), 1)

    def row_of(table, index):
        return jnp.sum(jnp.where(sublane == index, table, 0.0), 0, keepdims=True)

    def col_of(table, index):
        return jnp.sum(jnp.where(lane == index, table, 0.0), 1, keepdims=True)

    for local in range(2):
        columns = slice(local * DH, (local + 1) * DH)
        head = pair * 2 + local
        total_row, delta_row = row_of(stat, head), row_of(stat, head + 4)
        edge_total, edge_delta = row_of(edge_stat, head), row_of(edge_stat, head + 4)
        raw = jnp.concatenate([head_query_ref[:, columns], tail_query_ref[:, columns]])
        values = jnp.concatenate([head_value_ref[:, columns], tail_value_ref[:, columns]])
        upstream = jnp.concatenate(
            [head_cotangent_ref[:, columns], tail_cotangent_ref[:, columns]]
        )
        units, inverse = unit_rows(raw)
        keys = units.astype(jnp.bfloat16)
        tail_keys = unit_rows(prior_query_ref[:, columns])[0].astype(jnp.bfloat16)

        keys_first = jnp.concatenate([tail_keys, keys[:GROUP]])
        values_first = jnp.concatenate([prior_value_ref[:, columns], values[:GROUP]])
        probs, slopes = backward_tile(
            raw[:GROUP],
            upstream[:GROUP],
            keys_first,
            values_first,
            own,
            total_row[:, :GROUP],
            delta_row[:, :GROUP],
        )
        query_first = dot(slopes, keys_first, 0, 0)
        unit_first = dot(slopes[GROUP:], raw[:GROUP])
        value_first = dot(probs[GROUP:], upstream[:GROUP])

        probs, slopes = backward_tile(
            raw[GROUP:],
            upstream[GROUP:],
            keys,
            values,
            own,
            total_row[:, GROUP:],
            delta_row[:, GROUP:],
        )
        query_second = dot(slopes, keys, 0, 0)
        unit_both = dot(slopes, raw[GROUP:])
        value_both = dot(probs, upstream[GROUP:])

        next_query = next_query_ref[:, columns]
        next_upstream = next_cotangent_ref[:, columns]
        probs, slopes = backward_tile(
            next_query,
            next_upstream,
            keys[GROUP:],
            values[GROUP:],
            None,
            edge_total,
            edge_delta,
        )
        unit_last = dot(slopes, next_query)
        value_last = dot(probs, next_upstream)

        for group, (query_slope, unit_slope, value_slope, out_ref, lse_ref) in enumerate(
            (
                (
                    query_first,
                    unit_first + unit_both[:GROUP],
                    value_first + value_both[:GROUP],
                    out_first_ref,
                    lse_first_ref,
                ),
                (
                    query_second,
                    unit_both[GROUP:] + unit_last,
                    value_both[GROUP:] + value_last,
                    out_second_ref,
                    lse_second_ref,
                ),
            )
        ):
            kept = slice(group * GROUP, (group + 1) * GROUP)
            unit = units[kept]
            key_slope = inverse[kept] * (
                unit_slope - unit * jnp.sum(unit * unit_slope, -1, keepdims=True)
            )
            share = jnp.exp(col_of(lse_ref[...] - columns_of_stat[kept], head))
            wide = 2 * DH
            shaped[kept, columns] = (out_ref[:, columns] * share).astype(jnp.bfloat16)
            shaped[kept, wide + local * DH : wide + (local + 1) * DH] = (
                query_slope + key_slope
            ).astype(jnp.bfloat16)
            shaped[kept, 2 * wide + local * DH : 2 * wide + (local + 1) * DH] = (
                value_slope.astype(jnp.bfloat16)
            )

    @pl.when(hash_round == 0)
    def _():
        payload_ref[...] = dot(back[:, :per_round], shaped[...]).astype(jnp.bfloat16)

    @pl.when(hash_round == 1)
    def _():
        payload_ref[...] += dot(back[:, per_round:], shaped[...]).astype(jnp.bfloat16)


def backward(table, stats, heads, tail, tail_cotangent, prior_tail, nexts, outs, lses):
    rows = PLACE_ROWS * LANES
    per_round = rows // 2
    slots = SLOT_ROWS * LANES
    wide = 2 * DH

    def whole(array):
        return pl.BlockSpec(array.shape, lambda p, r: (0,) * array.ndim)

    small = [table, stats]
    head_query, head_value, head_cotangent = heads
    return pl.pallas_call(
        backward_body,
        grid=(2, 2),
        in_specs=[whole(array) for array in small]
        + [group_spec()] * 3
        + [group_spec(2)]
        + [group_spec()] * 3
        + [group_spec(2)]
        + [group_spec()] * 4
        + [stat_spec()] * 2,
        out_specs=pl.BlockSpec((slots, 3 * wide), lambda p, r: (0, p)),
        out_shape=jax.ShapeDtypeStruct((slots, 6 * wide), jnp.bfloat16),
        scratch_shapes=[
            pltpu.VMEM((slots, rows), jnp.bfloat16),
            pltpu.VMEM((2, STAT, per_round), jnp.float32),
            pltpu.VMEM((2, STAT, GROUP), jnp.float32),
            pltpu.VMEM((2, per_round, LANES), jnp.float32),
            pltpu.VMEM((per_round, 3 * wide), jnp.bfloat16),
        ],
        compiler_params=params(),
        cost_estimate=cost(8e9, 1.5e7, 3e6),
        name="backward",
    )(
        *small,
        head_query,
        tail,
        head_value,
        tail,
        head_cotangent,
        tail_cotangent,
        prior_tail,
        prior_tail,
        *nexts,
        *outs,
        *lses,
    )


def combine_body(table_ref, arrived_ref, *out_refs):
    tokens, wide = out_refs[0].shape
    chosen = match(iota((tokens, 1), 0), table_row(table_ref, SEND, SLOT_ROWS))
    found = dot(chosen, arrived_ref[...])
    for place, out_ref in enumerate(out_refs):
        out_ref[...] = found[:, place * wide : (place + 1) * wide].astype(jnp.bfloat16)


def combine(table, arrived, tokens):
    slots, width = arrived.shape
    wide = width // 6
    return pl.pallas_call(
        combine_body,
        grid=(2,),
        in_specs=[
            pl.BlockSpec((LANES, LANES), lambda i: (0, 0)),
            pl.BlockSpec((slots, 3 * wide), lambda i: (0, i)),
        ],
        out_specs=[pl.BlockSpec((tokens, wide), lambda i: (0, i))] * 3,
        out_shape=[jax.ShapeDtypeStruct((tokens, 2 * wide), jnp.bfloat16)] * 3,
        compiler_params=params(),
        cost_estimate=cost(2 * slots * tokens * width, 2 * (slots + tokens) * width),
        name="combine_rows",
    )(table, arrived)


def per_device(query_key, value, attended_cotangent, send_rows, arrival_count, receive_slot):
    tokens, row_width = query_key.shape
    rounds = send_rows.shape[0]
    owners = lax.axis_size("seq")
    capacity = send_rows.shape[1] // owners
    per_owner = rounds * capacity
    slots = owners * per_owner

    code = (tokens * jnp.arange(rounds, dtype=jnp.int32))[:, None]
    half = lax.axis_index("head")

    def by_owner(table):
        return table.reshape(rounds, owners, capacity).transpose(1, 0, 2).reshape(owners, per_owner)

    def by_third(codes):
        return codes.reshape(owners, 3, STAT).transpose(1, 0, 2)

    def rows_of(codes, count):
        rows = codes.reshape(-1, LANES)
        return jnp.pad(rows, ((0, count - rows.shape[0]), (0, 0)), constant_values=-1)

    def sent(packed):
        return exchange(packed.reshape(owners, per_owner, -1)).reshape(slots, -1)

    blocks = send_rows.reshape(rounds, owners, capacity)
    send_rows = jnp.where(half == 0, blocks, blocks[:, ::-1]).reshape(rounds, -1)
    send = by_owner(send_rows)
    send_blocks = send.reshape(6, 2, LANES)
    send_blocks = jnp.pad(send_blocks, ((0, 0), (0, STAT - 2), (0, 0))).reshape(-1, LANES)
    packed = pack(send_blocks, query_key, value, attended_cotangent)

    within = jnp.arange(capacity, dtype=jnp.int32)

    def arrivals(counts):
        start = jnp.cumsum(counts, axis=1) - counts + code
        codes = jnp.where(within < counts[:, :, None], start[:, :, None] + within, -1)
        return by_owner(codes)

    arrival = arrivals(to_place(arrival_count))
    next_arrival = arrivals(to_place_prior(arrival_count))
    place = to_place(receive_slot) + code
    next_place = to_place_prior(receive_slot[:, :GROUP]) + code
    table = jnp.concatenate(
        [first] * 3 + [second] * 3 + [third_piece] * 3 + [spare]
    ).astype(jnp.bfloat16)
    third_slots = arrived_ref.shape[0]
    lane_third = (iota((third_slots, LANES), 1) % (3 * STAT)) // STAT
    result = jnp.zeros((third_slots, LANES), jnp.float32)
    for third in range(3):
        codes = slot_cols[4 * third : 4 * third + 4]
        cols = [jnp.where(code >= tokens, code - tokens, code) for code in codes]
        chosen = match_cols(cols, iota((LANES, tokens), 1))
        result = jnp.where(lane_third == third, dot(chosen, table, 1, 1), result)
    owners = third_slots // STAT
    by_owner = result.reshape(owners, STAT, LANES)
    out_ref[:, :STAT, :] = by_owner
    above = jnp.concatenate([by_owner[1:], by_owner[:1]])
    below = jnp.concatenate([by_owner[owners - 1 :], by_owner[: owners - 1]])
    half = table_ref[HALF : HALF + 1, :]
    out_ref[:, STAT:, :] = jnp.where(half[None] == 0, above, below)


def total_stats(table, arrived, tokens):
    owners = arrived.shape[0] // STAT
    return pl.pallas_call(
        functools.partial(total_body, tokens),
        out_shape=jax.ShapeDtypeStruct((owners, 2 * STAT, LANES), jnp.float32),
        compiler_params=params(),
        cost_estimate=cost(2 * 1536 * 1536 * LANES, 1 << 20),
        name="total_stats",
    )(table, arrived)


def backward_tile(query, upstream, keys, values, masked, total_row, delta_row):
    scores = dot(keys, query, 1, 1)
    if masked is not None:
        scores = jnp.where(masked, NEG_SELF, scores)
    probs = jnp.exp(scores - total_row)
    dots = dot(values, upstream, 1, 1)
    slopes = (probs * (dots - delta_row)).astype(jnp.bfloat16)
    return probs.astype(jnp.bfloat16), slopes


def backward_body(
    table_ref,
    stats_ref,
    head_query_ref,
    tail_query_ref,
    head_value_ref,
    tail_value_ref,
    head_cotangent_ref,
    tail_cotangent_ref,
    prior_query_ref,
    prior_value_ref,
    next_query_ref,
    next_cotangent_ref,
    out_first_ref,
    out_second_ref,
    lse_first_ref,
    lse_second_ref,
    payload_ref,
    back,
    totals,
    next_totals,
    total_cols,
    shaped,
):
    pair = pl.program_id(0)
    hash_round = pl.program_id(1)
    rows = PLACE_ROWS * LANES
    per_round = rows // 2

    @pl.when((pair == 0) & (hash_round == 0))
    def _():
        place_row = table_row(table_ref, PLACE, PLACE_ROWS)
        next_row = table_row(table_ref, NEXT_PLACE, NEXT_ROWS)
        back[...] = match_cols(table_cols(table_ref, ARRIVAL, SLOT_ROWS), place_row)
        own_stats = stats_ref[:, :STAT, :].reshape(-1, LANES)
        next_stats = stats_ref[:, STAT:, :].reshape(-1, LANES)
        found = gather_stats(place_row, table_cols(table_ref, ARRIVAL3, SLOT_ROWS), own_stats)
        edge = gather_stats(next_row, table_cols(table_ref, NEXT3, SLOT_ROWS), next_stats)
        for each in range(2):
            totals[each] = found[:, each * per_round : (each + 1) * per_round]
            next_totals[each] = edge[:, each * GROUP : (each + 1) * GROUP]
        padded = jnp.concatenate([found, jnp.zeros((LANES - STAT, rows), jnp.float32)])
        total_cols[...] = padded.T.reshape(2, per_round, LANES)

    own = iota((2 * GROUP, GROUP), 0) == iota((2 * GROUP, GROUP), 1) + GROUP
    stat = totals[hash_round]
    edge_stat = next_totals[hash_round]
    columns_of_stat = total_cols[hash_round]
    sublane = iota((STAT, 1), 0)
    lane = iota((1, LANES), 1)

    def row_of(table, index):
        return jnp.sum(jnp.where(sublane == index, table, 0.0), 0, keepdims=True)

    def col_of(table, index):
        return jnp.sum(jnp.where(lane == index, table, 0.0), 1, keepdims=True)

    for local in range(2):
        columns = slice(local * DH, (local + 1) * DH)
        head = pair * 2 + local
        total_row, delta_row = row_of(stat, head), row_of(stat, head + 4)
        edge_total, edge_delta = row_of(edge_stat, head), row_of(edge_stat, head + 4)
        raw = jnp.concatenate([head_query_ref[:, columns], tail_query_ref[:, columns]])
        values = jnp.concatenate([head_value_ref[:, columns], tail_value_ref[:, columns]])
        upstream = jnp.concatenate(
            [head_cotangent_ref[:, columns], tail_cotangent_ref[:, columns]]
        )
        units, inverse = unit_rows(raw)
        keys = units.astype(jnp.bfloat16)
        tail_keys = unit_rows(prior_query_ref[:, columns])[0].astype(jnp.bfloat16)

        keys_first = jnp.concatenate([tail_keys, keys[:GROUP]])
        values_first = jnp.concatenate([prior_value_ref[:, columns], values[:GROUP]])
        probs, slopes = backward_tile(
            raw[:GROUP],
            upstream[:GROUP],
            keys_first,
            values_first,
            own,
            total_row[:, :GROUP],
            delta_row[:, :GROUP],
        )
        query_first = dot(slopes, keys_first, 0, 0)
        unit_first = dot(slopes[GROUP:], raw[:GROUP])
        value_first = dot(probs[GROUP:], upstream[:GROUP])

        probs, slopes = backward_tile(
            raw[GROUP:],
            upstream[GROUP:],
            keys,
            values,
            own,
            total_row[:, GROUP:],
            delta_row[:, GROUP:],
        )
        query_second = dot(slopes, keys, 0, 0)
        unit_both = dot(slopes, raw[GROUP:])
        value_both = dot(probs, upstream[GROUP:])

        next_query = next_query_ref[:, columns]
        next_upstream = next_cotangent_ref[:, columns]
        probs, slopes = backward_tile(
            next_query,
            next_upstream,
            keys[GROUP:],
            values[GROUP:],
            None,
            edge_total,
            edge_delta,
        )
        unit_last = dot(slopes, next_query)
        value_last = dot(probs, next_upstream)

        for group, (query_slope, unit_slope, value_slope, out_ref, lse_ref) in enumerate(
            (
                (
                    query_first,
                    unit_first + unit_both[:GROUP],
                    value_first + value_both[:GROUP],
                    out_first_ref,
                    lse_first_ref,
                ),
                (
                    query_second,
                    unit_both[GROUP:] + unit_last,
                    value_both[GROUP:] + value_last,
                    out_second_ref,
                    lse_second_ref,
                ),
            )
        ):
            kept = slice(group * GROUP, (group + 1) * GROUP)
            unit = units[kept]
            key_slope = inverse[kept] * (
                unit_slope - unit * jnp.sum(unit * unit_slope, -1, keepdims=True)
            )
            share = jnp.exp(col_of(lse_ref[...] - columns_of_stat[kept], head))
            wide = 2 * DH
            shaped[kept, columns] = (out_ref[:, columns] * share).astype(jnp.bfloat16)
            shaped[kept, wide + local * DH : wide + (local + 1) * DH] = (
                query_slope + key_slope
            ).astype(jnp.bfloat16)
            shaped[kept, 2 * wide + local * DH : 2 * wide + (local + 1) * DH] = (
                value_slope.astype(jnp.bfloat16)
            )

    @pl.when(hash_round == 0)
    def _():
        payload_ref[...] = dot(back[:, :per_round], shaped[...]).astype(jnp.bfloat16)

    @pl.when(hash_round == 1)
    def _():
        payload_ref[...] += dot(back[:, per_round:], shaped[...]).astype(jnp.bfloat16)


def backward(table, stats, heads, tail, tail_cotangent, prior_tail, nexts, outs, lses):
    rows = PLACE_ROWS * LANES
    per_round = rows // 2
    slots = SLOT_ROWS * LANES
    wide = 2 * DH

    def whole(array):
        return pl.BlockSpec(array.shape, lambda p, r: (0,) * array.ndim)

    small = [table, stats]
    head_query, head_value, head_cotangent = heads
    return pl.pallas_call(
        backward_body,
        grid=(2, 2),
        in_specs=[whole(array) for array in small]
        + [group_spec()] * 3
        + [group_spec(2)]
        + [group_spec()] * 3
        + [group_spec(2)]
        + [group_spec()] * 4
        + [stat_spec()] * 2,
        out_specs=pl.BlockSpec((slots, 3 * wide), lambda p, r: (0, p)),
        out_shape=jax.ShapeDtypeStruct((slots, 6 * wide), jnp.bfloat16),
        scratch_shapes=[
            pltpu.VMEM((slots, rows), jnp.bfloat16),
            pltpu.VMEM((2, STAT, per_round), jnp.float32),
            pltpu.VMEM((2, STAT, GROUP), jnp.float32),
            pltpu.VMEM((2, per_round, LANES), jnp.float32),
            pltpu.VMEM((per_round, 3 * wide), jnp.bfloat16),
        ],
        compiler_params=params(),
        cost_estimate=cost(8e9, 1.5e7, 3e6),
        name="backward",
    )(
        *small,
        head_query,
        tail,
        head_value,
        tail,
        head_cotangent,
        tail_cotangent,
        prior_tail,
        prior_tail,
        *nexts,
        *outs,
        *lses,
    )


def combine_body(table_ref, arrived_ref, *out_refs):
    tokens, wide = out_refs[0].shape
    chosen = match(iota((tokens, 1), 0), table_row(table_ref, SEND, SLOT_ROWS))
    found = dot(chosen, arrived_ref[...])
    for place, out_ref in enumerate(out_refs):
        out_ref[...] = found[:, place * wide : (place + 1) * wide].astype(jnp.bfloat16)


def combine(table, arrived, tokens):
    slots, width = arrived.shape
    wide = width // 6
    return pl.pallas_call(
        combine_body,
        grid=(2,),
        in_specs=[
            pl.BlockSpec((LANES, LANES), lambda i: (0, 0)),
            pl.BlockSpec((slots, 3 * wide), lambda i: (0, i)),
        ],
        out_specs=[pl.BlockSpec((tokens, wide), lambda i: (0, i))] * 3,
        out_shape=[jax.ShapeDtypeStruct((tokens, 2 * wide), jnp.bfloat16)] * 3,
        compiler_params=params(),
        cost_estimate=cost(2 * slots * tokens * width, 2 * (slots + tokens) * width),
        name="combine_rows",
    )(table, arrived)


def per_device(query_key, value, attended_cotangent, send_rows, arrival_count, receive_slot):
    tokens, row_width = query_key.shape
    rounds = send_rows.shape[0]
    owners = lax.axis_size("seq")
    capacity = send_rows.shape[1] // owners
    per_owner = rounds * capacity
    slots = owners * per_owner

    code = (tokens * jnp.arange(rounds, dtype=jnp.int32))[:, None]
    half = lax.axis_index("head")

    def by_owner(table):
        return table.reshape(rounds, owners, capacity).transpose(1, 0, 2).reshape(owners, per_owner)

    def by_third(codes):
        return codes.reshape(owners, 3, STAT).transpose(1, 0, 2)

    def rows_of(codes, count):
        rows = codes.reshape(-1, LANES)
        return jnp.pad(rows, ((0, count - rows.shape[0]), (0, 0)), constant_values=-1)

    def sent(packed):
        return exchange(packed.reshape(owners, per_owner, -1)).reshape(slots, -1)

    blocks = send_rows.reshape(rounds, owners, capacity)
    send_rows = jnp.where(half == 0, blocks, blocks[:, ::-1]).reshape(rounds, -1)
    send = by_owner(send_rows)
    send_blocks = send.reshape(6, 2, LANES)
    send_blocks = jnp.pad(send_blocks, ((0, 0), (0, STAT - 2), (0, 0))).reshape(-1, LANES)
    packed = pack(send_blocks, query_key, value, attended_cotangent)

    arrival_count = to_place(arrival_count)
    receive_slot = to_place(receive_slot)
    running = jnp.cumsum(arrival_count, axis=1)
    within = jnp.arange(capacity, dtype=jnp.int32)
    arrival = (running - arrival_count + code)[:, :, None] + within
    arrival = by_owner(jnp.where(within < arrival_count[:, :, None], arrival, -1))
    place = receive_slot + code
    next_arrival = to_prior(arrival)
    next_place = to_prior(place[:, :GROUP])
    table = jnp.concatenate(
        [
            rows_of(arrival, ARRIVAL3 - ARRIVAL),
            rows_of(by_third(arrival), NEXT3 - ARRIVAL3),
            rows_of(by_third(next_arrival), PLACE - NEXT3),
            rows_of(place, NEXT_PLACE - PLACE),
            rows_of(next_place, SEND - NEXT_PLACE),
            rows_of(send, SEND3 - SEND),
            rows_of(by_third(by_owner(send_rows + code)), HALF - SEND3),
            jnp.full((LANES - HALF, LANES), half, jnp.int32),
        ]
    )

    arrived, table = lax.optimization_barrier((sent(packed), table))
    tail = sort_tail(table, arrived, 2 * row_width)
    prior_tail = to_next(tail)
    head_query, head_value, head_cotangent, tail_cotangent, out_second, stat_second = forward_own(
        table, arrived, tail
    )
    out_first, stat_first, stats = forward_edge(
        table, head_query, head_value, head_cotangent, prior_tail, stat_second
    )
    next_query = to_prior(head_query)
    next_cotangent = to_prior(head_cotangent)
    home_stats = exchange(stats.reshape(owners, STAT, LANES)).reshape(-1, LANES)
    totals = exchange(total_stats(table, home_stats, tokens))
    payload = backward(
        table,
        totals,
        (head_query, head_value, head_cotangent),
        tail,
        tail_cotangent,
        prior_tail,
        (next_query, next_cotangent),
        (out_first, out_second),
        (stat_first, stat_second),
    )
    return tuple(combine(table, sent(payload), tokens))


def solution(mesh):
    in_specs = (
        P("seq", "head"),
        P("seq", "head"),
        P("seq", "head"),
        P(None, "seq"),
        P(None, "seq"),
        P(None, "seq"),
    )
    out_specs = (P("seq", "head"), P("seq", "head"), P("seq", "head"))
    return jax.shard_map(
        per_device, mesh=mesh, in_specs=in_specs, out_specs=out_specs, check_vma=False
    )
```

```python
import functools

import jax
import jax.numpy as jnp
from jax import lax
from jax.experimental import pallas as pl
from jax.experimental.pallas import tpu as pltpu
from jax.sharding import PartitionSpec as P

DH = 128
GROUP = 256
NEG_SELF = -100000.0
EPS_KEY = 1e-06
LANES = 128
STAT = 8
PIECES = 3
MIB = 1 << 20


def dot(left, right, left_axis=1, right_axis=0):
    return lax.dot_general(
        left,
        right,
        (((left_axis,), (right_axis,)), ((), ())),
        preferred_element_type=jnp.float32,
    )


def params(mib=62):
    return pltpu.CompilerParams(vmem_limit_bytes=mib * MIB)


def cost(flops, moved, exps=0):
    return pl.CostEstimate(flops=int(flops), bytes_accessed=int(moved), transcendentals=int(exps))


def routed(block, route_of):
    owners, halves = lax.axis_size("seq"), lax.axis_size("head")
    route = [
        (i * halves + half, route_of(i, half, owners) * halves + half)
        for i in range(owners)
        for half in range(halves)
    ]
    return lax.ppermute(block, ("seq", "head"), route)


def to_next(block):
    return routed(block, lambda i, half, n: (i + (1 if half == 0 else -1)) % n)


def to_prior(block):
    return routed(block, lambda i, half, n: (i - (1 if half == 0 else -1)) % n)


def to_place_prior(block):
    return routed(block, lambda i, half, n: (i - 1) % n if half == 0 else n - 1 - (i - 1) % n)


def to_place(block):
    return routed(block, lambda i, half, n: i if half == 0 else n - 1 - i)


def exchange(block):
    return lax.all_to_all(block, "seq", split_axis=0, concat_axis=0, tiled=True)


def match(left, right):
    return jnp.where(left == right, 1.0, 0.0).astype(jnp.bfloat16)


ARRIVAL, ARRIVAL3, NEXT3, PLACE, NEXT_PLACE, SEND, SEND3, HALF = 0, 12, 24, 36, 44, 48, 60, 72
FIRST16, LAST16, SEND_CODE = 73, 81, 89
SLOT_ROWS, PLACE_ROWS, NEXT_ROWS, PART_ROWS = 12, 8, 4, 8


def table_row(table_ref, start, count):
    return jnp.concatenate([table_ref[start + i : start + i + 1, :] for i in range(count)], axis=1)


def table_cols(table_ref, start, count):
    turned = table_ref[...].T
    return [turned[:, start + i : start + i + 1] for i in range(count)]


def match_cols(cols, row):
    return jnp.concatenate([match(col, row) for col in cols])


def anywhere(count):
    return [pl.BlockSpec(memory_space=pl.ANY) for _ in range(count)]


def table_spec():
    return pl.BlockSpec((LANES, LANES), lambda *_: (0, 0))


def started(sources, targets, sems, first=0):
    copies = [
        pltpu.make_async_copy(source, target, sems.at[first + i])
        for i, (source, target) in enumerate(zip(sources, targets))
    ]
    for copy in copies:
        copy.start()
    return copies


def iota(shape, axis):
    return lax.broadcasted_iota(jnp.int32, shape, axis)


def pieces_of(wide):
    first = wide.astype(jnp.bfloat16)
    rest = wide - first.astype(jnp.float32)
    second = rest.astype(jnp.bfloat16)
    third = (rest - second.astype(jnp.float32)).astype(jnp.bfloat16)
    return first, second, third


def unit_rows(raw_rows):
    wide = raw_rows.astype(jnp.float32)
    inverse = lax.rsqrt(jnp.sum(wide * wide, -1, keepdims=True) + EPS_KEY)
    return wide * inverse, inverse


def pack_body(index_ref, *refs):
    sources, out_ref, held, staged, load, store = refs[:3], *refs[3:]
    tokens, width = sources[0].shape
    arriving = started(sources, [held.at[i] for i in range(3)], load)
    turned = index_ref[...].T
    chosen = match_cols(
        [turned[:, i : i + 1] for i in range(SLOT_ROWS)], iota((LANES, tokens), 1)
    )
    steps = 4
    block = chosen.shape[0] // steps
    leaving = []
    for step in range(steps):
        rows = slice(step * block, (step + 1) * block)
        for place in range(3):
            if step == 0:
                arriving[place].wait()
            staged[rows, place * width : (place + 1) * width] = dot(
                chosen[rows], held[place]
            ).astype(jnp.bfloat16)
        leaving += started(
            [staged.at[pl.ds(step * block, block)]],
            [out_ref.at[pl.ds(step * block, block)]],
            store,
            step,
        )
    for copy in leaving:
        copy.wait()


def pack(index, *sources):
    slots = SLOT_ROWS * LANES
    tokens, width = sources[0].shape
    total = width * len(sources)
    return pl.pallas_call(
        pack_body,
        in_specs=[pl.BlockSpec(index.shape, lambda *_: (0, 0))] + anywhere(3),
        out_specs=anywhere(1)[0],
        out_shape=jax.ShapeDtypeStruct((slots, total), jnp.bfloat16),
        scratch_shapes=[
            pltpu.VMEM((3, tokens, width), jnp.bfloat16),
            pltpu.VMEM((slots, total), jnp.bfloat16),
            pltpu.SemaphoreType.DMA((3,)),
            pltpu.SemaphoreType.DMA((4,)),
        ],
        compiler_params=params(),
        cost_estimate=cost(2 * slots * tokens * total, 2 * (slots + tokens) * total),
        name="pack_rows",
    )(index, *sources)


def place_cols(table_ref, group):
    cols = table_cols(table_ref, PLACE, PLACE_ROWS)
    each = GROUP // LANES
    first, second = group * each, PLACE_ROWS // 2 + group * each
    return cols[first : first + each], cols[second : second + each]


def tail_body(table_ref, arrived_ref, tail_ref, held, staged, load, store):
    parts, _, wide = held.shape
    columns = [pl.ds(i * wide, wide) for i in range(parts)]
    arriving = started(
        [arrived_ref.at[:, each] for each in columns], [held.at[i] for i in range(parts)], load
    )
    first, second = place_cols(table_ref, 1)
    chosen = match_cols(first + second, table_row(table_ref, ARRIVAL, SLOT_ROWS))
    leaving = []
    for part in range(parts):
        arriving[part].wait()
        staged[part] = dot(chosen, held[part]).astype(jnp.bfloat16)
        leaving += started([staged.at[part]], [tail_ref.at[:, columns[part]]], store, part)
    for copy in leaving:
        copy.wait()


def sort_tail(table, arrived, width):
    slots = arrived.shape[0]
    wide = width // 4
    return pl.pallas_call(
        tail_body,
        in_specs=[table_spec()] + anywhere(1),
        out_specs=anywhere(1)[0],
        out_shape=jax.ShapeDtypeStruct((2 * GROUP, width), jnp.bfloat16),
        scratch_shapes=[
            pltpu.VMEM((4, slots, wide), jnp.bfloat16),
            pltpu.VMEM((4, 2 * GROUP, wide), jnp.bfloat16),
            pltpu.SemaphoreType.DMA((4,)),
            pltpu.SemaphoreType.DMA((4,)),
        ],
        compiler_params=params(),
        cost_estimate=cost(4 * slots * GROUP * width, 2 * (slots + 2 * GROUP) * width),
        name="sort_tail",
    )(table, arrived)


def forward_tile(query, keys, values):
    scores = dot(query, keys, 1, 1)
    own = iota((GROUP, 2 * GROUP), 1) == iota((GROUP, 2 * GROUP), 0) + GROUP
    scores = jnp.where(own, NEG_SELF, scores)
    top = jnp.max(scores, -1, keepdims=True)
    raised = jnp.exp(scores - top)
    total = jnp.sum(raised, -1, keepdims=True)
    weights = (raised * (1.0 / total)).astype(jnp.bfloat16)
    return dot(weights, values), top + jnp.log(total)


def forward_pair(pair, query, raw, values, cotangent, out_ref):
    lane = iota((GROUP, LANES), 1) % STAT
    stat = jnp.zeros((GROUP, LANES), jnp.float32)
    for local in range(2):
        columns = slice(local * DH, (local + 1) * DH)
        keys = unit_rows(raw[:, columns])[0].astype(jnp.bfloat16)
        partial, lse = forward_tile(query[:, columns], keys, values[:, columns])
        out_ref[:, columns] = partial
        delta = jnp.sum(partial * cotangent[:, columns].astype(jnp.float32), -1, keepdims=True)
        head = pair * 2 + local
        stat = jnp.where(lane == head, lse, jnp.where(lane == head + 4, delta, stat))
    return stat


def own_body(
    table_ref,
    arrived_query_ref,
    arrived_value_ref,
    arrived_cotangent_ref,
    tail_query_ref,
    tail_value_ref,
    head_query_ref,
    head_value_ref,
    head_cotangent_ref,
    tail_cotangent_ref,
    out_ref,
    stat_ref,
    chosen,
):
    pair = pl.program_id(0)
    hash_round = pl.program_id(1)

    @pl.when((pair == 0) & (hash_round == 0))
    def _():
        row = table_row(table_ref, ARRIVAL, SLOT_ROWS)
        heads, tails = place_cols(table_ref, 0), place_cols(table_ref, 1)
        for each in range(2):
            chosen[each] = match_cols(heads[each] + tails[each], row)

    select_head = chosen[hash_round, :GROUP]
    query = dot(select_head, arrived_query_ref[...]).astype(jnp.bfloat16)
    value = dot(select_head, arrived_value_ref[...]).astype(jnp.bfloat16)
    cotangent = dot(chosen[hash_round], arrived_cotangent_ref[...]).astype(jnp.bfloat16)
    head_query_ref[...] = query
    head_value_ref[...] = value
    head_cotangent_ref[...] = cotangent[:GROUP]
    tail_cotangent_ref[...] = cotangent[GROUP:]
    stat_ref[...] = forward_pair(
        pair,
        tail_query_ref[...],
        jnp.concatenate([query, tail_query_ref[...]]),
        jnp.concatenate([value, tail_value_ref[...]]),
        cotangent[GROUP:],
        out_ref,
    )


def group_spec(offset=0):
    return pl.BlockSpec((GROUP, 2 * DH), lambda p, r: (r, p + offset))


def stat_spec():
    return pl.BlockSpec((GROUP, LANES), lambda p, r: (r, p))


def forward_own(table, arrived, tail):
    slots, width = arrived.shape
    wide = width // 6
    rows = 2 * GROUP
    array = jax.ShapeDtypeStruct((rows, width // 3), jnp.bfloat16)
    return pl.pallas_call(
        own_body,
        grid=(2, 2),
        in_specs=[pl.BlockSpec((LANES, LANES), lambda p, r: (0, 0))]
        + [pl.BlockSpec((slots, wide), lambda p, r, k=k: (0, p + 2 * k)) for k in range(3)]
        + [group_spec(), group_spec(2)],
        out_specs=[group_spec()] * 5 + [stat_spec()],
        out_shape=[array] * 4
        + [
            jax.ShapeDtypeStruct((rows, width // 3), jnp.float32),
            jax.ShapeDtypeStruct((rows, 2 * LANES), jnp.float32),
        ],
        scratch_shapes=[pltpu.VMEM((2, 2 * GROUP, slots), jnp.bfloat16)],
        compiler_params=params(),
        cost_estimate=cost(5e9, 1e7, 8 * GROUP * 512),
        name="forward_own",
    )(table, arrived, arrived, arrived, tail, tail)


def edge_body(
    table_ref,
    query_ref,
    value_ref,
    cotangent_ref,
    prior_query_ref,
    prior_value_ref,
    second_stat_ref,
    out_ref,
    stat_ref,
    stats_ref,
    both,
):
    pair = pl.program_id(0)
    hash_round = pl.program_id(1)
    stat = forward_pair(
        pair,
        query_ref[...],
        jnp.concatenate([prior_query_ref[...], query_ref[...]]),
        jnp.concatenate([prior_value_ref[...], value_ref[...]]),
        cotangent_ref[...],
        out_ref,
    )
    stat_ref[...] = stat

    @pl.when(pair == 0)
    def _():
        both[hash_round, :GROUP] = stat
        both[hash_round, GROUP:] = second_stat_ref[...]

    @pl.when(pair == 1)
    def _():
        both[hash_round, :GROUP] += stat
        both[hash_round, GROUP:] += second_stat_ref[...]

    @pl.when((pair == 1) & (hash_round == 1))
    def _():
        rows = 4 * GROUP
        piece = iota((rows, LANES), 1) // (PIECES * STAT)
        first, second, third = pieces_of(both[...].reshape(rows, LANES))
        nothing = jnp.zeros((rows, LANES), jnp.bfloat16)
        stats = jnp.where(
            piece == 0,
            first,
            jnp.where(piece == 1, second, jnp.where(piece == 2, third, nothing)),
        )
        place_row = table_row(table_ref, PLACE, PLACE_ROWS)
        third_slots = stats_ref.shape[0]
        arrival_cols = table_cols(table_ref, ARRIVAL3, SLOT_ROWS)
        lane_third = (iota((third_slots, LANES), 1) % (3 * STAT)) // STAT
        result = jnp.zeros((third_slots, LANES), jnp.float32)
        for third in range(3):
            back = match_cols(arrival_cols[4 * third : 4 * third + 4], place_row)
            result = jnp.where(lane_third == third, dot(back, stats), result)
        stats_ref[...] = result


def forward_edge(table, query, value, cotangent, prior_tail, second_stat):
    rows, width = query.shape
    third_slots = SLOT_ROWS * LANES // 3
    return pl.pallas_call(
        edge_body,
        grid=(2, 2),
        in_specs=[pl.BlockSpec((LANES, LANES), lambda p, r: (0, 0))]
        + [group_spec()] * 4
        + [group_spec(2), stat_spec()],
        out_specs=[
            group_spec(),
            stat_spec(),
            pl.BlockSpec((third_slots, LANES), lambda p, r: (0, 0)),
        ],
        out_shape=[
            jax.ShapeDtypeStruct((rows, width), jnp.float32),
            jax.ShapeDtypeStruct((rows, 2 * LANES), jnp.float32),
            jax.ShapeDtypeStruct((third_slots, LANES), jnp.float32),
        ],
        scratch_shapes=[pltpu.VMEM((2, 2 * GROUP, LANES), jnp.float32)],
        compiler_params=params(),
        cost_estimate=cost(2e9, 4e6, 8 * GROUP * 512),
        name="forward_edge",
    )(table, query, value, cotangent, prior_tail, prior_tail, second_stat)


def gather_stats(codes_row, slot_cols, stats):
    narrow = stats.astype(jnp.bfloat16)
    total = None
    for third in range(3):
        chosen = match_cols(slot_cols[4 * third : 4 * third + 4], codes_row)
        found = dot(narrow, chosen, 0, 0)
        for piece in range(PIECES):
            at = piece * PIECES * STAT + third * STAT
            part = found[at : at + STAT]
            total = part if total is None else total + part
    return total


def found_at_tokens(tokens, table_ref, stats):
    slot_cols = table_cols(table_ref, SEND3, SLOT_ROWS)
    found = gather_stats(iota((1, 2 * tokens), 1), slot_cols, stats)
    lse_first, lse_second = found[:4, :tokens], found[:4, tokens:]
    top = jnp.maximum(lse_first, lse_second)
    total = top + jnp.log(jnp.exp(lse_first - top) + jnp.exp(lse_second - top))
    shares = jnp.exp(lse_first - total), jnp.exp(lse_second - total)
    delta = found[4:, :tokens] * shares[0] + found[4:, tokens:] * shares[1]
    return slot_cols, total, delta, shares


def total_body(tokens, table_ref, arrived_ref, out_ref):
    slot_cols, total, delta, _ = found_at_tokens(tokens, table_ref, arrived_ref[...])
    stat = jnp.concatenate([total, delta])
    first, second, third_piece = [member.astype(jnp.float32) for member in pieces_of(stat)]
    spare = jnp.zeros((LANES - 9 * STAT, tokens), jnp.float32)
    table = jnp.concatenate(
        [first] * 3 + [second] * 3 + [third_piece] * 3 + [spare]
    ).astype(jnp.bfloat16)
    third_slots = arrived_ref.shape[0]
    lane_third = (iota((third_slots, LANES), 1) % (3 * STAT)) // STAT
    result = jnp.zeros((third_slots, LANES), jnp.float32)
    for third in range(3):
        codes = slot_cols[4 * third : 4 * third + 4]
        cols = [jnp.where(code >= tokens, code - tokens, code) for code in codes]
        chosen = match_cols(cols, iota((LANES, tokens), 1))
        result = jnp.where(lane_third == third, dot(chosen, table, 1, 1), result)
    owners = third_slots // STAT
    by_owner = result.reshape(owners, STAT, LANES)
    out_ref[:, :STAT, :] = by_owner
    above = jnp.concatenate([by_owner[1:], by_owner[:1]])
    below = jnp.concatenate([by_owner[owners - 1 :], by_owner[: owners - 1]])
    half = table_ref[HALF : HALF + 1, :]
    out_ref[:, STAT:, :] = jnp.where(half[None] == 0, above, below)


def total_stats(table, arrived, tokens):
    owners = arrived.shape[0] // STAT
    return pl.pallas_call(
        functools.partial(total_body, tokens),
        out_shape=jax.ShapeDtypeStruct((owners, 2 * STAT, LANES), jnp.float32),
        compiler_params=params(),
        cost_estimate=cost(2 * 1536 * 1536 * LANES, 1 << 20),
        name="total_stats",
    )(table, arrived)


def prepare_body(tokens, table_ref, arrived_ref, first_ref, second_ref, payload_ref, share_ref):
    @pl.when(pl.program_id(0) == 0)
    def _():
        shares = found_at_tokens(tokens, table_ref, arrived_ref[...])[3]
        spare = jnp.zeros((LANES - STAT, tokens), jnp.float32)
        share_ref[...] = jnp.concatenate([*shares, spare]).T

    back = match_cols(
        table_cols(table_ref, ARRIVAL, SLOT_ROWS), table_row(table_ref, PLACE, PLACE_ROWS)
    )
    rows = [first_ref[:GROUP], second_ref[:GROUP], first_ref[GROUP:], second_ref[GROUP:]]
    payload_ref[...] = dot(back, jnp.concatenate(rows).astype(jnp.bfloat16)).astype(jnp.bfloat16)


def prepare(table, home_stats, outs, tokens):
    slots = SLOT_ROWS * LANES
    rows, width = outs[0].shape
    wide = width // 2
    return pl.pallas_call(
        functools.partial(prepare_body, tokens),
        grid=(2,),
        in_specs=[
            table_spec(),
            pl.BlockSpec(home_stats.shape, lambda i: (0, 0)),
            pl.BlockSpec((rows, wide), lambda i: (0, i)),
            pl.BlockSpec((rows, wide), lambda i: (0, i)),
        ],
        out_specs=[
            pl.BlockSpec((slots, wide), lambda i: (0, i)),
            pl.BlockSpec((tokens, LANES), lambda i: (0, 0)),
        ],
        out_shape=[
            jax.ShapeDtypeStruct((slots, 3 * width), jnp.bfloat16),
            jax.ShapeDtypeStruct((tokens, LANES), jnp.float32),
        ],
        compiler_params=params(),
        cost_estimate=cost(2e9, 1e7),
        name="prepare_outputs",
    )(table, home_stats, *outs)


def backward_tile(query, upstream, keys, values, masked, total_row, delta_row):
    scores = dot(keys, query, 1, 1)
    if masked is not None:
        scores = jnp.where(masked, NEG_SELF, scores)
    probs = jnp.exp(scores - total_row)
    dots = dot(values, upstream, 1, 1)
    slopes = (probs * (dots - delta_row)).astype(jnp.bfloat16)
    return probs.astype(jnp.bfloat16), slopes


def backward_heads(pair, stat, edge_stat, refs, hash_round, shaped):
    heads, tail, tail_cotangent, prior, nexts = refs
    kept = pl.ds(hash_round * GROUP, GROUP)
    own = iota((2 * GROUP, GROUP), 0) == iota((2 * GROUP, GROUP), 1) + GROUP
    width = tail.shape[1] // 2
    for local in range(2):
        head = pair * 2 + local
        columns = pl.ds(head * DH, DH)
        values_at = pl.ds(width + head * DH, DH)
        total_row, delta_row = stat[head : head + 1], stat[head + 4 : head + 5]
        edge_total, edge_delta = edge_stat[head : head + 1], edge_stat[head + 4 : head + 5]
        raw = jnp.concatenate([heads[0][kept, columns], tail[kept, columns]])
        values = jnp.concatenate([heads[1][kept, columns], tail[kept, values_at]])
        upstream = jnp.concatenate([heads[2][kept, columns], tail_cotangent[kept, columns]])
        units, inverse = unit_rows(raw)
        keys = units.astype(jnp.bfloat16)
        prior_keys = unit_rows(prior[kept, columns])[0].astype(jnp.bfloat16)
        keys_first = jnp.concatenate([prior_keys, keys[:GROUP]])
        values_first = jnp.concatenate([prior[kept, values_at], values[:GROUP]])
        probs, slopes = backward_tile(
            raw[:GROUP],
            upstream[:GROUP],
            keys_first,
            values_first,
            own,
            total_row[:, :GROUP],
            delta_row[:, :GROUP],
        )
        query_first = dot(slopes, keys_first, 0, 0)
        unit_first = dot(slopes[GROUP:], raw[:GROUP])
        value_first = dot(probs[GROUP:], upstream[:GROUP])

        probs, slopes = backward_tile(
            raw[GROUP:],
            upstream[GROUP:],
            keys,
            values,
            own,
            total_row[:, GROUP:],
            delta_row[:, GROUP:],
        )
        query_second = dot(slopes, keys, 0, 0)
        unit_both = dot(slopes, raw[GROUP:])
        value_both = dot(probs, upstream[GROUP:])

        next_query = nexts[0][kept, columns]
        next_upstream = nexts[1][kept, columns]
        probs, slopes = backward_tile(
            next_query,
            next_upstream,
            keys[GROUP:],
            values[GROUP:],
            None,
            edge_total,
            edge_delta,
        )
        unit_last = dot(slopes, next_query)
        value_last = dot(probs, next_upstream)

        query_slope = jnp.concatenate([query_first, query_second])
        unit_slope = unit_both + jnp.concatenate([unit_first, unit_last])
        value_slope = value_both + jnp.concatenate([value_first, value_last])
        key_slope = inverse * (
            unit_slope - units * jnp.sum(units * unit_slope, -1, keepdims=True)
        )
        shaped[hash_round, :, local * DH : (local + 1) * DH] = (query_slope + key_slope).astype(
            jnp.bfloat16
        )
        shaped[hash_round, :, (2 + local) * DH : (3 + local) * DH] = value_slope.astype(
            jnp.bfloat16
        )


def backward_body(
    table_ref,
    stats_ref,
    head_query_ref,
    head_value_ref,
    head_cotangent_ref,
    tail_ref,
    tail_cotangent_ref,
    prior_ref,
    next_query_ref,
    next_cotangent_ref,
    _,
    payload_ref,
    stats,
    six,
    double,
    shaped,
    staged,
    load,
    store,
):
    rows = PLACE_ROWS * LANES
    per_round = rows // 2
    sources = [
        stats_ref,
        head_query_ref,
        head_value_ref,
        head_cotangent_ref,
        tail_cotangent_ref,
        next_query_ref,
        next_cotangent_ref,
        tail_ref,
        prior_ref,
    ]
    targets = [stats] + [six.at[i] for i in range(6)] + [double.at[i] for i in range(2)]
    arriving = started(sources, targets, load)
    place_row = table_row(table_ref, PLACE, PLACE_ROWS)
    next_row = table_row(table_ref, NEXT_PLACE, NEXT_ROWS)
    back = [
        match_cols(
            table_cols(table_ref, (FIRST16, LAST16)[each], PART_ROWS),
            place_row[:, each * per_round : (each + 1) * per_round],
        )
        for each in range(2)
    ]
    arriving[0].wait()
    own_stats = stats[:, :STAT, :].reshape(-1, LANES)
    next_stats = stats[:, STAT:, :].reshape(-1, LANES)
    found = gather_stats(place_row, table_cols(table_ref, ARRIVAL3, SLOT_ROWS), own_stats)
    edge = gather_stats(next_row, table_cols(table_ref, NEXT3, SLOT_ROWS), next_stats)
    for copy in arriving[1:]:
        copy.wait()
    refs = (
        (six.at[0], six.at[1], six.at[2]),
        double.at[0],
        six.at[3],
        double.at[1],
        (six.at[4], six.at[5]),
    )
    leaving = []
    width = shaped.shape[2]
    for pair in range(2):
        for hash_round in range(2):
            backward_heads(
                pair,
                found[:, hash_round * per_round : (hash_round + 1) * per_round],
                edge[:, hash_round * GROUP : (hash_round + 1) * GROUP],
                refs,
                hash_round,
                shaped,
            )
        chunks = 2
        for chunk in range(chunks):
            kept = slice(chunk * 1024 // chunks, (chunk + 1) * 1024 // chunks)
            first = dot(back[0][kept], shaped[0]).reshape(-1, 2, STAT, width)
            second = dot(back[1][kept], shaped[1]).reshape(-1, 2, STAT, width)
            whole = jnp.concatenate(
                [first[:, :1], first[:, 1:] + second[:, :1], second[:, 1:]], axis=1
            ).reshape(-1, width)
            count = whole.shape[0]
            at = pl.ds(chunk * count, count)
            staged[pair, at] = whole.astype(jnp.bfloat16)
            leaving += started(
                [staged.at[pair, at]],
                [payload_ref.at[at, pl.ds((pair + 1) * width, width)]],
                store,
                pair * chunks + chunk,
            )
    for copy in leaving:
        copy.wait()


def backward(table, stats, heads, tail, tail_cotangent, prior_tail, nexts, payload):
    slots = SLOT_ROWS * LANES
    rows, width = heads[0].shape
    return pl.pallas_call(
        backward_body,
        in_specs=[table_spec()] + anywhere(10),
        out_specs=anywhere(1)[0],
        out_shape=jax.ShapeDtypeStruct((slots, 3 * width), jnp.bfloat16),
        input_output_aliases={10: 0},
        scratch_shapes=[
            pltpu.VMEM(stats.shape, jnp.float32),
            pltpu.VMEM((6, rows, width), jnp.bfloat16),
            pltpu.VMEM((2, rows, 2 * width), jnp.bfloat16),
            pltpu.VMEM((2, 2 * GROUP, width), jnp.bfloat16),
            pltpu.VMEM((2, slots, width), jnp.bfloat16),
            pltpu.SemaphoreType.DMA((9,)),
            pltpu.SemaphoreType.DMA((4,)),
        ],
        compiler_params=params(),
        cost_estimate=cost(8e9, 1.5e7, 3e6),
        name="backward",
    )(table, stats, *heads, tail, tail_cotangent, prior_tail, *nexts, payload)


def combine_body(
    table_ref, share_ref, arrived_ref, out_ref, first_ref, second_ref, held, staged, load, store
):
    parts, _, wide = held.shape
    tokens = share_ref.shape[0]
    arriving = started(
        [arrived_ref.at[:, pl.ds(i * wide, wide)] for i in range(parts)],
        [held.at[i] for i in range(parts)],
        load,
    )
    token = iota((tokens, 1), 0)
    code = table_row(table_ref, SEND_CODE, SLOT_ROWS)
    by_round = [match(token + tokens * each, code) for each in range(2)]
    chosen = by_round[0] + by_round[1]
    leaving = []
    for part in range(parts):
        arriving[part].wait()
        if part < 2:
            found = 0.0
            for each in range(2):
                at = 4 * each + 2 * part
                share = jnp.concatenate(
                    [
                        jnp.broadcast_to(share_ref[:, at + i : at + i + 1], (tokens, DH))
                        for i in range(2)
                    ],
                    axis=1,
                )
                found = found + share * dot(by_round[each], held[part])
            target = out_ref.at[:, pl.ds(part * wide, wide)]
        else:
            found = dot(chosen, held[part])
            target = (first_ref, second_ref)[part % 2].at[:, pl.ds((part // 2 - 1) * wide, wide)]
        staged[part] = found.astype(jnp.bfloat16)
        leaving += started([staged.at[part]], [target], store, part)
    for copy in leaving:
        copy.wait()


def combine(table, shares, arrived, tokens):
    slots, width = arrived.shape
    wide = width // 6
    return pl.pallas_call(
        combine_body,
        in_specs=[table_spec(), pl.BlockSpec(shares.shape, lambda *_: (0, 0))] + anywhere(1),
        out_specs=anywhere(3),
        out_shape=[jax.ShapeDtypeStruct((tokens, 2 * wide), jnp.bfloat16)] * 3,
        scratch_shapes=[
            pltpu.VMEM((6, slots, wide), jnp.bfloat16),
            pltpu.VMEM((6, tokens, wide), jnp.bfloat16),
            pltpu.SemaphoreType.DMA((6,)),
            pltpu.SemaphoreType.DMA((6,)),
        ],
        compiler_params=params(),
        cost_estimate=cost(2 * slots * tokens * width, 2 * (slots + tokens) * width),
        name="combine_rows",
    )(table, shares, arrived)


def per_device(query_key, value, attended_cotangent, send_rows, arrival_count, receive_slot):
    tokens, row_width = query_key.shape
    rounds = send_rows.shape[0]
    owners = lax.axis_size("seq")
    capacity = send_rows.shape[1] // owners
    per_owner = rounds * capacity
    slots = owners * per_owner

    code = (tokens * jnp.arange(rounds, dtype=jnp.int32))[:, None]
    half = lax.axis_index("head")

    def by_owner(table):
        return table.reshape(rounds, owners, capacity).transpose(1, 0, 2).reshape(owners, per_owner)

    def by_third(codes):
        return codes.reshape(owners, 3, STAT).transpose(1, 0, 2)

    def sent(packed):
        return exchange(packed.reshape(owners, per_owner, -1)).reshape(slots, -1)

    blocks = send_rows.reshape(rounds, owners, capacity)
    send_rows = jnp.where(half == 0, blocks, blocks[:, ::-1]).reshape(rounds, -1)
    send = by_owner(send_rows)
    send_blocks = jnp.pad(send.reshape(-1, LANES), ((0, 4), (0, 0)))
    packed = pack(send_blocks, query_key, value, attended_cotangent)

    within = jnp.arange(capacity, dtype=jnp.int32)

    def arrivals(counts):
        start = jnp.cumsum(counts, axis=1) - counts + code
        codes = jnp.where(within < counts[:, :, None], start[:, :, None] + within, -1)
        return by_owner(codes)

    arrival = arrivals(to_place(arrival_count))
    next_arrival = arrivals(to_place_prior(arrival_count))
    place = to_place(receive_slot) + code
    next_place = to_place_prior(receive_slot[:, :GROUP]) + code
    def half_blocks(codes, first):
        return codes[:, first : first + 2 * STAT]

    members = [
        (ARRIVAL, arrival),
        (ARRIVAL3, by_third(arrival)),
        (NEXT3, by_third(next_arrival)),
        (PLACE, place),
        (NEXT_PLACE, next_place),
        (SEND, send),
        (SEND3, by_third(by_owner(send_rows + code))),
        (HALF, jnp.full((1, LANES), half, jnp.int32)),
        (FIRST16, half_blocks(arrival, 0)),
        (LAST16, half_blocks(arrival, STAT)),
        (SEND_CODE, by_owner(send_rows + code)),
    ]
    rows = [codes.reshape(-1, LANES) for _, codes in members]
    assert [at for at, _ in members] == [sum(map(len, rows[:i])) for i in range(len(rows))]
    table = jnp.concatenate(rows)
    table = jnp.pad(table, ((0, LANES - len(table)), (0, 0)), constant_values=-1)

    arrived, table = lax.optimization_barrier((sent(packed), table))
    tail = sort_tail(table, arrived, 2 * row_width)
    prior_tail = to_next(tail)
    head_query, head_value, head_cotangent, tail_cotangent, out_second, stat_second = forward_own(
        table, arrived, tail
    )
    out_first, stat_first, stats = forward_edge(
        table, head_query, head_value, head_cotangent, prior_tail, stat_second
    )
    next_query = to_prior(head_query)
    next_cotangent = to_prior(head_cotangent)
    home_stats = exchange(stats.reshape(owners, STAT, LANES)).reshape(-1, LANES)
    totals = exchange(total_stats(table, home_stats, tokens))
    payload, shares = prepare(table, home_stats, (out_first, out_second), tokens)
    payload = backward(
        table,
        totals,
        (head_query, head_value, head_cotangent),
        tail,
        tail_cotangent,
        prior_tail,
        (next_query, next_cotangent),
        payload,
    )
    return tuple(combine(table, shares, sent(payload), tokens))


def solution(mesh):
    in_specs = (
        P("seq", "head"),
        P("seq", "head"),
        P("seq", "head"),
        P(None, "seq"),
        P(None, "seq"),
        P(None, "seq"),
    )
    out_specs = (P("seq", "head"), P("seq", "head"), P("seq", "head"))
    return jax.shard_map(
        per_device, mesh=mesh, in_specs=in_specs, out_specs=out_specs, check_vma=False
    )
```

```python
import functools

import jax
import jax.numpy as jnp
from jax import lax
from jax.experimental import pallas as pl
from jax.experimental.pallas import tpu as pltpu
from jax.sharding import PartitionSpec as P

DH = 128
GROUP = 256
NEG_SELF = -100000.0
EPS_KEY = 1e-06
LANES = 128
STAT = 8
PIECES = 3
MIB = 1 << 20


def dot(left, right, left_axis=1, right_axis=0):
    return lax.dot_general(
        left,
        right,
        (((left_axis,), (right_axis,)), ((), ())),
        preferred_element_type=jnp.float32,
    )


def params(mib=62):
    return pltpu.CompilerParams(vmem_limit_bytes=mib * MIB)


def cost(flops, moved, exps=0):
    return pl.CostEstimate(flops=int(flops), bytes_accessed=int(moved), transcendentals=int(exps))


def routed(block, route_of):
    owners, halves = lax.axis_size("seq"), lax.axis_size("head")
    route = [
        (i * halves + half, route_of(i, half, owners) * halves + half)
        for i in range(owners)
        for half in range(halves)
    ]
    return lax.ppermute(block, ("seq", "head"), route)


def to_next(block):
    return routed(block, lambda i, half, n: (i + (1 if half == 0 else -1)) % n)


def to_prior(block):
    return routed(block, lambda i, half, n: (i - (1 if half == 0 else -1)) % n)


def to_place_prior(block):
    return routed(block, lambda i, half, n: (i - 1) % n if half == 0 else n - 1 - (i - 1) % n)


def to_place(block):
    return routed(block, lambda i, half, n: i if half == 0 else n - 1 - i)


def exchange(block):
    return lax.all_to_all(block, "seq", split_axis=0, concat_axis=0, tiled=True)


def match(left, right):
    return jnp.where(left == right, 1.0, 0.0).astype(jnp.bfloat16)


ARRIVAL, ARRIVAL3, NEXT3, PLACE, NEXT_PLACE, SEND, SEND3, HALF = 0, 12, 24, 36, 44, 48, 60, 72
FIRST16, LAST16, SEND_CODE = 73, 81, 89
SLOT_ROWS, PLACE_ROWS, NEXT_ROWS, PART_ROWS = 12, 8, 4, 8


def table_row(table_ref, start, count):
    return jnp.concatenate([table_ref[start + i : start + i + 1, :] for i in range(count)], axis=1)


def table_cols(table_ref, start, count):
    turned = table_ref[...].T
    return [turned[:, start + i : start + i + 1] for i in range(count)]


def match_cols(cols, row):
    return jnp.concatenate([match(col, row) for col in cols])


def anywhere(count):
    return [pl.BlockSpec(memory_space=pl.ANY) for _ in range(count)]


def table_spec():
    return pl.BlockSpec((LANES, LANES), lambda *_: (0, 0))


def started(sources, targets, sems, first=0):
    copies = [
        pltpu.make_async_copy(source, target, sems.at[first + i])
        for i, (source, target) in enumerate(zip(sources, targets))
    ]
    for copy in copies:
        copy.start()
    return copies


def iota(shape, axis):
    return lax.broadcasted_iota(jnp.int32, shape, axis)


def pieces_of(wide):
    first = wide.astype(jnp.bfloat16)
    rest = wide - first.astype(jnp.float32)
    second = rest.astype(jnp.bfloat16)
    third = (rest - second.astype(jnp.float32)).astype(jnp.bfloat16)
    return first, second, third


def unit_rows(raw_rows):
    wide = raw_rows.astype(jnp.float32)
    inverse = lax.rsqrt(jnp.sum(wide * wide, -1, keepdims=True) + EPS_KEY)
    return wide * inverse, inverse


def pack_body(index_ref, *refs):
    sources, out_ref, held, staged, chosen, load, store = refs[:3], *refs[3:]
    tokens, width = sources[0].shape
    arriving = started(sources, [held.at[i] for i in range(3)], load)
    turned = index_ref[...].T
    chosen[...] = match_cols(
        [turned[:, i : i + 1] for i in range(SLOT_ROWS)], iota((LANES, tokens), 1)
    )
    steps = 4
    block = chosen.shape[0] // steps
    leaving = []
    for step in range(steps):
        rows = slice(step * block, (step + 1) * block)
        for place in range(3):
            if step == 0:
                arriving[place].wait()
            staged[rows, place * width : (place + 1) * width] = dot(
                chosen[rows], held[place]
            ).astype(jnp.bfloat16)
        leaving += started(
            [staged.at[pl.ds(step * block, block)]],
            [out_ref.at[pl.ds(step * block, block)]],
            store,
            step,
        )
    for copy in leaving:
        copy.wait()


def pack(index, *sources):
    slots = SLOT_ROWS * LANES
    tokens, width = sources[0].shape
    total = width * len(sources)
    return pl.pallas_call(
        pack_body,
        in_specs=[pl.BlockSpec(index.shape, lambda *_: (0, 0))] + anywhere(3),
        out_specs=anywhere(1)[0],
        out_shape=jax.ShapeDtypeStruct((slots, total), jnp.bfloat16),
        scratch_shapes=[
            pltpu.VMEM((3, tokens, width), jnp.bfloat16),
            pltpu.VMEM((slots, total), jnp.bfloat16),
            pltpu.VMEM((slots, tokens), jnp.bfloat16),
            pltpu.SemaphoreType.DMA((3,)),
            pltpu.SemaphoreType.DMA((4,)),
        ],
        compiler_params=params(),
        cost_estimate=cost(2 * slots * tokens * total, 2 * (slots + tokens) * total),
        name="pack_rows",
    )(index, *sources)


def place_cols(table_ref, group):
    cols = table_cols(table_ref, PLACE, PLACE_ROWS)
    each = GROUP // LANES
    first, second = group * each, PLACE_ROWS // 2 + group * each
    return cols[first : first + each], cols[second : second + each]


def tail_body(table_ref, arrived_ref, tail_ref, held, staged, chosen, load, store):
    parts, _, wide = held.shape
    columns = [pl.ds(i * wide, wide) for i in range(parts)]
    arriving = started(
        [arrived_ref.at[:, each] for each in columns], [held.at[i] for i in range(parts)], load
    )
    first, second = place_cols(table_ref, 1)
    chosen[...] = match_cols(first + second, table_row(table_ref, ARRIVAL, SLOT_ROWS))
    leaving = []
    for part in range(parts):
        arriving[part].wait()
        staged[part] = dot(chosen[...], held[part]).astype(jnp.bfloat16)
        leaving += started([staged.at[part]], [tail_ref.at[:, columns[part]]], store, part)
    for copy in leaving:
        copy.wait()


def sort_tail(table, arrived, width):
    slots = arrived.shape[0]
    wide = width // 4
    return pl.pallas_call(
        tail_body,
        in_specs=[table_spec()] + anywhere(1),
        out_specs=anywhere(1)[0],
        out_shape=jax.ShapeDtypeStruct((2 * GROUP, width), jnp.bfloat16),
        scratch_shapes=[
            pltpu.VMEM((4, slots, wide), jnp.bfloat16),
            pltpu.VMEM((4, 2 * GROUP, wide), jnp.bfloat16),
            pltpu.VMEM((2 * GROUP, slots), jnp.bfloat16),
            pltpu.SemaphoreType.DMA((4,)),
            pltpu.SemaphoreType.DMA((4,)),
        ],
        compiler_params=params(),
        cost_estimate=cost(4 * slots * GROUP * width, 2 * (slots + 2 * GROUP) * width),
        name="sort_tail",
    )(table, arrived)


def forward_tile(query, keys, values):
    scores = dot(query, keys, 1, 1)
    own = iota((GROUP, 2 * GROUP), 1) == iota((GROUP, 2 * GROUP), 0) + GROUP
    scores = jnp.where(own, NEG_SELF, scores)
    top = jnp.max(scores, -1, keepdims=True)
    raised = jnp.exp(scores - top)
    total = jnp.sum(raised, -1, keepdims=True)
    weights = (raised * (1.0 / total)).astype(jnp.bfloat16)
    return dot(weights, values), top + jnp.log(total)


def forward_pair(pair, query, raw, values, cotangent, out_ref):
    lane = iota((GROUP, LANES), 1) % STAT
    stat = jnp.zeros((GROUP, LANES), jnp.float32)
    for local in range(2):
        columns = slice(local * DH, (local + 1) * DH)
        keys = unit_rows(raw[:, columns])[0].astype(jnp.bfloat16)
        partial, lse = forward_tile(query[:, columns], keys, values[:, columns])
        out_ref[:, columns] = partial
        delta = jnp.sum(partial * cotangent[:, columns].astype(jnp.float32), -1, keepdims=True)
        head = pair * 2 + local
        stat = jnp.where(lane == head, lse, jnp.where(lane == head + 4, delta, stat))
    return stat


def own_body(
    table_ref,
    arrived_query_ref,
    arrived_value_ref,
    arrived_cotangent_ref,
    tail_query_ref,
    tail_value_ref,
    head_query_ref,
    head_value_ref,
    head_cotangent_ref,
    tail_cotangent_ref,
    out_ref,
    stat_ref,
    chosen,
):
    pair = pl.program_id(0)
    hash_round = pl.program_id(1)

    @pl.when((pair == 0) & (hash_round == 0))
    def _():
        row = table_row(table_ref, ARRIVAL, SLOT_ROWS)
        heads, tails = place_cols(table_ref, 0), place_cols(table_ref, 1)
        for each in range(2):
            chosen[each] = match_cols(heads[each] + tails[each], row)

    select_head = chosen[hash_round, :GROUP]
    query = dot(select_head, arrived_query_ref[...]).astype(jnp.bfloat16)
    value = dot(select_head, arrived_value_ref[...]).astype(jnp.bfloat16)
    cotangent = dot(chosen[hash_round], arrived_cotangent_ref[...]).astype(jnp.bfloat16)
    head_query_ref[...] = query
    head_value_ref[...] = value
    head_cotangent_ref[...] = cotangent[:GROUP]
    tail_cotangent_ref[...] = cotangent[GROUP:]
    stat_ref[...] = forward_pair(
        pair,
        tail_query_ref[...],
        jnp.concatenate([query, tail_query_ref[...]]),
        jnp.concatenate([value, tail_value_ref[...]]),
        cotangent[GROUP:],
        out_ref,
    )


def group_spec(offset=0):
    return pl.BlockSpec((GROUP, 2 * DH), lambda p, r: (r, p + offset))


def stat_spec():
    return pl.BlockSpec((GROUP, LANES), lambda p, r: (r, p))


def forward_own(table, arrived, tail):
    slots, width = arrived.shape
    wide = width // 6
    rows = 2 * GROUP
    array = jax.ShapeDtypeStruct((rows, width // 3), jnp.bfloat16)
    return pl.pallas_call(
        own_body,
        grid=(2, 2),
        in_specs=[pl.BlockSpec((LANES, LANES), lambda p, r: (0, 0))]
        + [pl.BlockSpec((slots, wide), lambda p, r, k=k: (0, p + 2 * k)) for k in range(3)]
        + [group_spec(), group_spec(2)],
        out_specs=[group_spec()] * 5 + [stat_spec()],
        out_shape=[array] * 4
        + [
            jax.ShapeDtypeStruct((rows, width // 3), jnp.float32),
            jax.ShapeDtypeStruct((rows, 2 * LANES), jnp.float32),
        ],
        scratch_shapes=[pltpu.VMEM((2, 2 * GROUP, slots), jnp.bfloat16)],
        compiler_params=params(),
        cost_estimate=cost(5e9, 1e7, 8 * GROUP * 512),
        name="forward_own",
    )(table, arrived, arrived, arrived, tail, tail)


def edge_body(
    table_ref,
    query_ref,
    value_ref,
    cotangent_ref,
    prior_query_ref,
    prior_value_ref,
    second_stat_ref,
    out_ref,
    stat_ref,
    stats_ref,
    both,
):
    pair = pl.program_id(0)
    hash_round = pl.program_id(1)
    stat = forward_pair(
        pair,
        query_ref[...],
        jnp.concatenate([prior_query_ref[...], query_ref[...]]),
        jnp.concatenate([prior_value_ref[...], value_ref[...]]),
        cotangent_ref[...],
        out_ref,
    )
    stat_ref[...] = stat

    @pl.when(pair == 0)
    def _():
        both[hash_round, :GROUP] = stat
        both[hash_round, GROUP:] = second_stat_ref[...]

    @pl.when(pair == 1)
    def _():
        both[hash_round, :GROUP] += stat
        both[hash_round, GROUP:] += second_stat_ref[...]

    @pl.when((pair == 1) & (hash_round == 1))
    def _():
        rows = 4 * GROUP
        piece = iota((rows, LANES), 1) // (PIECES * STAT)
        first, second, third = pieces_of(both[...].reshape(rows, LANES))
        nothing = jnp.zeros((rows, LANES), jnp.bfloat16)
        stats = jnp.where(
            piece == 0,
            first,
            jnp.where(piece == 1, second, jnp.where(piece == 2, third, nothing)),
        )
        place_row = table_row(table_ref, PLACE, PLACE_ROWS)
        third_slots = stats_ref.shape[0]
        arrival_cols = table_cols(table_ref, ARRIVAL3, SLOT_ROWS)
        lane_third = (iota((third_slots, LANES), 1) % (3 * STAT)) // STAT
        result = jnp.zeros((third_slots, LANES), jnp.float32)
        for third in range(3):
            back = match_cols(arrival_cols[4 * third : 4 * third + 4], place_row)
            result = jnp.where(lane_third == third, dot(back, stats), result)
        stats_ref[...] = result


def forward_edge(table, query, value, cotangent, prior_tail, second_stat):
    rows, width = query.shape
    third_slots = SLOT_ROWS * LANES // 3
    return pl.pallas_call(
        edge_body,
        grid=(2, 2),
        in_specs=[pl.BlockSpec((LANES, LANES), lambda p, r: (0, 0))]
        + [group_spec()] * 4
        + [group_spec(2), stat_spec()],
        out_specs=[
            group_spec(),
            stat_spec(),
            pl.BlockSpec((third_slots, LANES), lambda p, r: (0, 0)),
        ],
        out_shape=[
            jax.ShapeDtypeStruct((rows, width), jnp.float32),
            jax.ShapeDtypeStruct((rows, 2 * LANES), jnp.float32),
            jax.ShapeDtypeStruct((third_slots, LANES), jnp.float32),
        ],
        scratch_shapes=[pltpu.VMEM((2, 2 * GROUP, LANES), jnp.float32)],
        compiler_params=params(),
        cost_estimate=cost(2e9, 4e6, 8 * GROUP * 512),
        name="forward_edge",
    )(table, query, value, cotangent, prior_tail, prior_tail, second_stat)


def gather_stats(codes_row, slot_cols, stats):
    narrow = stats.astype(jnp.bfloat16)
    total = None
    for third in range(3):
        chosen = match_cols(slot_cols[4 * third : 4 * third + 4], codes_row)
        found = dot(narrow, chosen, 0, 0)
        for piece in range(PIECES):
            at = piece * PIECES * STAT + third * STAT
            part = found[at : at + STAT]
            total = part if total is None else total + part
    return total


def found_at_tokens(tokens, table_ref, stats):
    slot_cols = table_cols(table_ref, SEND3, SLOT_ROWS)
    found = gather_stats(iota((1, 2 * tokens), 1), slot_cols, stats)
    lse_first, lse_second = found[:4, :tokens], found[:4, tokens:]
    top = jnp.maximum(lse_first, lse_second)
    total = top + jnp.log(jnp.exp(lse_first - top) + jnp.exp(lse_second - top))
    shares = jnp.exp(lse_first - total), jnp.exp(lse_second - total)
    delta = found[4:, :tokens] * shares[0] + found[4:, tokens:] * shares[1]
    return slot_cols, total, delta, shares


def total_body(tokens, table_ref, arrived_ref, out_ref):
    slot_cols, total, delta, _ = found_at_tokens(tokens, table_ref, arrived_ref[...])
    stat = jnp.concatenate([total, delta])
    first, second, third_piece = [member.astype(jnp.float32) for member in pieces_of(stat)]
    spare = jnp.zeros((LANES - 9 * STAT, tokens), jnp.float32)
    table = jnp.concatenate(
        [first] * 3 + [second] * 3 + [third_piece] * 3 + [spare]
    ).astype(jnp.bfloat16)
    third_slots = arrived_ref.shape[0]
    lane_third = (iota((third_slots, LANES), 1) % (3 * STAT)) // STAT
    result = jnp.zeros((third_slots, LANES), jnp.float32)
    for third in range(3):
        codes = slot_cols[4 * third : 4 * third + 4]
        cols = [jnp.where(code >= tokens, code - tokens, code) for code in codes]
        chosen = match_cols(cols, iota((LANES, tokens), 1))
        result = jnp.where(lane_third == third, dot(chosen, table, 1, 1), result)
    owners = third_slots // STAT
    by_owner = result.reshape(owners, STAT, LANES)
    out_ref[:, :STAT, :] = by_owner
    above = jnp.concatenate([by_owner[1:], by_owner[:1]])
    below = jnp.concatenate([by_owner[owners - 1 :], by_owner[: owners - 1]])
    half = table_ref[HALF : HALF + 1, :]
    out_ref[:, STAT:, :] = jnp.where(half[None] == 0, above, below)


def total_stats(table, arrived, tokens):
    owners = arrived.shape[0] // STAT
    return pl.pallas_call(
        functools.partial(total_body, tokens),
        out_shape=jax.ShapeDtypeStruct((owners, 2 * STAT, LANES), jnp.float32),
        compiler_params=params(),
        cost_estimate=cost(2 * 1536 * 1536 * LANES, 1 << 20),
        name="total_stats",
    )(table, arrived)


def prepare_body(tokens, table_ref, arrived_ref, first_ref, second_ref, payload_ref, share_ref):
    @pl.when(pl.program_id(0) == 0)
    def _():
        shares = found_at_tokens(tokens, table_ref, arrived_ref[...])[3]
        spare = jnp.zeros((LANES - STAT, tokens), jnp.float32)
        share_ref[...] = jnp.concatenate([*shares, spare]).T

    back = match_cols(
        table_cols(table_ref, ARRIVAL, SLOT_ROWS), table_row(table_ref, PLACE, PLACE_ROWS)
    )
    rows = [first_ref[:GROUP], second_ref[:GROUP], first_ref[GROUP:], second_ref[GROUP:]]
    payload_ref[...] = dot(back, jnp.concatenate(rows).astype(jnp.bfloat16)).astype(jnp.bfloat16)


def prepare(table, home_stats, outs, tokens):
    slots = SLOT_ROWS * LANES
    rows, width = outs[0].shape
    wide = width // 2
    return pl.pallas_call(
        functools.partial(prepare_body, tokens),
        grid=(2,),
        in_specs=[
            table_spec(),
            pl.BlockSpec(home_stats.shape, lambda i: (0, 0)),
            pl.BlockSpec((rows, wide), lambda i: (0, i)),
            pl.BlockSpec((rows, wide), lambda i: (0, i)),
        ],
        out_specs=[
            pl.BlockSpec((slots, wide), lambda i: (0, i)),
            pl.BlockSpec((tokens, LANES), lambda i: (0, 0)),
        ],
        out_shape=[
            jax.ShapeDtypeStruct((slots, 3 * width), jnp.bfloat16),
            jax.ShapeDtypeStruct((tokens, LANES), jnp.float32),
        ],
        compiler_params=params(62),
        cost_estimate=cost(2e9, 1e7),
        name="prepare_outputs",
    )(table, home_stats, *outs)


def backward_tile(query, upstream, keys, values, masked, total_row, delta_row):
    scores = dot(keys, query, 1, 1)
    if masked is not None:
        low, high = scores[GROUP : GROUP + LANES], scores[GROUP + LANES :]
        low = jnp.concatenate(
            [jnp.where(masked, NEG_SELF, low[:, :LANES]), low[:, LANES:]], axis=1
        )
        high = jnp.concatenate(
            [high[:, :LANES], jnp.where(masked, NEG_SELF, high[:, LANES:])], axis=1
        )
        scores = jnp.concatenate([scores[:GROUP], low, high])
    probs = jnp.exp(scores - total_row)
    dots = dot(values, upstream, 1, 1)
    slopes = (probs * (dots - delta_row)).astype(jnp.bfloat16)
    return probs.astype(jnp.bfloat16), slopes


def backward_heads(pair, stat, edge_stat, refs, hash_round, shaped):
    heads, tail, tail_cotangent, prior, nexts = refs
    kept = pl.ds(hash_round * GROUP, GROUP)
    own = iota((LANES, LANES), 0) == iota((LANES, LANES), 1)
    width = tail.shape[1] // 2
    for local in range(2):
        head = pair * 2 + local
        columns = pl.ds(head * DH, DH)
        values_at = pl.ds(width + head * DH, DH)
        total_row, delta_row = stat[head : head + 1], stat[head + 4 : head + 5]
        edge_total, edge_delta = edge_stat[head : head + 1], edge_stat[head + 4 : head + 5]
        raw = jnp.concatenate([heads[0][kept, columns], tail[kept, columns]])
        values = jnp.concatenate([heads[1][kept, columns], tail[kept, values_at]])
        upstream = jnp.concatenate([heads[2][kept, columns], tail_cotangent[kept, columns]])
        units, inverse = unit_rows(raw)
        keys = units.astype(jnp.bfloat16)
        prior_keys = unit_rows(prior[kept, columns])[0].astype(jnp.bfloat16)
        keys_first = jnp.concatenate([prior_keys, keys[:GROUP]])
        values_first = jnp.concatenate([prior[kept, values_at], values[:GROUP]])
        probs, slopes = backward_tile(
            raw[:GROUP],
            upstream[:GROUP],
            keys_first,
            values_first,
            own,
            total_row[:, :GROUP],
            delta_row[:, :GROUP],
        )
        query_first = dot(keys_first, slopes, 0, 0).T
        unit_first = dot(slopes[GROUP:], raw[:GROUP])
        value_first = dot(probs[GROUP:], upstream[:GROUP])

        probs, slopes = backward_tile(
            raw[GROUP:],
            upstream[GROUP:],
            keys,
            values,
            own,
            total_row[:, GROUP:],
            delta_row[:, GROUP:],
        )
        query_second = dot(keys, slopes, 0, 0).T
        unit_both = dot(slopes, raw[GROUP:])
        value_both = dot(probs, upstream[GROUP:])

        next_query = nexts[0][kept, columns]
        next_upstream = nexts[1][kept, columns]
        probs, slopes = backward_tile(
            next_query,
            next_upstream,
            keys[GROUP:],
            values[GROUP:],
            None,
            edge_total,
            edge_delta,
        )
        unit_last = dot(slopes, next_query)
        value_last = dot(probs, next_upstream)

        query_slope = jnp.concatenate([query_first, query_second])
        unit_slope = unit_both + jnp.concatenate([unit_first, unit_last])
        value_slope = value_both + jnp.concatenate([value_first, value_last])
        key_slope = inverse * (
            unit_slope - units * jnp.sum(units * unit_slope, -1, keepdims=True)
        )
        shaped[hash_round, :, local * DH : (local + 1) * DH] = (query_slope + key_slope).astype(
            jnp.bfloat16
        )
        shaped[hash_round, :, (2 + local) * DH : (3 + local) * DH] = value_slope.astype(
            jnp.bfloat16
        )


def backward_body(
    table_ref,
    stats_ref,
    head_query_ref,
    head_value_ref,
    head_cotangent_ref,
    tail_ref,
    tail_cotangent_ref,
    prior_ref,
    next_query_ref,
    next_cotangent_ref,
    _,
    payload_ref,
    stats,
    six,
    double,
    shaped,
    staged,
    load,
    store,
):
    rows = PLACE_ROWS * LANES
    per_round = rows // 2
    sources = [
        stats_ref,
        head_query_ref,
        head_value_ref,
        head_cotangent_ref,
        tail_cotangent_ref,
        next_query_ref,
        next_cotangent_ref,
        tail_ref,
        prior_ref,
    ]
    targets = [stats] + [six.at[i] for i in range(6)] + [double.at[i] for i in range(2)]
    arriving = started(sources, targets, load)
    place_row = table_row(table_ref, PLACE, PLACE_ROWS)
    next_row = table_row(table_ref, NEXT_PLACE, NEXT_ROWS)
    back = [
        match_cols(
            table_cols(table_ref, (FIRST16, LAST16)[each], PART_ROWS),
            place_row[:, each * per_round : (each + 1) * per_round],
        )
        for each in range(2)
    ]
    arriving[0].wait()
    own_stats = stats[:, :STAT, :].reshape(-1, LANES)
    next_stats = stats[:, STAT:, :].reshape(-1, LANES)
    found = gather_stats(place_row, table_cols(table_ref, ARRIVAL3, SLOT_ROWS), own_stats)
    edge = gather_stats(next_row, table_cols(table_ref, NEXT3, SLOT_ROWS), next_stats)
    for copy in arriving[1:]:
        copy.wait()
    refs = (
        (six.at[0], six.at[1], six.at[2]),
        double.at[0],
        six.at[3],
        double.at[1],
        (six.at[4], six.at[5]),
    )
    leaving = []
    width = shaped.shape[2]
    for pair in range(2):
        for hash_round in range(2):
            backward_heads(
                pair,
                found[:, hash_round * per_round : (hash_round + 1) * per_round],
                edge[:, hash_round * GROUP : (hash_round + 1) * GROUP],
                refs,
                hash_round,
                shaped,
            )
        chunks = 2
        for chunk in range(chunks):
            kept = slice(chunk * 1024 // chunks, (chunk + 1) * 1024 // chunks)
            first = dot(back[0][kept], shaped[0]).reshape(-1, 2, STAT, width)
            second = dot(back[1][kept], shaped[1]).reshape(-1, 2, STAT, width)
            whole = jnp.concatenate(
                [first[:, :1], first[:, 1:] + second[:, :1], second[:, 1:]], axis=1
            ).reshape(-1, width)
            count = whole.shape[0]
            at = pl.ds(chunk * count, count)
            staged[pair, at] = whole.astype(jnp.bfloat16)
            leaving += started(
                [staged.at[pair, at]],
                [payload_ref.at[at, pl.ds((pair + 1) * width, width)]],
                store,
                pair * chunks + chunk,
            )
    for copy in leaving:
        copy.wait()


def backward(table, stats, heads, tail, tail_cotangent, prior_tail, nexts, payload):
    slots = SLOT_ROWS * LANES
    rows, width = heads[0].shape
    return pl.pallas_call(
        backward_body,
        in_specs=[table_spec()] + anywhere(10),
        out_specs=anywhere(1)[0],
        out_shape=jax.ShapeDtypeStruct((slots, 3 * width), jnp.bfloat16),
        input_output_aliases={10: 0},
        scratch_shapes=[
            pltpu.VMEM(stats.shape, jnp.float32),
            pltpu.VMEM((6, rows, width), jnp.bfloat16),
            pltpu.VMEM((2, rows, 2 * width), jnp.bfloat16),
            pltpu.VMEM((2, 2 * GROUP, width), jnp.bfloat16),
            pltpu.VMEM((2, slots, width), jnp.bfloat16),
            pltpu.SemaphoreType.DMA((9,)),
            pltpu.SemaphoreType.DMA((4,)),
        ],
        compiler_params=params(62),
        cost_estimate=cost(8e9, 1.5e7, 3e6),
        name="backward",
    )(table, stats, *heads, tail, tail_cotangent, prior_tail, *nexts, payload)


def combine_body(
    table_ref,
    share_ref,
    arrived_ref,
    out_ref,
    first_ref,
    second_ref,
    staged,
    chosen,
    store,
):
    parts, tokens, wide = staged.shape
    token = iota((tokens, 1), 0)
    code = table_row(table_ref, SEND_CODE, SLOT_ROWS)
    chosen[0] = match(token, code)
    chosen[1] = match(token + tokens, code)
    chosen[2] = match(token, table_row(table_ref, SEND, SLOT_ROWS))
    leaving = []
    for part in range(parts):
        arrived = arrived_ref[:, part * wide : (part + 1) * wide]
        if part < 2:
            found = 0.0
            for each in range(2):
                at = 4 * each + 2 * part
                share = jnp.concatenate(
                    [
                        jnp.broadcast_to(share_ref[:, at + i : at + i + 1], (tokens, DH))
                        for i in range(2)
                    ],
                    axis=1,
                )
                found = found + share * dot(chosen[each], arrived)
            target = out_ref.at[:, pl.ds(part * wide, wide)]
        else:
            found = dot(chosen[2], arrived)
            target = (first_ref, second_ref)[part % 2].at[:, pl.ds((part // 2 - 1) * wide, wide)]
        staged[part] = found.astype(jnp.bfloat16)
        leaving += started([staged.at[part]], [target], store, part)
    for copy in leaving:
        copy.wait()


def combine(table, shares, arrived, tokens):
    slots, width = arrived.shape
    wide = width // 6
    return pl.pallas_call(
        combine_body,
        in_specs=[table_spec(), pl.BlockSpec(shares.shape, lambda *_: (0, 0))]
        + [pl.BlockSpec(memory_space=pltpu.VMEM)],
        out_specs=anywhere(3),
        out_shape=[jax.ShapeDtypeStruct((tokens, 2 * wide), jnp.bfloat16)] * 3,
        scratch_shapes=[
            pltpu.VMEM((6, tokens, wide), jnp.bfloat16),
            pltpu.VMEM((3, tokens, slots), jnp.bfloat16),
            pltpu.SemaphoreType.DMA((6,)),
        ],
        compiler_params=params(40),
        cost_estimate=cost(2 * slots * tokens * width, 2 * (slots + tokens) * width),
        name="combine_rows",
    )(table, shares, arrived)


def per_device(query_key, value, attended_cotangent, send_rows, arrival_count, receive_slot):
    tokens, row_width = query_key.shape
    rounds = send_rows.shape[0]
    owners = lax.axis_size("seq")
    capacity = send_rows.shape[1] // owners
    per_owner = rounds * capacity
    slots = owners * per_owner

    code = (tokens * jnp.arange(rounds, dtype=jnp.int32))[:, None]
    half = lax.axis_index("head")

    def by_owner(table):
        return table.reshape(rounds, owners, capacity).transpose(1, 0, 2).reshape(owners, per_owner)

    def by_third(codes):
        return codes.reshape(owners, 3, STAT).transpose(1, 0, 2)

    def sent(packed):
        return exchange(packed.reshape(owners, per_owner, -1)).reshape(slots, -1)

    blocks = send_rows.reshape(rounds, owners, capacity)
    send_rows = jnp.where(half == 0, blocks, blocks[:, ::-1]).reshape(rounds, -1)
    send = by_owner(send_rows)
    send_blocks = jnp.pad(send.reshape(-1, LANES), ((0, 4), (0, 0)))
    packed = pack(send_blocks, query_key, value, attended_cotangent)

    within = jnp.arange(capacity, dtype=jnp.int32)

    def arrivals(counts):
        start = jnp.cumsum(counts, axis=1) - counts + code
        codes = jnp.where(within < counts[:, :, None], start[:, :, None] + within, -1)
        return by_owner(codes)

    tables = jnp.concatenate([arrival_count, receive_slot], axis=1)
    packed, mine, following = lax.optimization_barrier(
        (packed, to_place(tables), to_place_prior(tables[:, : owners + GROUP]))
    )
    arrival = arrivals(mine[:, :owners])
    next_arrival = arrivals(following[:, :owners])
    place = mine[:, owners:] + code
    next_place = following[:, owners:] + code

    def half_blocks(codes, first):
        return codes[:, first : first + 2 * STAT]

    members = [
        (ARRIVAL, arrival),
        (ARRIVAL3, by_third(arrival)),
        (NEXT3, by_third(next_arrival)),
        (PLACE, place),
        (NEXT_PLACE, next_place),
        (SEND, send),
        (SEND3, by_third(by_owner(send_rows + code))),
        (HALF, jnp.full((1, LANES), half, jnp.int32)),
        (FIRST16, half_blocks(arrival, 0)),
        (LAST16, half_blocks(arrival, STAT)),
        (SEND_CODE, by_owner(send_rows + code)),
    ]
    rows = [codes.reshape(-1, LANES) for _, codes in members]
    assert [at for at, _ in members] == [sum(map(len, rows[:i])) for i in range(len(rows))]
    table = jnp.concatenate(rows)
    table = jnp.pad(table, ((0, LANES - len(table)), (0, 0)), constant_values=-1)

    arrived, table = lax.optimization_barrier((sent(packed), table))
    tail = sort_tail(table, arrived, 2 * row_width)
    prior_tail = to_next(tail)
    head_query, head_value, head_cotangent, tail_cotangent, out_second, stat_second = forward_own(
        table, arrived, tail
    )
    out_first, stat_first, stats = forward_edge(
        table, head_query, head_value, head_cotangent, prior_tail, stat_second
    )
    next_query = to_prior(head_query)
    next_cotangent = to_prior(head_cotangent)
    home_stats = exchange(stats.reshape(owners, STAT, LANES)).reshape(-1, LANES)
    totals = exchange(total_stats(table, home_stats, tokens))
    payload, shares = prepare(table, home_stats, (out_first, out_second), tokens)
    payload = backward(
        table,
        totals,
        (head_query, head_value, head_cotangent),
        tail,
        tail_cotangent,
        prior_tail,
        (next_query, next_cotangent),
        payload,
    )
    return tuple(combine(table, shares, sent(payload), tokens))


def solution(mesh):
    in_specs = (
        P("seq", "head"),
        P("seq", "head"),
        P("seq", "head"),
        P(None, "seq"),
        P(None, "seq"),
        P(None, "seq"),
    )
    out_specs = (P("seq", "head"), P("seq", "head"), P("seq", "head"))
    return jax.shard_map(
        per_device, mesh=mesh, in_specs=in_specs, out_specs=out_specs, check_vma=False
    )
```

```python
import functools

import jax
import jax.numpy as jnp
from jax import lax
from jax.experimental import pallas as pl
from jax.experimental.pallas import tpu as pltpu
from jax.sharding import PartitionSpec as P

DH = 128
GROUP = 256
NEG_SELF = -100000.0
EPS_KEY = 1e-06
LANES = 128
STAT = 8
PIECES = 3
MIB = 1 << 20


def dot(left, right, left_axis=1, right_axis=0):
    return lax.dot_general(
        left,
        right,
        (((left_axis,), (right_axis,)), ((), ())),
        preferred_element_type=jnp.float32,
    )


def params(mib=62):
    return pltpu.CompilerParams(vmem_limit_bytes=mib * MIB)


def cost(flops, moved, exps=0):
    return pl.CostEstimate(flops=int(flops), bytes_accessed=int(moved), transcendentals=int(exps))


def routed(block, route_of):
    owners, halves = lax.axis_size("seq"), lax.axis_size("head")
    route = [
        (i * halves + half, route_of(i, half, owners) * halves + half)
        for i in range(owners)
        for half in range(halves)
    ]
    return lax.ppermute(block, ("seq", "head"), route)


def to_next(block):
    return routed(block, lambda i, half, n: (i + (1 if half == 0 else -1)) % n)


def to_prior(block):
    return routed(block, lambda i, half, n: (i - (1 if half == 0 else -1)) % n)


def to_place_prior(block):
    return routed(block, lambda i, half, n: (i - 1) % n if half == 0 else n - 1 - (i - 1) % n)


def to_place(block):
    return routed(block, lambda i, half, n: i if half == 0 else n - 1 - i)


def exchange(block):
    return lax.all_to_all(block, "seq", split_axis=0, concat_axis=0, tiled=True)


def match(left, right):
    return jnp.where(left == right, 1.0, 0.0).astype(jnp.bfloat16)


ARRIVAL3, PLACE, ARRIVAL, SEND, SEND3, HALF, FIRST16, LAST16, SEND_CODE = 0, 12, 20, 32, 44, 56, 57, 65, 73
SLOT_ROWS, PLACE_ROWS, PART_ROWS = 12, 8, 8
SHARED_ROWS = 24


def table_row(table_ref, start, count):
    return jnp.concatenate([table_ref[start + i : start + i + 1, :] for i in range(count)], axis=1)


def table_cols(table_ref, start, count):
    turned = table_ref[...].T
    return [turned[:, start + i : start + i + 1] for i in range(count)]


def match_cols(cols, row):
    return jnp.concatenate([match(col, row) for col in cols])


def anywhere(count):
    return [pl.BlockSpec(memory_space=pl.ANY) for _ in range(count)]


def table_spec():
    return pl.BlockSpec((LANES, LANES), lambda *_: (0, 0))


def started(sources, targets, sems, first=0):
    copies = [
        pltpu.make_async_copy(source, target, sems.at[first + i])
        for i, (source, target) in enumerate(zip(sources, targets))
    ]
    for copy in copies:
        copy.start()
    return copies


def iota(shape, axis):
    return lax.broadcasted_iota(jnp.int32, shape, axis)


def pieces_of(wide):
    first = wide.astype(jnp.bfloat16)
    rest = wide - first.astype(jnp.float32)
    second = rest.astype(jnp.bfloat16)
    third = (rest - second.astype(jnp.float32)).astype(jnp.bfloat16)
    return first, second, third


def unit_rows(raw_rows):
    wide = raw_rows.astype(jnp.float32)
    inverse = lax.rsqrt(jnp.sum(wide * wide, -1, keepdims=True) + EPS_KEY)
    return wide * inverse, inverse


def pack_body(index_ref, *refs):
    sources, out_ref, held, staged, chosen, load, store = refs[:3], *refs[3:]
    tokens, width = sources[0].shape
    arriving = started(sources, [held.at[i] for i in range(3)], load)
    turned = index_ref[...].T
    chosen[...] = match_cols(
        [turned[:, i : i + 1] for i in range(SLOT_ROWS)], iota((LANES, tokens), 1)
    )
    steps = 4
    block = chosen.shape[0] // steps
    leaving = []
    for step in range(steps):
        rows = slice(step * block, (step + 1) * block)
        for place in range(3):
            if step == 0:
                arriving[place].wait()
            staged[rows, place * width : (place + 1) * width] = dot(
                chosen[rows], held[place]
            ).astype(jnp.bfloat16)
        leaving += started(
            [staged.at[pl.ds(step * block, block)]],
            [out_ref.at[pl.ds(step * block, block)]],
            store,
            step,
        )
    for copy in leaving:
        copy.wait()


def pack(index, *sources):
    slots = SLOT_ROWS * LANES
    tokens, width = sources[0].shape
    total = width * len(sources)
    return pl.pallas_call(
        pack_body,
        in_specs=[pl.BlockSpec(index.shape, lambda *_: (0, 0))] + anywhere(3),
        out_specs=anywhere(1)[0],
        out_shape=jax.ShapeDtypeStruct((slots, total), jnp.bfloat16),
        scratch_shapes=[
            pltpu.VMEM((3, tokens, width), jnp.bfloat16),
            pltpu.VMEM((slots, total), jnp.bfloat16),
            pltpu.VMEM((slots, tokens), jnp.bfloat16),
            pltpu.SemaphoreType.DMA((3,)),
            pltpu.SemaphoreType.DMA((4,)),
        ],
        compiler_params=params(),
        cost_estimate=cost(2 * slots * tokens * total, 2 * (slots + tokens) * total),
        name="pack_rows",
    )(index, *sources)


def place_cols(table_ref, group):
    cols = table_cols(table_ref, PLACE, PLACE_ROWS)
    each = GROUP // LANES
    first, second = group * each, PLACE_ROWS // 2 + group * each
    return cols[first : first + each], cols[second : second + each]


def tail_body(table_ref, arrived_ref, tail_ref, held, staged, chosen, load, store):
    width = held.shape[1]
    arriving = started([arrived_ref.at[:, pl.ds(0, width)]], [held], load)
    first, second = place_cols(table_ref, 1)
    row = table_row(table_ref, ARRIVAL, SLOT_ROWS)
    for i, col in enumerate(first + second):
        chosen[i * LANES : (i + 1) * LANES] = match(col, row)
    arriving[0].wait()
    leaving = []
    for i in range(2):
        staged[i * GROUP : (i + 1) * GROUP] = dot(
            chosen[i * GROUP : (i + 1) * GROUP], held[...]
        ).astype(jnp.bfloat16)
        at = pl.ds(i * GROUP, GROUP)
        leaving += started([staged.at[at]], [tail_ref.at[at]], store, i)
    for copy in leaving:
        copy.wait()


def sort_tail(table, arrived, width):
    slots = arrived.shape[0]
    wide = width // 4
    return pl.pallas_call(
        tail_body,
        in_specs=[table_spec()] + anywhere(1),
        out_specs=anywhere(1)[0],
        out_shape=jax.ShapeDtypeStruct((2 * GROUP, width), jnp.bfloat16),
        scratch_shapes=[
            pltpu.VMEM((slots, width), jnp.bfloat16),
            pltpu.VMEM((2 * GROUP, width), jnp.bfloat16),
            pltpu.VMEM((2 * GROUP, slots), jnp.bfloat16),
            pltpu.SemaphoreType.DMA((4,)),
            pltpu.SemaphoreType.DMA((4,)),
        ],
        compiler_params=params(),
        cost_estimate=cost(4 * slots * GROUP * width, 2 * (slots + 2 * GROUP) * width),
        name="sort_tail",
    )(table, arrived)


def forward_tile(query, keys, values):
    scores = dot(query, keys, 1, 1)
    own = iota((GROUP, 2 * GROUP), 1) == iota((GROUP, 2 * GROUP), 0) + GROUP
    scores = jnp.where(own, NEG_SELF, scores)
    top = jnp.max(scores, -1, keepdims=True)
    raised = jnp.exp(scores - top)
    total = jnp.sum(raised, -1, keepdims=True)
    weights = (raised * (1.0 / total)).astype(jnp.bfloat16)
    return dot(weights, values), top + jnp.log(total)


def forward_pair(pair, query, raw, values, cotangent, out_ref):
    lane = iota((GROUP, LANES), 1) % STAT
    stat = jnp.zeros((GROUP, LANES), jnp.float32)
    for local in range(2):
        columns = slice(local * DH, (local + 1) * DH)
        keys = unit_rows(raw[:, columns])[0].astype(jnp.bfloat16)
        partial, lse = forward_tile(query[:, columns], keys, values[:, columns])
        out_ref[:, columns] = partial.astype(jnp.bfloat16)
        delta = jnp.sum(partial * cotangent[:, columns].astype(jnp.float32), -1, keepdims=True)
        head = pair * 2 + local
        stat = jnp.where(lane == head, lse, jnp.where(lane == head + 4, delta, stat))
    return stat


def own_body(
    table_ref,
    arrived_query_ref,
    arrived_value_ref,
    arrived_cotangent_ref,
    tail_query_ref,
    tail_value_ref,
    head_query_ref,
    head_value_ref,
    head_cotangent_ref,
    tail_cotangent_ref,
    out_ref,
    stat_ref,
    chosen,
):
    pair = pl.program_id(0)
    hash_round = pl.program_id(1)

    @pl.when((pair == 0) & (hash_round == 0))
    def _():
        row = table_row(table_ref, ARRIVAL, SLOT_ROWS)
        heads, tails = place_cols(table_ref, 0), place_cols(table_ref, 1)
        for each in range(2):
            chosen[each] = match_cols(heads[each] + tails[each], row)

    select_head = chosen[hash_round, :GROUP]
    query = dot(select_head, arrived_query_ref[...]).astype(jnp.bfloat16)
    value = dot(select_head, arrived_value_ref[...]).astype(jnp.bfloat16)
    cotangent = dot(chosen[hash_round], arrived_cotangent_ref[...]).astype(jnp.bfloat16)
    head_query_ref[...] = query
    head_value_ref[...] = value
    head_cotangent_ref[...] = cotangent[:GROUP]
    tail_cotangent_ref[...] = cotangent[GROUP:]
    stat_ref[...] = forward_pair(
        pair,
        tail_query_ref[...],
        jnp.concatenate([query, tail_query_ref[...]]),
        jnp.concatenate([value, tail_value_ref[...]]),
        cotangent[GROUP:],
        out_ref,
    )


def group_spec(offset=0):
    return pl.BlockSpec((GROUP, 2 * DH), lambda p, r: (r, p + offset))


def stat_spec():
    return pl.BlockSpec((GROUP, LANES), lambda p, r: (r, p))


def forward_own(table, arrived, tail):
    slots, width = arrived.shape
    wide = width // 6
    rows = 2 * GROUP
    array = jax.ShapeDtypeStruct((rows, width // 3), jnp.bfloat16)
    return pl.pallas_call(
        own_body,
        grid=(2, 2),
        in_specs=[pl.BlockSpec((LANES, LANES), lambda p, r: (0, 0))]
        + [pl.BlockSpec((slots, wide), lambda p, r, k=k: (0, p + 2 * k)) for k in range(3)]
        + [group_spec(), group_spec(2)],
        out_specs=[group_spec()] * 5 + [stat_spec()],
        out_shape=[array] * 4
        + [
            jax.ShapeDtypeStruct((rows, width // 3), jnp.bfloat16),
            jax.ShapeDtypeStruct((rows, 2 * LANES), jnp.float32),
        ],
        scratch_shapes=[pltpu.VMEM((2, 2 * GROUP, slots), jnp.bfloat16)],
        compiler_params=params(),
        cost_estimate=cost(5e9, 1e7, 8 * GROUP * 512),
        name="forward_own",
    )(table, arrived, arrived, arrived, tail, tail)


def edge_body(
    table_ref,
    query_ref,
    value_ref,
    cotangent_ref,
    prior_ref,
    second_stat_ref,
    out_ref,
    stats_ref,
    three,
    prior,
    second_stat,
    staged,
    both,
    load,
    store,
):
    arriving = started(
        [query_ref, prior_ref, value_ref, cotangent_ref, second_stat_ref],
        [three.at[0], prior, three.at[1], three.at[2], second_stat],
        load,
    )
    place_row = table_row(table_ref, PLACE, PLACE_ROWS)
    arrival_cols = table_cols(table_ref, ARRIVAL3, SLOT_ROWS)
    for copy in arriving:
        copy.wait()
    width = staged.shape[1]
    leaving = []
    for hash_round in range(2):
        kept = slice(hash_round * GROUP, (hash_round + 1) * GROUP)
        at = pl.ds(hash_round * GROUP, GROUP)
        stat = 0.0
        second = 0.0
        for pair in range(2):
            columns = slice(pair * 2 * DH, (pair + 1) * 2 * DH)
            values_at = slice(width + pair * 2 * DH, width + (pair + 1) * 2 * DH)
            query = three[0, kept, columns]
            stat = stat + forward_pair(
                pair,
                query,
                jnp.concatenate([prior[kept, columns], query]),
                jnp.concatenate([prior[kept, values_at], three[1, kept, columns]]),
                three[2, kept, columns],
                staged.at[at, pl.ds(pair * 2 * DH, 2 * DH)],
            )
            second = second + second_stat[kept, pair * LANES : (pair + 1) * LANES]
        leaving += started([staged.at[at]], [out_ref.at[at]], store, hash_round)
        both[2 * hash_round * GROUP : (2 * hash_round + 1) * GROUP] = stat
        both[(2 * hash_round + 1) * GROUP : (2 * hash_round + 2) * GROUP] = second
    rows = 4 * GROUP
    piece = iota((rows, LANES), 1) // (PIECES * STAT)
    first, second, third = pieces_of(both[...])
    nothing = jnp.zeros((rows, LANES), jnp.bfloat16)
    stats = jnp.where(
        piece == 0,
        first,
        jnp.where(piece == 1, second, jnp.where(piece == 2, third, nothing)),
    )
    third_slots = stats_ref.shape[0]
    lane_third = (iota((third_slots, LANES), 1) % (3 * STAT)) // STAT
    result = jnp.zeros((third_slots, LANES), jnp.float32)
    for third in range(3):
        span = slice((0, 0, rows // 2)[third], (rows // 2, rows, rows)[third])
        back = match_cols(arrival_cols[4 * third : 4 * third + 4], place_row[:, span])
        result = jnp.where(lane_third == third, dot(back, stats[span]), result)
    stats_ref[...] = result
    for copy in leaving:
        copy.wait()


def forward_edge(table, query, value, cotangent, prior_tail, second_stat):
    rows, width = query.shape
    third_slots = SLOT_ROWS * LANES // 3
    return pl.pallas_call(
        edge_body,
        in_specs=[table_spec()] + anywhere(5),
        out_specs=anywhere(1) + [pl.BlockSpec(memory_space=pltpu.VMEM)],
        out_shape=[
            jax.ShapeDtypeStruct((rows, width), jnp.bfloat16),
            jax.ShapeDtypeStruct((third_slots, LANES), jnp.float32),
        ],
        scratch_shapes=[
            pltpu.VMEM((3, rows, width), jnp.bfloat16),
            pltpu.VMEM((rows, 2 * width), jnp.bfloat16),
            pltpu.VMEM((rows, 2 * LANES), jnp.float32),
            pltpu.VMEM((rows, width), jnp.bfloat16),
            pltpu.VMEM((2 * rows, LANES), jnp.float32),
            pltpu.SemaphoreType.DMA((5,)),
            pltpu.SemaphoreType.DMA((2,)),
        ],
        compiler_params=params(62),
        cost_estimate=cost(2e9, 4e6, 8 * GROUP * 512),
        name="forward_edge",
    )(table, query, value, cotangent, prior_tail, second_stat)


def gather_stats(codes_row, slot_cols, stats):
    narrow = stats.astype(jnp.bfloat16)
    half = codes_row.shape[1] // 2
    sums = [0.0, 0.0]
    for third in range(3):
        for each in ((0,), (0, 1), (1,))[third]:
            codes = codes_row[:, each * half : (each + 1) * half]
            chosen = match_cols(slot_cols[4 * third : 4 * third + 4], codes)
            found = dot(narrow, chosen, 0, 0)
            for piece in range(PIECES):
                at = piece * PIECES * STAT + third * STAT
                sums[each] = sums[each] + found[at : at + STAT]
    return jnp.concatenate(sums, axis=1)


def found_at_tokens(tokens, table_ref, stats):
    slot_cols = table_cols(table_ref, SEND3, SLOT_ROWS)
    found = gather_stats(iota((1, 2 * tokens), 1), slot_cols, stats)
    lse_first, lse_second = found[:4, :tokens], found[:4, tokens:]
    top = jnp.maximum(lse_first, lse_second)
    total = top + jnp.log(jnp.exp(lse_first - top) + jnp.exp(lse_second - top))
    shares = jnp.exp(lse_first - total), jnp.exp(lse_second - total)
    delta = found[4:, :tokens] * shares[0] + found[4:, tokens:] * shares[1]
    return slot_cols, total, delta, shares


def total_body(tokens, table_ref, arrived_ref, out_ref):
    slot_cols, total, delta, _ = found_at_tokens(tokens, table_ref, arrived_ref[...])
    stat = jnp.concatenate([total, delta])
    first, second, third_piece = [member.astype(jnp.float32) for member in pieces_of(stat)]
    spare = jnp.zeros((LANES - 9 * STAT, tokens), jnp.float32)
    table = jnp.concatenate(
        [first] * 3 + [second] * 3 + [third_piece] * 3 + [spare]
    ).astype(jnp.bfloat16)
    third_slots = arrived_ref.shape[0]
    lane_third = (iota((third_slots, LANES), 1) % (3 * STAT)) // STAT
    result = jnp.zeros((third_slots, LANES), jnp.float32)
    for third in range(3):
        codes = slot_cols[4 * third : 4 * third + 4]
        cols = [jnp.where(code >= tokens, code - tokens, code) for code in codes]
        chosen = match_cols(cols, iota((LANES, tokens), 1))
        result = jnp.where(lane_third == third, dot(chosen, table, 1, 1), result)
    owners = third_slots // STAT
    by_owner = result.reshape(owners, STAT, LANES)
    out_ref[:, :STAT, :] = by_owner
    above = jnp.concatenate([by_owner[1:], by_owner[:1]])
    below = jnp.concatenate([by_owner[owners - 1 :], by_owner[: owners - 1]])
    half = table_ref[HALF : HALF + 1, :]
    out_ref[:, STAT:, :] = jnp.where(half[None] == 0, above, below)


def total_stats(table, arrived, tokens):
    owners = arrived.shape[0] // STAT
    return pl.pallas_call(
        functools.partial(total_body, tokens),
        out_shape=jax.ShapeDtypeStruct((owners, 2 * STAT, LANES), jnp.float32),
        compiler_params=params(24),
        cost_estimate=cost(2 * 1536 * 1536 * LANES, 1 << 20),
        name="total_stats",
    )(table, arrived)


def prepare_body(tokens, table_ref, arrived_ref, first_ref, second_ref, payload_ref, share_ref):
    @pl.when(pl.program_id(0) == 0)
    def _():
        shares = found_at_tokens(tokens, table_ref, arrived_ref[...])[3]
        spare = jnp.zeros((LANES - STAT, tokens), jnp.float32)
        share_ref[...] = jnp.concatenate([*shares, spare]).T

    back = match_cols(
        table_cols(table_ref, ARRIVAL, SLOT_ROWS), table_row(table_ref, PLACE, PLACE_ROWS)
    )
    rows = [first_ref[:GROUP], second_ref[:GROUP], first_ref[GROUP:], second_ref[GROUP:]]
    payload_ref[...] = dot(back, jnp.concatenate(rows)).astype(jnp.bfloat16)


def prepare(table, home_stats, outs, tokens):
    slots = SLOT_ROWS * LANES
    rows, width = outs[0].shape
    wide = width // 2
    return pl.pallas_call(
        functools.partial(prepare_body, tokens),
        grid=(2,),
        in_specs=[
            table_spec(),
            pl.BlockSpec(home_stats.shape, lambda i: (0, 0)),
            pl.BlockSpec((rows, wide), lambda i: (0, i)),
            pl.BlockSpec((rows, wide), lambda i: (0, i)),
        ],
        out_specs=[
            pl.BlockSpec((slots, wide), lambda i: (0, i)),
            pl.BlockSpec((tokens, LANES), lambda i: (0, 0)),
        ],
        out_shape=[
            jax.ShapeDtypeStruct((slots, 3 * width), jnp.bfloat16),
            jax.ShapeDtypeStruct((tokens, LANES), jnp.float32),
        ],
        compiler_params=params(62),
        cost_estimate=cost(2e9, 1e7),
        name="prepare_outputs",
    )(table, home_stats, *outs)


def backward_tile(query, upstream, keys, values, masked, total_row, delta_row):
    scores = dot(keys, query, 1, 1)
    if masked is not None:
        low, high = scores[GROUP : GROUP + LANES], scores[GROUP + LANES :]
        low = jnp.concatenate(
            [jnp.where(masked, NEG_SELF, low[:, :LANES]), low[:, LANES:]], axis=1
        )
        high = jnp.concatenate(
            [high[:, :LANES], jnp.where(masked, NEG_SELF, high[:, LANES:])], axis=1
        )
        scores = jnp.concatenate([scores[:GROUP], low, high])
    probs = jnp.exp(scores - total_row)
    dots = dot(values, upstream, 1, 1)
    slopes = (probs * (dots - delta_row)).astype(jnp.bfloat16)
    return probs.astype(jnp.bfloat16), slopes


def backward_heads(pair, stat, edge_stat, refs, hash_round, shaped):
    heads, tail, tail_cotangent, prior, nexts = refs
    kept = pl.ds(hash_round * GROUP, GROUP)
    own = iota((LANES, LANES), 0) == iota((LANES, LANES), 1)
    width = tail.shape[1] // 2
    for local in range(2):
        head = pair * 2 + local
        columns = pl.ds(head * DH, DH)
        values_at = pl.ds(width + head * DH, DH)
        total_row, delta_row = stat[head : head + 1], stat[head + 4 : head + 5]
        edge_total, edge_delta = edge_stat[head : head + 1], edge_stat[head + 4 : head + 5]
        raw = jnp.concatenate([heads[0][kept, columns], tail[kept, columns]])
        values = jnp.concatenate([heads[1][kept, columns], tail[kept, values_at]])
        upstream = jnp.concatenate([heads[2][kept, columns], tail_cotangent[kept, columns]])
        units, inverse = unit_rows(raw)
        keys = units.astype(jnp.bfloat16)
        prior_keys = unit_rows(prior[kept, columns])[0].astype(jnp.bfloat16)
        keys_first = jnp.concatenate([prior_keys, keys[:GROUP]])
        values_first = jnp.concatenate([prior[kept, values_at], values[:GROUP]])
        probs, slopes = backward_tile(
            raw[:GROUP],
            upstream[:GROUP],
            keys_first,
            values_first,
            own,
            total_row[:, :GROUP],
            delta_row[:, :GROUP],
        )
        query_first = dot(keys_first, slopes, 0, 0).T
        unit_first = dot(slopes[GROUP:], raw[:GROUP])
        value_first = dot(probs[GROUP:], upstream[:GROUP])

        probs, slopes = backward_tile(
            raw[GROUP:],
            upstream[GROUP:],
            keys,
            values,
            own,
            total_row[:, GROUP:],
            delta_row[:, GROUP:],
        )
        query_second = dot(keys, slopes, 0, 0).T
        unit_both = dot(slopes, raw[GROUP:])
        value_both = dot(probs, upstream[GROUP:])

        next_query = nexts[0][kept, columns]
        next_upstream = nexts[1][kept, columns]
        probs, slopes = backward_tile(
            next_query,
            next_upstream,
            keys[GROUP:],
            values[GROUP:],
            None,
            edge_total,
            edge_delta,
        )
        unit_last = dot(slopes, next_query)
        value_last = dot(probs, next_upstream)

        query_slope = jnp.concatenate([query_first, query_second])
        unit_slope = unit_both + jnp.concatenate([unit_first, unit_last])
        value_slope = value_both + jnp.concatenate([value_first, value_last])
        key_slope = inverse * (
            unit_slope - units * jnp.sum(units * unit_slope, -1, keepdims=True)
        )
        shaped[hash_round, :, local * DH : (local + 1) * DH] = (query_slope + key_slope).astype(
            jnp.bfloat16
        )
        shaped[hash_round, :, (2 + local) * DH : (3 + local) * DH] = value_slope.astype(
            jnp.bfloat16
        )


def backward_body(
    table_ref,
    next_table_ref,
    stats_ref,
    head_query_ref,
    head_value_ref,
    head_cotangent_ref,
    tail_ref,
    tail_cotangent_ref,
    prior_ref,
    next_query_ref,
    next_cotangent_ref,
    _,
    payload_ref,
    stats,
    six,
    double,
    shaped,
    staged,
    load,
    store,
):
    rows = PLACE_ROWS * LANES
    per_round = rows // 2
    sources = [
        stats_ref,
        head_query_ref,
        head_value_ref,
        head_cotangent_ref,
        tail_cotangent_ref,
        next_query_ref,
        next_cotangent_ref,
        tail_ref,
        prior_ref,
    ]
    targets = [stats] + [six.at[i] for i in range(6)] + [double.at[i] for i in range(2)]
    arriving = started(sources, targets, load)
    place_row = table_row(table_ref, PLACE, PLACE_ROWS)
    next_places = table_row(next_table_ref, PLACE, PLACE_ROWS)
    next_row = jnp.concatenate(
        [next_places[:, each * per_round : each * per_round + GROUP] for each in range(2)], axis=1
    )
    back = [
        match_cols(
            table_cols(table_ref, (FIRST16, LAST16)[each], PART_ROWS),
            place_row[:, each * per_round : (each + 1) * per_round],
        )
        for each in range(2)
    ]
    arriving[0].wait()
    own_stats = stats[:, :STAT, :].reshape(-1, LANES)
    next_stats = stats[:, STAT:, :].reshape(-1, LANES)
    found = gather_stats(place_row, table_cols(table_ref, ARRIVAL3, SLOT_ROWS), own_stats)
    edge = gather_stats(next_row, table_cols(next_table_ref, ARRIVAL3, SLOT_ROWS), next_stats)
    for copy in arriving[1:]:
        copy.wait()
    refs = (
        (six.at[0], six.at[1], six.at[2]),
        double.at[0],
        six.at[3],
        double.at[1],
        (six.at[4], six.at[5]),
    )
    leaving = []
    width = shaped.shape[2]
    for pair in range(2):
        for hash_round in range(2):
            backward_heads(
                pair,
                found[:, hash_round * per_round : (hash_round + 1) * per_round],
                edge[:, hash_round * GROUP : (hash_round + 1) * GROUP],
                refs,
                hash_round,
                shaped,
            )
        chunks = 2
        for chunk in range(chunks):
            kept = slice(chunk * 1024 // chunks, (chunk + 1) * 1024 // chunks)
            first = dot(back[0][kept], shaped[0]).reshape(-1, 2, STAT, width)
            second = dot(back[1][kept], shaped[1]).reshape(-1, 2, STAT, width)
            whole = jnp.concatenate(
                [first[:, :1], first[:, 1:] + second[:, :1], second[:, 1:]], axis=1
            ).reshape(-1, width)
            count = whole.shape[0]
            at = pl.ds(chunk * count, count)
            staged[pair, at] = whole.astype(jnp.bfloat16)
            leaving += started(
                [staged.at[pair, at]],
                [payload_ref.at[at, pl.ds((pair + 1) * width, width)]],
                store,
                pair * chunks + chunk,
            )
    for copy in leaving:
        copy.wait()


def backward(table, next_table, stats, heads, tail, tail_cotangent, prior_tail, nexts, payload):
    slots = SLOT_ROWS * LANES
    rows, width = heads[0].shape
    return pl.pallas_call(
        backward_body,
        in_specs=[table_spec(), pl.BlockSpec(next_table.shape, lambda *_: (0, 0))] + anywhere(10),
        out_specs=anywhere(1)[0],
        out_shape=jax.ShapeDtypeStruct((slots, 3 * width), jnp.bfloat16),
        input_output_aliases={11: 0},
        scratch_shapes=[
            pltpu.VMEM(stats.shape, jnp.float32),
            pltpu.VMEM((6, rows, width), jnp.bfloat16),
            pltpu.VMEM((2, rows, 2 * width), jnp.bfloat16),
            pltpu.VMEM((2, 2 * GROUP, width), jnp.bfloat16),
            pltpu.VMEM((2, slots, width), jnp.bfloat16),
            pltpu.SemaphoreType.DMA((9,)),
            pltpu.SemaphoreType.DMA((4,)),
        ],
        compiler_params=params(62),
        cost_estimate=cost(8e9, 1.5e7, 3e6),
        name="backward",
    )(table, next_table, stats, *heads, tail, tail_cotangent, prior_tail, *nexts, payload)


def combine_body(
    table_ref,
    share_ref,
    arrived_ref,
    out_ref,
    first_ref,
    second_ref,
    staged,
    chosen,
    store,
):
    parts, tokens, wide = staged.shape
    token = iota((tokens, 1), 0)
    code = table_row(table_ref, SEND_CODE, SLOT_ROWS)
    chosen[0] = match(token, code)
    chosen[1] = match(token + tokens, code)
    chosen[2] = match(token, table_row(table_ref, SEND, SLOT_ROWS))
    width = parts * wide // 3
    leaving = []
    for half in range(2):
        kept = slice(half * tokens // 2, (half + 1) * tokens // 2)
        at = pl.ds(half * tokens // 2, tokens // 2)
        slopes = dot(chosen[2, kept], arrived_ref[:, width:]).astype(jnp.bfloat16)
        for place in range(4):
            staged[2 + place, kept] = slopes[:, place * wide : (place + 1) * wide]
            leaving += started(
                [staged.at[2 + place, at]],
                [(first_ref, second_ref)[place % 2].at[at, pl.ds((place // 2) * wide, wide)]],
                store,
                half * parts + 2 + place,
            )
        found = 0.0
        for each in range(2):
            share = jnp.concatenate(
                [
                    jnp.broadcast_to(
                        share_ref[kept, 4 * each + head : 4 * each + head + 1], (tokens // 2, DH)
                    )
                    for head in range(4)
                ],
                axis=1,
            )
            found = found + share * dot(chosen[each, kept], arrived_ref[:, :width])
        found = found.astype(jnp.bfloat16)
        for place in range(2):
            staged[place, kept] = found[:, place * wide : (place + 1) * wide]
            leaving += started(
                [staged.at[place, at]],
                [out_ref.at[at, pl.ds(place * wide, wide)]],
                store,
                half * parts + place,
            )
    for copy in leaving:
        copy.wait()


def combine(table, shares, arrived, tokens):
    slots, width = arrived.shape
    wide = width // 6
    return pl.pallas_call(
        combine_body,
        in_specs=[table_spec(), pl.BlockSpec(shares.shape, lambda *_: (0, 0))]
        + [pl.BlockSpec(memory_space=pltpu.VMEM)],
        out_specs=anywhere(3),
        out_shape=[jax.ShapeDtypeStruct((tokens, 2 * wide), jnp.bfloat16)] * 3,
        scratch_shapes=[
            pltpu.VMEM((6, tokens, wide), jnp.bfloat16),
            pltpu.VMEM((3, tokens, slots), jnp.bfloat16),
            pltpu.SemaphoreType.DMA((12,)),
        ],
        compiler_params=params(40),
        cost_estimate=cost(2 * slots * tokens * width, 2 * (slots + tokens) * width),
        name="combine_rows",
    )(table, shares, arrived)


def per_device(query_key, value, attended_cotangent, send_rows, arrival_count, receive_slot):
    tokens, row_width = query_key.shape
    rounds = send_rows.shape[0]
    owners = lax.axis_size("seq")
    capacity = send_rows.shape[1] // owners
    per_owner = rounds * capacity
    slots = owners * per_owner

    code = (tokens * jnp.arange(rounds, dtype=jnp.int32))[:, None]
    half = lax.axis_index("head")

    def by_owner(table):
        return table.reshape(rounds, owners, capacity).transpose(1, 0, 2).reshape(owners, per_owner)

    def by_third(codes):
        return codes.reshape(owners, 3, STAT).transpose(1, 0, 2)

    def sent(packed):
        return exchange(packed.reshape(owners, per_owner, -1)).reshape(slots, -1)

    blocks = send_rows.reshape(rounds, owners, capacity)
    send_rows = jnp.where(half == 0, blocks, blocks[:, ::-1]).reshape(rounds, -1)
    send = by_owner(send_rows)
    send_blocks = jnp.pad(send.reshape(-1, LANES), ((0, 4), (0, 0)))
    packed = pack(send_blocks, query_key, value, attended_cotangent)

    within = jnp.arange(capacity, dtype=jnp.int32)

    def arrivals(counts):
        start = jnp.cumsum(counts, axis=1) - counts + code
        codes = jnp.where(within < counts[:, :, None], start[:, :, None] + within, -1)
        return by_owner(codes)

    tables = to_place(jnp.concatenate([arrival_count, receive_slot], axis=1))
    arrival = arrivals(tables[:, :owners])
    place = tables[:, owners:] + code

    def half_blocks(codes, first):
        return codes[:, first : first + 2 * STAT]

    members = [
        (ARRIVAL3, by_third(arrival)),
        (PLACE, place),
        (ARRIVAL, arrival),
        (SEND, send),
        (SEND3, by_third(by_owner(send_rows + code))),
        (HALF, jnp.full((1, LANES), half, jnp.int32)),
        (FIRST16, half_blocks(arrival, 0)),
        (LAST16, half_blocks(arrival, STAT)),
        (SEND_CODE, by_owner(send_rows + code)),
    ]
    rows = [codes.reshape(-1, LANES) for _, codes in members]
    assert [at for at, _ in members] == [sum(map(len, rows[:i])) for i in range(len(rows))]
    table = jnp.concatenate(rows)
    table = jnp.pad(table, ((0, LANES - len(table)), (0, 0)), constant_values=-1)

    arrived, table = lax.optimization_barrier((sent(packed), table))
    tail = sort_tail(table, arrived, 2 * row_width)
    prior_tail = to_next(tail)
    head_query, head_value, head_cotangent, tail_cotangent, out_second, stat_second = forward_own(
        table, arrived, tail
    )
    out_first, stats = forward_edge(
        table, head_query, head_value, head_cotangent, prior_tail, stat_second
    )
    shared, stats = lax.optimization_barrier((table[:SHARED_ROWS], stats))
    next_table = to_prior(shared)
    next_query = to_prior(head_query)
    next_cotangent = to_prior(head_cotangent)
    home_stats = exchange(stats.reshape(owners, STAT, LANES)).reshape(-1, LANES)
    totals = exchange(total_stats(table, home_stats, tokens))
    payload, shares = prepare(table, home_stats, (out_first, out_second), tokens)
    payload = backward(
        table,
        next_table,
        totals,
        (head_query, head_value, head_cotangent),
        tail,
        tail_cotangent,
        prior_tail,
        (next_query, next_cotangent),
        payload,
    )
    return tuple(combine(table, shares, sent(payload), tokens))


def solution(mesh):
    in_specs = (
        P("seq", "head"),
        P("seq", "head"),
        P("seq", "head"),
        P(None, "seq"),
        P(None, "seq"),
        P(None, "seq"),
    )
    out_specs = (P("seq", "head"), P("seq", "head"), P("seq", "head"))
    return jax.shard_map(
        per_device, mesh=mesh, in_specs=in_specs, out_specs=out_specs, check_vma=False
    )
```

```python
import functools

import jax
import jax.numpy as jnp
from jax import lax
from jax.experimental import pallas as pl
from jax.experimental.pallas import tpu as pltpu
from jax.sharding import PartitionSpec as P

DH = 128
GROUP = 256
NEG_SELF = -100000.0
EPS_KEY = 1e-06
LANES = 128
STAT = 8
PIECES = 3
MIB = 1 << 20


def dot(left, right, left_axis=1, right_axis=0):
    return lax.dot_general(
        left,
        right,
        (((left_axis,), (right_axis,)), ((), ())),
        preferred_element_type=jnp.float32,
    )


def params(mib=62):
    return pltpu.CompilerParams(vmem_limit_bytes=mib * MIB)


def cost(flops, moved, exps=0):
    return pl.CostEstimate(flops=int(flops), bytes_accessed=int(moved), transcendentals=int(exps))


def routed(block, route_of):
    owners, halves = lax.axis_size("seq"), lax.axis_size("head")
    route = [
        (i * halves + half, route_of(i, half, owners) * halves + half)
        for i in range(owners)
        for half in range(halves)
    ]
    return lax.ppermute(block, ("seq", "head"), route)


def to_next(block):
    return routed(block, lambda i, half, n: (i + (1 if half == 0 else -1)) % n)


def to_prior(block):
    return routed(block, lambda i, half, n: (i - (1 if half == 0 else -1)) % n)


def to_place_prior(block):
    return routed(block, lambda i, half, n: (i - 1) % n if half == 0 else n - 1 - (i - 1) % n)


def to_place(block):
    return routed(block, lambda i, half, n: i if half == 0 else n - 1 - i)


def exchange(block):
    return lax.all_to_all(block, "seq", split_axis=0, concat_axis=0, tiled=True)


def match(left, right):
    return jnp.where(left == right, 1.0, 0.0).astype(jnp.bfloat16)


ARRIVAL3, PLACE, ARRIVAL, SEND, SEND3, HALF, FIRST16, LAST16, SEND_CODE = 0, 12, 20, 32, 44, 56, 57, 65, 73
SLOT_ROWS, PLACE_ROWS, PART_ROWS = 12, 8, 8
SHARED_ROWS = 24


def table_row(table_ref, start, count):
    return jnp.concatenate([table_ref[start + i : start + i + 1, :] for i in range(count)], axis=1)


def table_cols(table_ref, start, count):
    turned = table_ref[...].T
    return [turned[:, start + i : start + i + 1] for i in range(count)]


def match_cols(cols, row):
    return jnp.concatenate([match(col, row) for col in cols])


def anywhere(count):
    return [pl.BlockSpec(memory_space=pl.ANY) for _ in range(count)]


def table_spec():
    return pl.BlockSpec((LANES, LANES), lambda *_: (0, 0))


def started(sources, targets, sems, first=0):
    copies = [
        pltpu.make_async_copy(source, target, sems.at[first + i])
        for i, (source, target) in enumerate(zip(sources, targets))
    ]
    for copy in copies:
        copy.start()
    return copies


def iota(shape, axis):
    return lax.broadcasted_iota(jnp.int32, shape, axis)


def pieces_of(wide):
    first = wide.astype(jnp.bfloat16)
    rest = wide - first.astype(jnp.float32)
    second = rest.astype(jnp.bfloat16)
    third = (rest - second.astype(jnp.float32)).astype(jnp.bfloat16)
    return first, second, third


def unit_rows(raw_rows):
    wide = raw_rows.astype(jnp.float32)
    inverse = lax.rsqrt(jnp.sum(wide * wide, -1, keepdims=True) + EPS_KEY)
    return wide * inverse, inverse


def pack_body(index_ref, *refs):
    sources, out_ref, held, staged, chosen, load, store = refs[:3], *refs[3:]
    tokens, width = sources[0].shape
    arriving = started(sources, [held.at[i] for i in range(3)], load)
    turned = index_ref[...].T
    chosen[...] = match_cols(
        [turned[:, i : i + 1] for i in range(SLOT_ROWS)], iota((LANES, tokens), 1)
    )
    steps = 4
    block = chosen.shape[0] // steps
    leaving = []
    for step in range(steps):
        rows = slice(step * block, (step + 1) * block)
        for place in range(3):
            if step == 0:
                arriving[place].wait()
            staged[rows, place * width : (place + 1) * width] = dot(
                chosen[rows], held[place]
            ).astype(jnp.bfloat16)
        leaving += started(
            [staged.at[pl.ds(step * block, block)]],
            [out_ref.at[pl.ds(step * block, block)]],
            store,
            step,
        )
    for copy in leaving:
        copy.wait()


def pack(index, *sources):
    slots = SLOT_ROWS * LANES
    tokens, width = sources[0].shape
    total = width * len(sources)
    return pl.pallas_call(
        pack_body,
        in_specs=[pl.BlockSpec(index.shape, lambda *_: (0, 0))] + anywhere(3),
        out_specs=anywhere(1)[0],
        out_shape=jax.ShapeDtypeStruct((slots, total), jnp.bfloat16),
        scratch_shapes=[
            pltpu.VMEM((3, tokens, width), jnp.bfloat16),
            pltpu.VMEM((slots, total), jnp.bfloat16),
            pltpu.VMEM((slots, tokens), jnp.bfloat16),
            pltpu.SemaphoreType.DMA((3,)),
            pltpu.SemaphoreType.DMA((4,)),
        ],
        compiler_params=params(),
        cost_estimate=cost(2 * slots * tokens * total, 2 * (slots + tokens) * total),
        name="pack_rows",
    )(index, *sources)


def place_cols(table_ref, group):
    cols = table_cols(table_ref, PLACE, PLACE_ROWS)
    each = GROUP // LANES
    first, second = group * each, PLACE_ROWS // 2 + group * each
    return cols[first : first + each], cols[second : second + each]


def tail_body(table_ref, arrived_ref, tail_ref, held, staged, chosen, load, store):
    width = held.shape[1]
    arriving = started([arrived_ref.at[:, pl.ds(0, width)]], [held], load)
    first, second = place_cols(table_ref, 1)
    row = table_row(table_ref, ARRIVAL, SLOT_ROWS)
    for i, col in enumerate(first + second):
        chosen[i * LANES : (i + 1) * LANES] = match(col, row)
    arriving[0].wait()
    leaving = []
    for i in range(2):
        staged[i * GROUP : (i + 1) * GROUP] = dot(
            chosen[i * GROUP : (i + 1) * GROUP], held[...]
        ).astype(jnp.bfloat16)
        at = pl.ds(i * GROUP, GROUP)
        leaving += started([staged.at[at]], [tail_ref.at[at]], store, i)
    for copy in leaving:
        copy.wait()


def sort_tail(table, arrived, width):
    slots = arrived.shape[0]
    wide = width // 4
    return pl.pallas_call(
        tail_body,
        in_specs=[table_spec()] + anywhere(1),
        out_specs=anywhere(1)[0],
        out_shape=jax.ShapeDtypeStruct((2 * GROUP, width), jnp.bfloat16),
        scratch_shapes=[
            pltpu.VMEM((slots, width), jnp.bfloat16),
            pltpu.VMEM((2 * GROUP, width), jnp.bfloat16),
            pltpu.VMEM((2 * GROUP, slots), jnp.bfloat16),
            pltpu.SemaphoreType.DMA((4,)),
            pltpu.SemaphoreType.DMA((4,)),
        ],
        compiler_params=params(),
        cost_estimate=cost(4 * slots * GROUP * width, 2 * (slots + 2 * GROUP) * width),
        name="sort_tail",
    )(table, arrived)


def forward_tile(query, keys, values):
    scores = dot(query, keys, 1, 1)
    own = iota((GROUP, 2 * GROUP), 1) == iota((GROUP, 2 * GROUP), 0) + GROUP
    scores = jnp.where(own, NEG_SELF, scores)
    top = jnp.max(scores, -1, keepdims=True)
    raised = jnp.exp(scores - top)
    total = jnp.sum(raised, -1, keepdims=True)
    weights = (raised * (1.0 / total)).astype(jnp.bfloat16)
    return dot(weights, values), top + jnp.log(total)


def forward_pair(pair, query, raw, values, cotangent, out_ref):
    lane = iota((GROUP, LANES), 1) % STAT
    stat = jnp.zeros((GROUP, LANES), jnp.float32)
    for local in range(2):
        columns = slice(local * DH, (local + 1) * DH)
        keys = unit_rows(raw[:, columns])[0].astype(jnp.bfloat16)
        partial, lse = forward_tile(query[:, columns], keys, values[:, columns])
        out_ref[:, columns] = partial.astype(jnp.bfloat16)
        delta = jnp.sum(partial * cotangent[:, columns].astype(jnp.float32), -1, keepdims=True)
        head = pair * 2 + local
        stat = jnp.where(lane == head, lse, jnp.where(lane == head + 4, delta, stat))
    return stat


def own_body(
    table_ref,
    arrived_query_ref,
    arrived_value_ref,
    arrived_cotangent_ref,
    tail_query_ref,
    tail_value_ref,
    head_query_ref,
    head_value_ref,
    head_cotangent_ref,
    tail_cotangent_ref,
    out_ref,
    stat_ref,
    chosen,
):
    pair = pl.program_id(0)
    hash_round = pl.program_id(1)

    @pl.when((pair == 0) & (hash_round == 0))
    def _():
        row = table_row(table_ref, ARRIVAL, SLOT_ROWS)
        heads, tails = place_cols(table_ref, 0), place_cols(table_ref, 1)
        for each in range(2):
            chosen[each] = match_cols(heads[each] + tails[each], row)

    select_head = chosen[hash_round, :GROUP]
    query = dot(select_head, arrived_query_ref[...]).astype(jnp.bfloat16)
    value = dot(select_head, arrived_value_ref[...]).astype(jnp.bfloat16)
    cotangent = dot(chosen[hash_round], arrived_cotangent_ref[...]).astype(jnp.bfloat16)
    head_query_ref[...] = query
    head_value_ref[...] = value
    head_cotangent_ref[...] = cotangent[:GROUP]
    tail_cotangent_ref[...] = cotangent[GROUP:]
    stat_ref[...] = forward_pair(
        pair,
        tail_query_ref[...],
        jnp.concatenate([query, tail_query_ref[...]]),
        jnp.concatenate([value, tail_value_ref[...]]),
        cotangent[GROUP:],
        out_ref,
    )


def group_spec(offset=0):
    return pl.BlockSpec((GROUP, 2 * DH), lambda p, r: (r, p + offset))


def stat_spec():
    return pl.BlockSpec((GROUP, LANES), lambda p, r: (r, p))


def forward_own(table, arrived, tail):
    slots, width = arrived.shape
    wide = width // 6
    rows = 2 * GROUP
    array = jax.ShapeDtypeStruct((rows, width // 3), jnp.bfloat16)
    return pl.pallas_call(
        own_body,
        grid=(2, 2),
        in_specs=[pl.BlockSpec((LANES, LANES), lambda p, r: (0, 0))]
        + [pl.BlockSpec((slots, wide), lambda p, r, k=k: (0, p + 2 * k)) for k in range(3)]
        + [group_spec(), group_spec(2)],
        out_specs=[group_spec()] * 5 + [stat_spec()],
        out_shape=[array] * 4
        + [
            jax.ShapeDtypeStruct((rows, width // 3), jnp.bfloat16),
            jax.ShapeDtypeStruct((rows, 2 * LANES), jnp.float32),
        ],
        scratch_shapes=[pltpu.VMEM((2, 2 * GROUP, slots), jnp.bfloat16)],
        compiler_params=params(),
        cost_estimate=cost(5e9, 1e7, 8 * GROUP * 512),
        name="forward_own",
    )(table, arrived, arrived, arrived, tail, tail)


def edge_body(
    table_ref,
    query_ref,
    value_ref,
    cotangent_ref,
    prior_ref,
    second_stat_ref,
    out_ref,
    stats_ref,
    three,
    prior,
    second_stat,
    staged,
    both,
    load,
    store,
):
    each = [pl.ds(hash_round * GROUP, GROUP) for hash_round in range(2)]
    arriving = [
        started(
            [source.at[at] for source in (query_ref, prior_ref, value_ref, cotangent_ref)],
            [three.at[0, at], prior.at[at], three.at[1, at], three.at[2, at]],
            load,
            4 * hash_round,
        )
        for hash_round, at in enumerate(each)
    ]
    arriving[1] += started([second_stat_ref], [second_stat], load, 8)
    place_row = table_row(table_ref, PLACE, PLACE_ROWS)
    arrival_cols = table_cols(table_ref, ARRIVAL3, SLOT_ROWS)
    width = staged.shape[1]
    leaving = []
    for hash_round in range(2):
        kept = slice(hash_round * GROUP, (hash_round + 1) * GROUP)
        at = each[hash_round]
        for copy in arriving[hash_round]:
            copy.wait()
        stat = 0.0
        for pair in range(2):
            columns = slice(pair * 2 * DH, (pair + 1) * 2 * DH)
            values_at = slice(width + pair * 2 * DH, width + (pair + 1) * 2 * DH)
            query = three[0, kept, columns]
            stat = stat + forward_pair(
                pair,
                query,
                jnp.concatenate([prior[kept, columns], query]),
                jnp.concatenate([prior[kept, values_at], three[1, kept, columns]]),
                three[2, kept, columns],
                staged.at[at, pl.ds(pair * 2 * DH, 2 * DH)],
            )
        leaving += started([staged.at[at]], [out_ref.at[at]], store, hash_round)
        both[2 * hash_round * GROUP : (2 * hash_round + 1) * GROUP] = stat
    for hash_round in range(2):
        kept = slice(hash_round * GROUP, (hash_round + 1) * GROUP)
        both[(2 * hash_round + 1) * GROUP : (2 * hash_round + 2) * GROUP] = (
            second_stat[kept, :LANES] + second_stat[kept, LANES:]
        )
    rows = 4 * GROUP
    piece = iota((rows, LANES), 1) // (PIECES * STAT)
    first, second, third = pieces_of(both[...])
    nothing = jnp.zeros((rows, LANES), jnp.bfloat16)
    stats = jnp.where(
        piece == 0,
        first,
        jnp.where(piece == 1, second, jnp.where(piece == 2, third, nothing)),
    )
    third_slots = stats_ref.shape[0]
    lane_third = (iota((third_slots, LANES), 1) % (3 * STAT)) // STAT
    result = jnp.zeros((third_slots, LANES), jnp.float32)
    for third in range(3):
        span = slice((0, 0, rows // 2)[third], (rows // 2, rows, rows)[third])
        back = match_cols(arrival_cols[4 * third : 4 * third + 4], place_row[:, span])
        result = jnp.where(lane_third == third, dot(back, stats[span]), result)
    stats_ref[...] = result
    for copy in leaving:
        copy.wait()


def forward_edge(table, query, value, cotangent, prior_tail, second_stat):
    rows, width = query.shape
    third_slots = SLOT_ROWS * LANES // 3
    return pl.pallas_call(
        edge_body,
        in_specs=[table_spec()] + anywhere(5),
        out_specs=anywhere(1) + [pl.BlockSpec(memory_space=pltpu.VMEM)],
        out_shape=[
            jax.ShapeDtypeStruct((rows, width), jnp.bfloat16),
            jax.ShapeDtypeStruct((third_slots, LANES), jnp.float32),
        ],
        scratch_shapes=[
            pltpu.VMEM((3, rows, width), jnp.bfloat16),
            pltpu.VMEM((rows, 2 * width), jnp.bfloat16),
            pltpu.VMEM((rows, 2 * LANES), jnp.float32),
            pltpu.VMEM((rows, width), jnp.bfloat16),
            pltpu.VMEM((2 * rows, LANES), jnp.float32),
            pltpu.SemaphoreType.DMA((9,)),
            pltpu.SemaphoreType.DMA((2,)),
        ],
        compiler_params=params(59),
        cost_estimate=cost(2e9, 4e6, 8 * GROUP * 512),
        name="forward_edge",
    )(table, query, value, cotangent, prior_tail, second_stat)


def gather_stats(codes_row, slot_cols, stats):
    narrow = stats.astype(jnp.bfloat16)
    half = codes_row.shape[1] // 2
    sums = [0.0, 0.0]
    for third in range(3):
        for each in ((0,), (0, 1), (1,))[third]:
            codes = codes_row[:, each * half : (each + 1) * half]
            chosen = match_cols(slot_cols[4 * third : 4 * third + 4], codes)
            found = dot(narrow, chosen, 0, 0)
            for piece in range(PIECES):
                at = piece * PIECES * STAT + third * STAT
                sums[each] = sums[each] + found[at : at + STAT]
    return jnp.concatenate(sums, axis=1)


def found_at_tokens(tokens, table_ref, stats):
    slot_cols = table_cols(table_ref, SEND3, SLOT_ROWS)
    found = gather_stats(iota((1, 2 * tokens), 1), slot_cols, stats)
    lse_first, lse_second = found[:4, :tokens], found[:4, tokens:]
    top = jnp.maximum(lse_first, lse_second)
    total = top + jnp.log(jnp.exp(lse_first - top) + jnp.exp(lse_second - top))
    shares = jnp.exp(lse_first - total), jnp.exp(lse_second - total)
    delta = found[4:, :tokens] * shares[0] + found[4:, tokens:] * shares[1]
    return slot_cols, total, delta, shares


def total_body(tokens, table_ref, arrived_ref, out_ref):
    slot_cols, total, delta, _ = found_at_tokens(tokens, table_ref, arrived_ref[...])
    stat = jnp.concatenate([total, delta])
    first, second, third_piece = [member.astype(jnp.float32) for member in pieces_of(stat)]
    spare = jnp.zeros((LANES - 9 * STAT, tokens), jnp.float32)
    table = jnp.concatenate(
        [first] * 3 + [second] * 3 + [third_piece] * 3 + [spare]
    ).astype(jnp.bfloat16)
    third_slots = arrived_ref.shape[0]
    lane_third = (iota((third_slots, LANES), 1) % (3 * STAT)) // STAT
    result = jnp.zeros((third_slots, LANES), jnp.float32)
    for third in range(3):
        codes = slot_cols[4 * third : 4 * third + 4]
        cols = [jnp.where(code >= tokens, code - tokens, code) for code in codes]
        chosen = match_cols(cols, iota((LANES, tokens), 1))
        result = jnp.where(lane_third == third, dot(chosen, table, 1, 1), result)
    owners = third_slots // STAT
    by_owner = result.reshape(owners, STAT, LANES)
    out_ref[:, :STAT, :] = by_owner
    above = jnp.concatenate([by_owner[1:], by_owner[:1]])
    below = jnp.concatenate([by_owner[owners - 1 :], by_owner[: owners - 1]])
    half = table_ref[HALF : HALF + 1, :]
    out_ref[:, STAT:, :] = jnp.where(half[None] == 0, above, below)


def total_stats(table, arrived, tokens):
    owners = arrived.shape[0] // STAT
    return pl.pallas_call(
        functools.partial(total_body, tokens),
        out_shape=jax.ShapeDtypeStruct((owners, 2 * STAT, LANES), jnp.float32),
        compiler_params=params(24),
        cost_estimate=cost(2 * 1536 * 1536 * LANES, 1 << 20),
        name="total_stats",
    )(table, arrived)


def prepare_body(tokens, table_ref, arrived_ref, first_ref, second_ref, payload_ref, share_ref):
    @pl.when(pl.program_id(0) == 0)
    def _():
        shares = found_at_tokens(tokens, table_ref, arrived_ref[...])[3]
        spare = jnp.zeros((LANES - STAT, tokens), jnp.float32)
        share_ref[...] = jnp.concatenate([*shares, spare]).T

    back = match_cols(
        table_cols(table_ref, ARRIVAL, SLOT_ROWS), table_row(table_ref, PLACE, PLACE_ROWS)
    )
    rows = [first_ref[:GROUP], second_ref[:GROUP], first_ref[GROUP:], second_ref[GROUP:]]
    payload_ref[...] = dot(back, jnp.concatenate(rows)).astype(jnp.bfloat16)


def prepare(table, home_stats, outs, tokens):
    slots = SLOT_ROWS * LANES
    rows, width = outs[0].shape
    wide = width // 2
    return pl.pallas_call(
        functools.partial(prepare_body, tokens),
        grid=(2,),
        in_specs=[
            table_spec(),
            pl.BlockSpec(home_stats.shape, lambda i: (0, 0)),
            pl.BlockSpec((rows, wide), lambda i: (0, i)),
            pl.BlockSpec((rows, wide), lambda i: (0, i)),
        ],
        out_specs=[
            pl.BlockSpec((slots, wide), lambda i: (0, i)),
            pl.BlockSpec((tokens, LANES), lambda i: (0, 0)),
        ],
        out_shape=[
            jax.ShapeDtypeStruct((slots, 3 * width), jnp.bfloat16),
            jax.ShapeDtypeStruct((tokens, LANES), jnp.float32),
        ],
        compiler_params=params(62),
        cost_estimate=cost(2e9, 1e7),
        name="prepare_outputs",
    )(table, home_stats, *outs)


def backward_tile(query, upstream, keys, values, masked, total_row, delta_row):
    scores = dot(keys, query, 1, 1)
    if masked is not None:
        low, high = scores[GROUP : GROUP + LANES], scores[GROUP + LANES :]
        low = jnp.concatenate(
            [jnp.where(masked, NEG_SELF, low[:, :LANES]), low[:, LANES:]], axis=1
        )
        high = jnp.concatenate(
            [high[:, :LANES], jnp.where(masked, NEG_SELF, high[:, LANES:])], axis=1
        )
        scores = jnp.concatenate([scores[:GROUP], low, high])
    probs = jnp.exp(scores - total_row)
    dots = dot(values, upstream, 1, 1)
    slopes = (probs * (dots - delta_row)).astype(jnp.bfloat16)
    return probs.astype(jnp.bfloat16), slopes


def backward_heads(pair, stat, edge_stat, refs, hash_round, shaped):
    heads, tail, tail_cotangent, prior, nexts = refs
    kept = pl.ds(hash_round * GROUP, GROUP)
    own = iota((LANES, LANES), 0) == iota((LANES, LANES), 1)
    width = tail.shape[1] // 2
    for local in range(2):
        head = pair * 2 + local
        columns = pl.ds(head * DH, DH)
        values_at = pl.ds(width + head * DH, DH)
        total_row, delta_row = stat[head : head + 1], stat[head + 4 : head + 5]
        edge_total, edge_delta = edge_stat[head : head + 1], edge_stat[head + 4 : head + 5]
        raw = jnp.concatenate([heads[0][kept, columns], tail[kept, columns]])
        values = jnp.concatenate([heads[1][kept, columns], tail[kept, values_at]])
        upstream = jnp.concatenate([heads[2][kept, columns], tail_cotangent[kept, columns]])
        units, inverse = unit_rows(raw)
        keys = units.astype(jnp.bfloat16)
        prior_keys = unit_rows(prior[kept, columns])[0].astype(jnp.bfloat16)
        keys_first = jnp.concatenate([prior_keys, keys[:GROUP]])
        values_first = jnp.concatenate([prior[kept, values_at], values[:GROUP]])
        probs, slopes = backward_tile(
            raw[:GROUP],
            upstream[:GROUP],
            keys_first,
            values_first,
            own,
            total_row[:, :GROUP],
            delta_row[:, :GROUP],
        )
        query_first = dot(keys_first, slopes, 0, 0).T
        unit_first = dot(slopes[GROUP:], raw[:GROUP])
        value_first = dot(probs[GROUP:], upstream[:GROUP])

        probs, slopes = backward_tile(
            raw[GROUP:],
            upstream[GROUP:],
            keys,
            values,
            own,
            total_row[:, GROUP:],
            delta_row[:, GROUP:],
        )
        query_second = dot(keys, slopes, 0, 0).T
        unit_both = dot(slopes, raw[GROUP:])
        value_both = dot(probs, upstream[GROUP:])

        next_query = nexts[0][kept, columns]
        next_upstream = nexts[1][kept, columns]
        probs, slopes = backward_tile(
            next_query,
            next_upstream,
            keys[GROUP:],
            values[GROUP:],
            None,
            edge_total,
            edge_delta,
        )
        unit_last = dot(slopes, next_query)
        value_last = dot(probs, next_upstream)

        query_slope = jnp.concatenate([query_first, query_second])
        unit_slope = unit_both + jnp.concatenate([unit_first, unit_last])
        value_slope = value_both + jnp.concatenate([value_first, value_last])
        key_slope = inverse * (
            unit_slope - units * jnp.sum(units * unit_slope, -1, keepdims=True)
        )
        shaped[hash_round, :, local * DH : (local + 1) * DH] = (query_slope + key_slope).astype(
            jnp.bfloat16
        )
        shaped[hash_round, :, (2 + local) * DH : (3 + local) * DH] = value_slope.astype(
            jnp.bfloat16
        )


def backward_body(
    table_ref,
    next_table_ref,
    stats_ref,
    head_query_ref,
    head_value_ref,
    head_cotangent_ref,
    tail_ref,
    tail_cotangent_ref,
    prior_ref,
    next_query_ref,
    next_cotangent_ref,
    _,
    payload_ref,
    stats,
    six,
    double,
    shaped,
    staged,
    load,
    store,
):
    rows = PLACE_ROWS * LANES
    per_round = rows // 2
    sources = [
        stats_ref,
        head_query_ref,
        head_value_ref,
        head_cotangent_ref,
        tail_cotangent_ref,
        next_query_ref,
        next_cotangent_ref,
        tail_ref,
        prior_ref,
    ]
    targets = [stats] + [six.at[i] for i in range(6)] + [double.at[i] for i in range(2)]
    arriving = started(sources, targets, load)
    place_row = table_row(table_ref, PLACE, PLACE_ROWS)
    next_places = table_row(next_table_ref, PLACE, PLACE_ROWS)
    next_row = jnp.concatenate(
        [next_places[:, each * per_round : each * per_round + GROUP] for each in range(2)], axis=1
    )
    back = [
        match_cols(
            table_cols(table_ref, (FIRST16, LAST16)[each], PART_ROWS),
            place_row[:, each * per_round : (each + 1) * per_round],
        )
        for each in range(2)
    ]
    arriving[0].wait()
    own_stats = stats[:, :STAT, :].reshape(-1, LANES)
    next_stats = stats[:, STAT:, :].reshape(-1, LANES)
    found = gather_stats(place_row, table_cols(table_ref, ARRIVAL3, SLOT_ROWS), own_stats)
    edge = gather_stats(next_row, table_cols(next_table_ref, ARRIVAL3, SLOT_ROWS), next_stats)
    for copy in arriving[1:]:
        copy.wait()
    refs = (
        (six.at[0], six.at[1], six.at[2]),
        double.at[0],
        six.at[3],
        double.at[1],
        (six.at[4], six.at[5]),
    )
    leaving = []
    width = shaped.shape[2]
    for pair in range(2):
        for hash_round in range(2):
            backward_heads(
                pair,
                found[:, hash_round * per_round : (hash_round + 1) * per_round],
                edge[:, hash_round * GROUP : (hash_round + 1) * GROUP],
                refs,
                hash_round,
                shaped,
            )
        chunks = 2
        for chunk in range(chunks):
            kept = slice(chunk * 1024 // chunks, (chunk + 1) * 1024 // chunks)
            first = dot(back[0][kept], shaped[0]).reshape(-1, 2, STAT, width)
            second = dot(back[1][kept], shaped[1]).reshape(-1, 2, STAT, width)
            whole = jnp.concatenate(
                [first[:, :1], first[:, 1:] + second[:, :1], second[:, 1:]], axis=1
            ).reshape(-1, width)
            count = whole.shape[0]
            at = pl.ds(chunk * count, count)
            staged[pair, at] = whole.astype(jnp.bfloat16)
            leaving += started(
                [staged.at[pair, at]],
                [payload_ref.at[at, pl.ds((pair + 1) * width, width)]],
                store,
                pair * chunks + chunk,
            )
    for copy in leaving:
        copy.wait()


def backward(table, next_table, stats, heads, tail, tail_cotangent, prior_tail, nexts, payload):
    slots = SLOT_ROWS * LANES
    rows, width = heads[0].shape
    return pl.pallas_call(
        backward_body,
        in_specs=[table_spec(), pl.BlockSpec(next_table.shape, lambda *_: (0, 0))] + anywhere(10),
        out_specs=anywhere(1)[0],
        out_shape=jax.ShapeDtypeStruct((slots, 3 * width), jnp.bfloat16),
        input_output_aliases={11: 0},
        scratch_shapes=[
            pltpu.VMEM(stats.shape, jnp.float32),
            pltpu.VMEM((6, rows, width), jnp.bfloat16),
            pltpu.VMEM((2, rows, 2 * width), jnp.bfloat16),
            pltpu.VMEM((2, 2 * GROUP, width), jnp.bfloat16),
            pltpu.VMEM((2, slots, width), jnp.bfloat16),
            pltpu.SemaphoreType.DMA((9,)),
            pltpu.SemaphoreType.DMA((4,)),
        ],
        compiler_params=params(57),
        cost_estimate=cost(8e9, 1.5e7, 3e6),
        name="backward",
    )(table, next_table, stats, *heads, tail, tail_cotangent, prior_tail, *nexts, payload)


def combine_body(
    table_ref,
    share_ref,
    arrived_ref,
    out_ref,
    first_ref,
    second_ref,
    staged,
    chosen,
    store,
):
    parts, tokens, wide = staged.shape
    token = iota((tokens, 1), 0)
    code = table_row(table_ref, SEND_CODE, SLOT_ROWS)
    chosen[0] = match(token, code)
    chosen[1] = match(token + tokens, code)
    chosen[2] = match(token, table_row(table_ref, SEND, SLOT_ROWS))
    width = parts * wide // 3
    leaving = []
    for half in range(2):
        kept = slice(half * tokens // 2, (half + 1) * tokens // 2)
        at = pl.ds(half * tokens // 2, tokens // 2)
        slopes = dot(chosen[2, kept], arrived_ref[:, width:]).astype(jnp.bfloat16)
        for place in range(4):
            staged[2 + place, kept] = slopes[:, place * wide : (place + 1) * wide]
            leaving += started(
                [staged.at[2 + place, at]],
                [(first_ref, second_ref)[place % 2].at[at, pl.ds((place // 2) * wide, wide)]],
                store,
                half * parts + 2 + place,
            )
        found = 0.0
        for each in range(2):
            share = jnp.concatenate(
                [
                    jnp.broadcast_to(
                        share_ref[kept, 4 * each + head : 4 * each + head + 1], (tokens // 2, DH)
                    )
                    for head in range(4)
                ],
                axis=1,
            )
            found = found + share * dot(chosen[each, kept], arrived_ref[:, :width])
        found = found.astype(jnp.bfloat16)
        for place in range(2):
            staged[place, kept] = found[:, place * wide : (place + 1) * wide]
            leaving += started(
                [staged.at[place, at]],
                [out_ref.at[at, pl.ds(place * wide, wide)]],
                store,
                half * parts + place,
            )
    for copy in leaving:
        copy.wait()


def combine(table, shares, arrived, tokens):
    slots, width = arrived.shape
    wide = width // 6
    return pl.pallas_call(
        combine_body,
        in_specs=[table_spec(), pl.BlockSpec(shares.shape, lambda *_: (0, 0))]
        + [pl.BlockSpec(memory_space=pltpu.VMEM)],
        out_specs=anywhere(3),
        out_shape=[jax.ShapeDtypeStruct((tokens, 2 * wide), jnp.bfloat16)] * 3,
        scratch_shapes=[
            pltpu.VMEM((6, tokens, wide), jnp.bfloat16),
            pltpu.VMEM((3, tokens, slots), jnp.bfloat16),
            pltpu.SemaphoreType.DMA((12,)),
        ],
        compiler_params=params(40),
        cost_estimate=cost(2 * slots * tokens * width, 2 * (slots + tokens) * width),
        name="combine_rows",
    )(table, shares, arrived)


def per_device(query_key, value, attended_cotangent, send_rows, arrival_count, receive_slot):
    tokens, row_width = query_key.shape
    rounds = send_rows.shape[0]
    owners = lax.axis_size("seq")
    capacity = send_rows.shape[1] // owners
    per_owner = rounds * capacity
    slots = owners * per_owner

    code = (tokens * jnp.arange(rounds, dtype=jnp.int32))[:, None]
    half = lax.axis_index("head")

    def by_owner(table):
        return table.reshape(rounds, owners, capacity).transpose(1, 0, 2).reshape(owners, per_owner)

    def by_third(codes):
        return codes.reshape(owners, 3, STAT).transpose(1, 0, 2)

    def sent(packed):
        return exchange(packed.reshape(owners, per_owner, -1)).reshape(slots, -1)

    blocks = send_rows.reshape(rounds, owners, capacity)
    send_rows = jnp.where(half == 0, blocks, blocks[:, ::-1]).reshape(rounds, -1)
    send = by_owner(send_rows)
    send_blocks = jnp.pad(send.reshape(-1, LANES), ((0, 4), (0, 0)))
    packed = pack(send_blocks, query_key, value, attended_cotangent)

    within = jnp.arange(capacity, dtype=jnp.int32)

    def arrivals(counts):
        start = jnp.cumsum(counts, axis=1) - counts + code
        codes = jnp.where(within < counts[:, :, None], start[:, :, None] + within, -1)
        return by_owner(codes)

    tables = to_place(jnp.concatenate([arrival_count, receive_slot], axis=1))
    packed, tables = lax.optimization_barrier((packed, tables))
    arrival = arrivals(tables[:, :owners])
    place = tables[:, owners:] + code

    def half_blocks(codes, first):
        return codes[:, first : first + 2 * STAT]

    members = [
        (ARRIVAL3, by_third(arrival)),
        (PLACE, place),
        (ARRIVAL, arrival),
        (SEND, send),
        (SEND3, by_third(by_owner(send_rows + code))),
        (HALF, jnp.full((1, LANES), half, jnp.int32)),
        (FIRST16, half_blocks(arrival, 0)),
        (LAST16, half_blocks(arrival, STAT)),
        (SEND_CODE, by_owner(send_rows + code)),
    ]
    rows = [codes.reshape(-1, LANES) for _, codes in members]
    assert [at for at, _ in members] == [sum(map(len, rows[:i])) for i in range(len(rows))]
    table = jnp.concatenate(rows)
    table = jnp.pad(table, ((0, LANES - len(table)), (0, 0)), constant_values=-1)

    arrived, table = lax.optimization_barrier((sent(packed), table))
    tail = sort_tail(table, arrived, 2 * row_width)
    prior_tail = to_next(tail)
    head_query, head_value, head_cotangent, tail_cotangent, out_second, stat_second = forward_own(
        table, arrived, tail
    )
    out_first, stats = forward_edge(
        table, head_query, head_value, head_cotangent, prior_tail, stat_second
    )
    shared, stats = lax.optimization_barrier((table[:SHARED_ROWS], stats))
    next_table = to_prior(shared)
    next_query = to_prior(head_query)
    next_cotangent = to_prior(head_cotangent)
    home_stats = exchange(stats.reshape(owners, STAT, LANES)).reshape(-1, LANES)
    totals = exchange(total_stats(table, home_stats, tokens))
    payload, shares = prepare(table, home_stats, (out_first, out_second), tokens)
    payload = backward(
        table,
        next_table,
        totals,
        (head_query, head_value, head_cotangent),
        tail,
        tail_cotangent,
        prior_tail,
        (next_query, next_cotangent),
        payload,
    )
    return tuple(combine(table, shares, sent(payload), tokens))


def solution(mesh):
    in_specs = (
        P("seq", "head"),
        P("seq", "head"),
        P("seq", "head"),
        P(None, "seq"),
        P(None, "seq"),
        P(None, "seq"),
    )
    out_specs = (P("seq", "head"), P("seq", "head"), P("seq", "head"))
    return jax.shard_map(
        per_device, mesh=mesh, in_specs=in_specs, out_specs=out_specs, check_vma=False
    )
```

```python
import functools

import jax
import jax.numpy as jnp
from jax import lax
from jax.experimental import pallas as pl
from jax.experimental.pallas import tpu as pltpu
from jax.sharding import PartitionSpec as P

DH = 128
GROUP = 256
NEG_SELF = -100000.0
EPS_KEY = 1e-06
LANES = 128
STAT = 8
PIECES = 3
MIB = 1 << 20


def dot(left, right, left_axis=1, right_axis=0):
    return lax.dot_general(
        left,
        right,
        (((left_axis,), (right_axis,)), ((), ())),
        preferred_element_type=jnp.float32,
    )


def params(mib=62):
    return pltpu.CompilerParams(vmem_limit_bytes=mib * MIB)


def cost(flops, moved, exps=0):
    return pl.CostEstimate(flops=int(flops), bytes_accessed=int(moved), transcendentals=int(exps))


def routed(block, route_of):
    owners, halves = lax.axis_size("seq"), lax.axis_size("head")
    route = [
        (i * halves + half, route_of(i, half, owners) * halves + half)
        for i in range(owners)
        for half in range(halves)
    ]
    return lax.ppermute(block, ("seq", "head"), route)


def to_next(block):
    return routed(block, lambda i, half, n: (i + (1 if half == 0 else -1)) % n)


def to_prior(block):
    return routed(block, lambda i, half, n: (i - (1 if half == 0 else -1)) % n)


def to_place_prior(block):
    return routed(block, lambda i, half, n: (i - 1) % n if half == 0 else n - 1 - (i - 1) % n)


def to_place(block):
    return routed(block, lambda i, half, n: i if half == 0 else n - 1 - i)


def exchange(block):
    return lax.all_to_all(block, "seq", split_axis=0, concat_axis=0, tiled=True)


def match(left, right):
    return jnp.where(left == right, 1.0, 0.0).astype(jnp.bfloat16)


ARRIVAL3, PLACE, ARRIVAL, SEND, SEND3, HALF, FIRST16, LAST16, SEND_CODE = 0, 12, 20, 32, 44, 56, 57, 65, 73
SLOT_ROWS, PLACE_ROWS, PART_ROWS = 12, 8, 8
SHARED_ROWS = 24


def table_row(table_ref, start, count):
    return jnp.concatenate([table_ref[start + i : start + i + 1, :] for i in range(count)], axis=1)


def table_cols(table_ref, start, count):
    turned = table_ref[...].T
    return [turned[:, start + i : start + i + 1] for i in range(count)]


def match_cols(cols, row):
    return jnp.concatenate([match(col, row) for col in cols])


def anywhere(count):
    return [pl.BlockSpec(memory_space=pl.ANY) for _ in range(count)]


def table_spec():
    return pl.BlockSpec((LANES, LANES), lambda *_: (0, 0))


def started(sources, targets, sems, first=0):
    copies = [
        pltpu.make_async_copy(source, target, sems.at[first + i])
        for i, (source, target) in enumerate(zip(sources, targets))
    ]
    for copy in copies:
        copy.start()
    return copies


def iota(shape, axis):
    return lax.broadcasted_iota(jnp.int32, shape, axis)


def pieces_of(wide):
    first = wide.astype(jnp.bfloat16)
    rest = wide - first.astype(jnp.float32)
    second = rest.astype(jnp.bfloat16)
    third = (rest - second.astype(jnp.float32)).astype(jnp.bfloat16)
    return first, second, third


def unit_rows(raw_rows):
    wide = raw_rows.astype(jnp.float32)
    inverse = lax.rsqrt(jnp.sum(wide * wide, -1, keepdims=True) + EPS_KEY)
    return wide * inverse, inverse


def pack_body(index_ref, *refs):
    sources, out_ref, held, staged, chosen, load, store = refs[:3], *refs[3:]
    tokens, width = sources[0].shape
    arriving = started(sources, [held.at[i] for i in range(3)], load)
    turned = index_ref[...].T
    chosen[...] = match_cols(
        [turned[:, i : i + 1] for i in range(SLOT_ROWS)], iota((LANES, tokens), 1)
    )
    steps = 4
    block = chosen.shape[0] // steps
    leaving = []
    for step in range(steps):
        rows = slice(step * block, (step + 1) * block)
        for place in range(3):
            if step == 0:
                arriving[place].wait()
            staged[rows, place * width : (place + 1) * width] = dot(
                chosen[rows], held[place]
            ).astype(jnp.bfloat16)
        leaving += started(
            [staged.at[pl.ds(step * block, block)]],
            [out_ref.at[pl.ds(step * block, block)]],
            store,
            step,
        )
    for copy in leaving:
        copy.wait()


def pack(index, *sources):
    slots = SLOT_ROWS * LANES
    tokens, width = sources[0].shape
    total = width * len(sources)
    return pl.pallas_call(
        pack_body,
        in_specs=[pl.BlockSpec(index.shape, lambda *_: (0, 0))] + anywhere(3),
        out_specs=anywhere(1)[0],
        out_shape=jax.ShapeDtypeStruct((slots, total), jnp.bfloat16),
        scratch_shapes=[
            pltpu.VMEM((3, tokens, width), jnp.bfloat16),
            pltpu.VMEM((slots, total), jnp.bfloat16),
            pltpu.VMEM((slots, tokens), jnp.bfloat16),
            pltpu.SemaphoreType.DMA((3,)),
            pltpu.SemaphoreType.DMA((4,)),
        ],
        compiler_params=params(),
        cost_estimate=cost(2 * slots * tokens * total, 2 * (slots + tokens) * total),
        name="pack_rows",
    )(index, *sources)


def place_cols(table_ref, group):
    cols = table_cols(table_ref, PLACE, PLACE_ROWS)
    each = GROUP // LANES
    first, second = group * each, PLACE_ROWS // 2 + group * each
    return cols[first : first + each], cols[second : second + each]


def tail_body(table_ref, arrived_ref, tail_ref, held, staged, chosen, load, store):
    width = held.shape[1]
    arriving = started([arrived_ref.at[:, pl.ds(0, width)]], [held], load)
    first, second = place_cols(table_ref, 1)
    row = table_row(table_ref, ARRIVAL, SLOT_ROWS)
    for i, col in enumerate(first + second):
        chosen[i * LANES : (i + 1) * LANES] = match(col, row)
    arriving[0].wait()
    leaving = []
    for i in range(2):
        staged[i * GROUP : (i + 1) * GROUP] = dot(
            chosen[i * GROUP : (i + 1) * GROUP], held[...]
        ).astype(jnp.bfloat16)
        at = pl.ds(i * GROUP, GROUP)
        leaving += started([staged.at[at]], [tail_ref.at[at]], store, i)
    for copy in leaving:
        copy.wait()


def sort_tail(table, arrived, width):
    slots = arrived.shape[0]
    wide = width // 4
    return pl.pallas_call(
        tail_body,
        in_specs=[table_spec()] + anywhere(1),
        out_specs=anywhere(1)[0],
        out_shape=jax.ShapeDtypeStruct((2 * GROUP, width), jnp.bfloat16),
        scratch_shapes=[
            pltpu.VMEM((slots, width), jnp.bfloat16),
            pltpu.VMEM((2 * GROUP, width), jnp.bfloat16),
            pltpu.VMEM((2 * GROUP, slots), jnp.bfloat16),
            pltpu.SemaphoreType.DMA((4,)),
            pltpu.SemaphoreType.DMA((4,)),
        ],
        compiler_params=params(),
        cost_estimate=cost(4 * slots * GROUP * width, 2 * (slots + 2 * GROUP) * width),
        name="sort_tail",
    )(table, arrived)


def forward_tile(query, keys, values):
    scores = dot(query, keys, 1, 1)
    own = iota((GROUP, 2 * GROUP), 1) == iota((GROUP, 2 * GROUP), 0) + GROUP
    scores = jnp.where(own, NEG_SELF, scores)
    top = jnp.max(scores, -1, keepdims=True)
    raised = jnp.exp(scores - top)
    total = jnp.sum(raised, -1, keepdims=True)
    weights = (raised * (1.0 / total)).astype(jnp.bfloat16)
    return dot(weights, values), top + jnp.log(total)


def forward_pair(pair, query, raw, values, cotangent, out_ref):
    lane = iota((GROUP, LANES), 1) % STAT
    stat = jnp.zeros((GROUP, LANES), jnp.float32)
    for local in range(2):
        columns = slice(local * DH, (local + 1) * DH)
        keys = unit_rows(raw[:, columns])[0].astype(jnp.bfloat16)
        partial, lse = forward_tile(query[:, columns], keys, values[:, columns])
        out_ref[:, columns] = partial.astype(jnp.bfloat16)
        delta = jnp.sum(partial * cotangent[:, columns].astype(jnp.float32), -1, keepdims=True)
        head = pair * 2 + local
        stat = jnp.where(lane == head, lse, jnp.where(lane == head + 4, delta, stat))
    return stat


def own_body(
    table_ref,
    arrived_query_ref,
    arrived_value_ref,
    arrived_cotangent_ref,
    tail_query_ref,
    tail_value_ref,
    head_query_ref,
    head_value_ref,
    head_cotangent_ref,
    tail_cotangent_ref,
    out_ref,
    stat_ref,
    chosen,
):
    pair = pl.program_id(0)
    hash_round = pl.program_id(1)

    @pl.when((pair == 0) & (hash_round == 0))
    def _():
        row = table_row(table_ref, ARRIVAL, SLOT_ROWS)
        heads, tails = place_cols(table_ref, 0), place_cols(table_ref, 1)
        for each in range(2):
            chosen[each] = match_cols(heads[each] + tails[each], row)

    select_head = chosen[hash_round, :GROUP]
    query = dot(select_head, arrived_query_ref[...]).astype(jnp.bfloat16)
    value = dot(select_head, arrived_value_ref[...]).astype(jnp.bfloat16)
    cotangent = dot(chosen[hash_round], arrived_cotangent_ref[...]).astype(jnp.bfloat16)
    head_query_ref[...] = query
    head_value_ref[...] = value
    head_cotangent_ref[...] = cotangent[:GROUP]
    tail_cotangent_ref[...] = cotangent[GROUP:]
    stat_ref[...] = forward_pair(
        pair,
        tail_query_ref[...],
        jnp.concatenate([query, tail_query_ref[...]]),
        jnp.concatenate([value, tail_value_ref[...]]),
        cotangent[GROUP:],
        out_ref,
    )


def group_spec(offset=0):
    return pl.BlockSpec((GROUP, 2 * DH), lambda p, r: (r, p + offset))


def stat_spec():
    return pl.BlockSpec((GROUP, LANES), lambda p, r: (r, p))


def forward_own(table, arrived, tail):
    slots, width = arrived.shape
    wide = width // 6
    rows = 2 * GROUP
    array = jax.ShapeDtypeStruct((rows, width // 3), jnp.bfloat16)
    return pl.pallas_call(
        own_body,
        grid=(2, 2),
        in_specs=[pl.BlockSpec((LANES, LANES), lambda p, r: (0, 0))]
        + [pl.BlockSpec((slots, wide), lambda p, r, k=k: (0, p + 2 * k)) for k in range(3)]
        + [group_spec(), group_spec(2)],
        out_specs=[group_spec()] * 5 + [stat_spec()],
        out_shape=[array] * 4
        + [
            jax.ShapeDtypeStruct((rows, width // 3), jnp.bfloat16),
            jax.ShapeDtypeStruct((rows, 2 * LANES), jnp.float32),
        ],
        scratch_shapes=[pltpu.VMEM((2, 2 * GROUP, slots), jnp.bfloat16)],
        compiler_params=params(),
        cost_estimate=cost(5e9, 1e7, 8 * GROUP * 512),
        name="forward_own",
    )(table, arrived, arrived, arrived, tail, tail)


def edge_body(
    table_ref,
    query_ref,
    value_ref,
    cotangent_ref,
    prior_ref,
    second_stat_ref,
    out_ref,
    stats_ref,
    three,
    prior,
    second_stat,
    staged,
    both,
    load,
    store,
):
    each = [pl.ds(hash_round * GROUP, GROUP) for hash_round in range(2)]
    arriving = [
        started(
            [source.at[at] for source in (query_ref, prior_ref, value_ref, cotangent_ref)],
            [three.at[0, at], prior.at[at], three.at[1, at], three.at[2, at]],
            load,
            4 * hash_round,
        )
        for hash_round, at in enumerate(each)
    ]
    arriving[1] += started([second_stat_ref], [second_stat], load, 8)
    place_row = table_row(table_ref, PLACE, PLACE_ROWS)
    arrival_cols = table_cols(table_ref, ARRIVAL3, SLOT_ROWS)
    width = staged.shape[1]
    leaving = []
    for hash_round in range(2):
        kept = slice(hash_round * GROUP, (hash_round + 1) * GROUP)
        at = each[hash_round]
        for copy in arriving[hash_round]:
            copy.wait()
        stat = 0.0
        for pair in range(2):
            columns = slice(pair * 2 * DH, (pair + 1) * 2 * DH)
            values_at = slice(width + pair * 2 * DH, width + (pair + 1) * 2 * DH)
            query = three[0, kept, columns]
            stat = stat + forward_pair(
                pair,
                query,
                jnp.concatenate([prior[kept, columns], query]),
                jnp.concatenate([prior[kept, values_at], three[1, kept, columns]]),
                three[2, kept, columns],
                staged.at[at, pl.ds(pair * 2 * DH, 2 * DH)],
            )
        leaving += started([staged.at[at]], [out_ref.at[at]], store, hash_round)
        both[2 * hash_round * GROUP : (2 * hash_round + 1) * GROUP] = stat
    for hash_round in range(2):
        kept = slice(hash_round * GROUP, (hash_round + 1) * GROUP)
        both[(2 * hash_round + 1) * GROUP : (2 * hash_round + 2) * GROUP] = (
            second_stat[kept, :LANES] + second_stat[kept, LANES:]
        )
    rows = 4 * GROUP
    piece = iota((rows, LANES), 1) // (PIECES * STAT)
    first, second, third = pieces_of(both[...])
    nothing = jnp.zeros((rows, LANES), jnp.bfloat16)
    stats = jnp.where(
        piece == 0,
        first,
        jnp.where(piece == 1, second, jnp.where(piece == 2, third, nothing)),
    )
    third_slots = stats_ref.shape[0]
    lane_third = (iota((third_slots, LANES), 1) % (3 * STAT)) // STAT
    result = jnp.zeros((third_slots, LANES), jnp.float32)
    for third in range(3):
        span = slice((0, 0, rows // 2)[third], (rows // 2, rows, rows)[third])
        back = match_cols(arrival_cols[4 * third : 4 * third + 4], place_row[:, span])
        result = jnp.where(lane_third == third, dot(back, stats[span]), result)
    stats_ref[...] = result
    for copy in leaving:
        copy.wait()


def forward_edge(table, query, value, cotangent, prior_tail, second_stat):
    rows, width = query.shape
    third_slots = SLOT_ROWS * LANES // 3
    return pl.pallas_call(
        edge_body,
        in_specs=[table_spec()] + anywhere(5),
        out_specs=anywhere(1) + [pl.BlockSpec(memory_space=pltpu.VMEM)],
        out_shape=[
            jax.ShapeDtypeStruct((rows, width), jnp.bfloat16),
            jax.ShapeDtypeStruct((third_slots, LANES), jnp.float32),
        ],
        scratch_shapes=[
            pltpu.VMEM((3, rows, width), jnp.bfloat16),
            pltpu.VMEM((rows, 2 * width), jnp.bfloat16),
            pltpu.VMEM((rows, 2 * LANES), jnp.float32),
            pltpu.VMEM((rows, width), jnp.bfloat16),
            pltpu.VMEM((2 * rows, LANES), jnp.float32),
            pltpu.SemaphoreType.DMA((9,)),
            pltpu.SemaphoreType.DMA((2,)),
        ],
        compiler_params=params(59),
        cost_estimate=cost(2e9, 4e6, 8 * GROUP * 512),
        name="forward_edge",
    )(table, query, value, cotangent, prior_tail, second_stat)


def gather_stats(codes_row, slot_cols, stats):
    narrow = stats.astype(jnp.bfloat16)
    half = codes_row.shape[1] // 2
    sums = [0.0, 0.0]
    for third in range(3):
        for each in ((0,), (0, 1), (1,))[third]:
            codes = codes_row[:, each * half : (each + 1) * half]
            chosen = match_cols(slot_cols[4 * third : 4 * third + 4], codes)
            found = dot(narrow, chosen, 0, 0)
            for piece in range(PIECES):
                at = piece * PIECES * STAT + third * STAT
                sums[each] = sums[each] + found[at : at + STAT]
    return jnp.concatenate(sums, axis=1)


def found_at_tokens(tokens, table_ref, stats):
    slot_cols = table_cols(table_ref, SEND3, SLOT_ROWS)
    found = gather_stats(iota((1, 2 * tokens), 1), slot_cols, stats)
    lse_first, lse_second = found[:4, :tokens], found[:4, tokens:]
    top = jnp.maximum(lse_first, lse_second)
    total = top + jnp.log(jnp.exp(lse_first - top) + jnp.exp(lse_second - top))
    shares = jnp.exp(lse_first - total), jnp.exp(lse_second - total)
    delta = found[4:, :tokens] * shares[0] + found[4:, tokens:] * shares[1]
    return slot_cols, total, delta, shares


def total_body(tokens, table_ref, arrived_ref, out_ref):
    slot_cols, total, delta, _ = found_at_tokens(tokens, table_ref, arrived_ref[...])
    stat = jnp.concatenate([total, delta])
    first, second, third_piece = [member.astype(jnp.float32) for member in pieces_of(stat)]
    spare = jnp.zeros((LANES - 9 * STAT, tokens), jnp.float32)
    table = jnp.concatenate(
        [first] * 3 + [second] * 3 + [third_piece] * 3 + [spare]
    ).astype(jnp.bfloat16)
    third_slots = arrived_ref.shape[0]
    lane_third = (iota((third_slots, LANES), 1) % (3 * STAT)) // STAT
    result = jnp.zeros((third_slots, LANES), jnp.float32)
    for third in range(3):
        codes = slot_cols[4 * third : 4 * third + 4]
        cols = [jnp.where(code >= tokens, code - tokens, code) for code in codes]
        chosen = match_cols(cols, iota((LANES, tokens), 1))
        result = jnp.where(lane_third == third, dot(chosen, table, 1, 1), result)
    owners = third_slots // STAT
    by_owner = result.reshape(owners, STAT, LANES)
    out_ref[:, :STAT, :] = by_owner
    above = jnp.concatenate([by_owner[1:], by_owner[:1]])
    below = jnp.concatenate([by_owner[owners - 1 :], by_owner[: owners - 1]])
    half = table_ref[HALF : HALF + 1, :]
    out_ref[:, STAT:, :] = jnp.where(half[None] == 0, above, below)


def total_stats(table, arrived, tokens):
    owners = arrived.shape[0] // STAT
    return pl.pallas_call(
        functools.partial(total_body, tokens),
        out_shape=jax.ShapeDtypeStruct((owners, 2 * STAT, LANES), jnp.float32),
        compiler_params=params(24),
        cost_estimate=cost(2 * 1536 * 1536 * LANES, 1 << 20),
        name="total_stats",
    )(table, arrived)


def prepare_body(tokens, table_ref, arrived_ref, first_ref, second_ref, payload_ref, share_ref):
    @pl.when(pl.program_id(0) == 0)
    def _():
        shares = found_at_tokens(tokens, table_ref, arrived_ref[...])[3]
        spare = jnp.zeros((LANES - STAT, tokens), jnp.float32)
        share_ref[...] = jnp.concatenate([*shares, spare]).T

    back = match_cols(
        table_cols(table_ref, ARRIVAL, SLOT_ROWS), table_row(table_ref, PLACE, PLACE_ROWS)
    )
    rows = [first_ref[:GROUP], second_ref[:GROUP], first_ref[GROUP:], second_ref[GROUP:]]
    payload_ref[...] = dot(back, jnp.concatenate(rows)).astype(jnp.bfloat16)


def prepare(table, home_stats, outs, tokens):
    slots = SLOT_ROWS * LANES
    rows, width = outs[0].shape
    wide = width // 2
    return pl.pallas_call(
        functools.partial(prepare_body, tokens),
        grid=(2,),
        in_specs=[
            table_spec(),
            pl.BlockSpec(home_stats.shape, lambda i: (0, 0)),
            pl.BlockSpec((rows, wide), lambda i: (0, i)),
            pl.BlockSpec((rows, wide), lambda i: (0, i)),
        ],
        out_specs=[
            pl.BlockSpec((slots, wide), lambda i: (0, i)),
            pl.BlockSpec((tokens, LANES), lambda i: (0, 0)),
        ],
        out_shape=[
            jax.ShapeDtypeStruct((slots, 3 * width), jnp.bfloat16),
            jax.ShapeDtypeStruct((tokens, LANES), jnp.float32),
        ],
        compiler_params=params(62),
        cost_estimate=cost(2e9, 1e7),
        name="prepare_outputs",
    )(table, home_stats, *outs)


def backward_tile(query, upstream, keys, values, masked, total_row, delta_row):
    scores = dot(keys, query, 1, 1)
    if masked is not None:
        low, high = scores[:LANES], scores[LANES:]
        low = jnp.concatenate(
            [jnp.where(masked, NEG_SELF, low[:, :LANES]), low[:, LANES:]], axis=1
        )
        high = jnp.concatenate(
            [
                high[:, :LANES],
                jnp.where(masked, NEG_SELF, high[:, LANES : 2 * LANES]),
                high[:, 2 * LANES :],
            ],
            axis=1,
        )
        scores = jnp.concatenate([low, high])
    probs = jnp.exp(scores - total_row)
    dots = dot(values, upstream, 1, 1)
    slopes = (probs * (dots - delta_row)).astype(jnp.bfloat16)
    return probs.astype(jnp.bfloat16), slopes


def backward_heads(pair, stat, edge_stat, refs, hash_round, shaped):
    heads, tail, tail_cotangent, prior, nexts = refs
    kept = pl.ds(hash_round * GROUP, GROUP)
    own = iota((LANES, LANES), 0) == iota((LANES, LANES), 1)
    width = tail.shape[1] // 2
    for local in range(2):
        head = pair * 2 + local
        columns = pl.ds(head * DH, DH)
        values_at = pl.ds(width + head * DH, DH)
        total_row, delta_row = stat[head : head + 1], stat[head + 4 : head + 5]
        edge_total, edge_delta = edge_stat[head : head + 1], edge_stat[head + 4 : head + 5]
        raw = jnp.concatenate([heads[0][kept, columns], tail[kept, columns]])
        values = jnp.concatenate([heads[1][kept, columns], tail[kept, values_at]])
        upstream = jnp.concatenate([heads[2][kept, columns], tail_cotangent[kept, columns]])
        units, inverse = unit_rows(raw)
        keys = units.astype(jnp.bfloat16)
        prior_keys = unit_rows(prior[kept, columns])[0].astype(jnp.bfloat16)
        _, prior_slopes = backward_tile(
            raw[:GROUP],
            upstream[:GROUP],
            prior_keys,
            prior[kept, values_at],
            None,
            total_row[:, :GROUP],
            delta_row[:, :GROUP],
        )
        first_probs, first_slopes = backward_tile(
            raw, upstream, keys[:GROUP], values[:GROUP], own, total_row, delta_row
        )
        second_raw = jnp.concatenate([raw[GROUP:], nexts[0][kept, columns]])
        second_upstream = jnp.concatenate([upstream[GROUP:], nexts[1][kept, columns]])
        second_probs, second_slopes = backward_tile(
            second_raw,
            second_upstream,
            keys[GROUP:],
            values[GROUP:],
            own,
            jnp.concatenate([total_row[:, GROUP:], edge_total], axis=1),
            jnp.concatenate([delta_row[:, GROUP:], edge_delta], axis=1),
        )
        query_slope = jnp.concatenate(
            [
                dot(
                    jnp.concatenate([prior_keys, keys[:GROUP]]),
                    jnp.concatenate([prior_slopes, first_slopes[:, :GROUP]]),
                    0,
                    0,
                ).T,
                dot(
                    keys,
                    jnp.concatenate([first_slopes[:, GROUP:], second_slopes[:, :GROUP]]),
                    0,
                    0,
                ).T,
            ]
        )
        unit_slope = jnp.concatenate([dot(first_slopes, raw), dot(second_slopes, second_raw)])
        value_slope = jnp.concatenate(
            [dot(first_probs, upstream), dot(second_probs, second_upstream)]
        )
        key_slope = inverse * (
            unit_slope - units * jnp.sum(units * unit_slope, -1, keepdims=True)
        )
        shaped[hash_round, :, local * DH : (local + 1) * DH] = (query_slope + key_slope).astype(
            jnp.bfloat16
        )
        shaped[hash_round, :, (2 + local) * DH : (3 + local) * DH] = value_slope.astype(
            jnp.bfloat16
        )


def backward_body(
    table_ref,
    next_table_ref,
    stats_ref,
    head_query_ref,
    head_value_ref,
    head_cotangent_ref,
    tail_ref,
    tail_cotangent_ref,
    prior_ref,
    next_query_ref,
    next_cotangent_ref,
    _,
    payload_ref,
    stats,
    six,
    double,
    shaped,
    staged,
    load,
    store,
):
    rows = PLACE_ROWS * LANES
    per_round = rows // 2
    sources = [
        stats_ref,
        head_query_ref,
        head_value_ref,
        head_cotangent_ref,
        tail_cotangent_ref,
        next_query_ref,
        next_cotangent_ref,
        tail_ref,
        prior_ref,
    ]
    targets = [stats] + [six.at[i] for i in range(6)] + [double.at[i] for i in range(2)]
    arriving = started(sources, targets, load)
    place_row = table_row(table_ref, PLACE, PLACE_ROWS)
    next_places = table_row(next_table_ref, PLACE, PLACE_ROWS)
    next_row = jnp.concatenate(
        [next_places[:, each * per_round : each * per_round + GROUP] for each in range(2)], axis=1
    )
    back = [
        match_cols(
            table_cols(table_ref, (FIRST16, LAST16)[each], PART_ROWS),
            place_row[:, each * per_round : (each + 1) * per_round],
        )
        for each in range(2)
    ]
    arriving[0].wait()
    own_stats = stats[:, :STAT, :].reshape(-1, LANES)
    next_stats = stats[:, STAT:, :].reshape(-1, LANES)
    found = gather_stats(place_row, table_cols(table_ref, ARRIVAL3, SLOT_ROWS), own_stats)
    edge = gather_stats(next_row, table_cols(next_table_ref, ARRIVAL3, SLOT_ROWS), next_stats)
    for copy in arriving[1:]:
        copy.wait()
    refs = (
        (six.at[0], six.at[1], six.at[2]),
        double.at[0],
        six.at[3],
        double.at[1],
        (six.at[4], six.at[5]),
    )
    leaving = []
    width = shaped.shape[2]
    for pair in range(2):
        for hash_round in range(2):
            backward_heads(
                pair,
                found[:, hash_round * per_round : (hash_round + 1) * per_round],
                edge[:, hash_round * GROUP : (hash_round + 1) * GROUP],
                refs,
                hash_round,
                shaped,
            )
        chunks = 2
        for chunk in range(chunks):
            kept = slice(chunk * 1024 // chunks, (chunk + 1) * 1024 // chunks)
            first = dot(back[0][kept], shaped[0]).reshape(-1, 2, STAT, width)
            second = dot(back[1][kept], shaped[1]).reshape(-1, 2, STAT, width)
            whole = jnp.concatenate(
                [first[:, :1], first[:, 1:] + second[:, :1], second[:, 1:]], axis=1
            ).reshape(-1, width)
            count = whole.shape[0]
            at = pl.ds(chunk * count, count)
            staged[pair, at] = whole.astype(jnp.bfloat16)
            leaving += started(
                [staged.at[pair, at]],
                [payload_ref.at[at, pl.ds((pair + 1) * width, width)]],
                store,
                pair * chunks + chunk,
            )
    for copy in leaving:
        copy.wait()


def backward(table, next_table, stats, heads, tail, tail_cotangent, prior_tail, nexts, payload):
    slots = SLOT_ROWS * LANES
    rows, width = heads[0].shape
    return pl.pallas_call(
        backward_body,
        in_specs=[table_spec(), pl.BlockSpec(next_table.shape, lambda *_: (0, 0))] + anywhere(10),
        out_specs=anywhere(1)[0],
        out_shape=jax.ShapeDtypeStruct((slots, 3 * width), jnp.bfloat16),
        input_output_aliases={11: 0},
        scratch_shapes=[
            pltpu.VMEM(stats.shape, jnp.float32),
            pltpu.VMEM((6, rows, width), jnp.bfloat16),
            pltpu.VMEM((2, rows, 2 * width), jnp.bfloat16),
            pltpu.VMEM((2, 2 * GROUP, width), jnp.bfloat16),
            pltpu.VMEM((2, slots, width), jnp.bfloat16),
            pltpu.SemaphoreType.DMA((9,)),
            pltpu.SemaphoreType.DMA((4,)),
        ],
        compiler_params=params(57),
        cost_estimate=cost(8e9, 1.5e7, 3e6),
        name="backward",
    )(table, next_table, stats, *heads, tail, tail_cotangent, prior_tail, *nexts, payload)


def combine_body(
    table_ref,
    share_ref,
    arrived_ref,
    out_ref,
    first_ref,
    second_ref,
    staged,
    chosen,
    store,
):
    parts, tokens, wide = staged.shape
    token = iota((tokens, 1), 0)
    code = table_row(table_ref, SEND_CODE, SLOT_ROWS)
    chosen[0] = match(token, code)
    chosen[1] = match(token + tokens, code)
    chosen[2] = match(token, table_row(table_ref, SEND, SLOT_ROWS))
    width = parts * wide // 3
    leaving = []
    for half in range(2):
        kept = slice(half * tokens // 2, (half + 1) * tokens // 2)
        at = pl.ds(half * tokens // 2, tokens // 2)
        slopes = dot(chosen[2, kept], arrived_ref[:, width:]).astype(jnp.bfloat16)
        for place in range(4):
            staged[2 + place, kept] = slopes[:, place * wide : (place + 1) * wide]
            leaving += started(
                [staged.at[2 + place, at]],
                [(first_ref, second_ref)[place % 2].at[at, pl.ds((place // 2) * wide, wide)]],
                store,
                half * parts + 2 + place,
            )
        found = 0.0
        for each in range(2):
            share = jnp.concatenate(
                [
                    jnp.broadcast_to(
                        share_ref[kept, 4 * each + head : 4 * each + head + 1], (tokens // 2, DH)
                    )
                    for head in range(4)
                ],
                axis=1,
            )
            found = found + share * dot(chosen[each, kept], arrived_ref[:, :width])
        found = found.astype(jnp.bfloat16)
        for place in range(2):
            staged[place, kept] = found[:, place * wide : (place + 1) * wide]
            leaving += started(
                [staged.at[place, at]],
                [out_ref.at[at, pl.ds(place * wide, wide)]],
                store,
                half * parts + place,
            )
    for copy in leaving:
        copy.wait()


def combine(table, shares, arrived, tokens):
    slots, width = arrived.shape
    wide = width // 6
    return pl.pallas_call(
        combine_body,
        in_specs=[table_spec(), pl.BlockSpec(shares.shape, lambda *_: (0, 0))]
        + [pl.BlockSpec(memory_space=pltpu.VMEM)],
        out_specs=anywhere(3),
        out_shape=[jax.ShapeDtypeStruct((tokens, 2 * wide), jnp.bfloat16)] * 3,
        scratch_shapes=[
            pltpu.VMEM((6, tokens, wide), jnp.bfloat16),
            pltpu.VMEM((3, tokens, slots), jnp.bfloat16),
            pltpu.SemaphoreType.DMA((12,)),
        ],
        compiler_params=params(40),
        cost_estimate=cost(2 * slots * tokens * width, 2 * (slots + tokens) * width),
        name="combine_rows",
    )(table, shares, arrived)


def per_device(query_key, value, attended_cotangent, send_rows, arrival_count, receive_slot):
    tokens, row_width = query_key.shape
    rounds = send_rows.shape[0]
    owners = lax.axis_size("seq")
    capacity = send_rows.shape[1] // owners
    per_owner = rounds * capacity
    slots = owners * per_owner

    code = (tokens * jnp.arange(rounds, dtype=jnp.int32))[:, None]
    half = lax.axis_index("head")

    def by_owner(table):
        return table.reshape(rounds, owners, capacity).transpose(1, 0, 2).reshape(owners, per_owner)

    def by_third(codes):
        return codes.reshape(owners, 3, STAT).transpose(1, 0, 2)

    def sent(packed):
        return exchange(packed.reshape(owners, per_owner, -1)).reshape(slots, -1)

    blocks = send_rows.reshape(rounds, owners, capacity)
    send_rows = jnp.where(half == 0, blocks, blocks[:, ::-1]).reshape(rounds, -1)
    send = by_owner(send_rows)
    send_blocks = jnp.pad(send.reshape(-1, LANES), ((0, 4), (0, 0)))
    packed = pack(send_blocks, query_key, value, attended_cotangent)

    within = jnp.arange(capacity, dtype=jnp.int32)

    def arrivals(counts):
        start = jnp.cumsum(counts, axis=1) - counts + code
        codes = jnp.where(within < counts[:, :, None], start[:, :, None] + within, -1)
        return by_owner(codes)

    tables = to_place(jnp.concatenate([arrival_count, receive_slot], axis=1))
    arrival = arrivals(tables[:, :owners])
    place = tables[:, owners:] + code

    def half_blocks(codes, first):
        return codes[:, first : first + 2 * STAT]

    members = [
        (ARRIVAL3, by_third(arrival)),
        (PLACE, place),
        (ARRIVAL, arrival),
        (SEND, send),
        (SEND3, by_third(by_owner(send_rows + code))),
        (HALF, jnp.full((1, LANES), half, jnp.int32)),
        (FIRST16, half_blocks(arrival, 0)),
        (LAST16, half_blocks(arrival, STAT)),
        (SEND_CODE, by_owner(send_rows + code)),
    ]
    rows = [codes.reshape(-1, LANES) for _, codes in members]
    assert [at for at, _ in members] == [sum(map(len, rows[:i])) for i in range(len(rows))]
    table = jnp.concatenate(rows)
    table = jnp.pad(table, ((0, LANES - len(table)), (0, 0)), constant_values=-1)

    arrived, table = lax.optimization_barrier((sent(packed), table))
    tail = sort_tail(table, arrived, 2 * row_width)
    prior_tail = to_next(tail)
    head_query, head_value, head_cotangent, tail_cotangent, out_second, stat_second = forward_own(
        table, arrived, tail
    )
    out_first, stats = forward_edge(
        table, head_query, head_value, head_cotangent, prior_tail, stat_second
    )
    shared, stats = lax.optimization_barrier((table[:SHARED_ROWS], stats))
    next_table = to_prior(shared)
    next_query = to_prior(head_query)
    next_cotangent = to_prior(head_cotangent)
    home_stats = exchange(stats.reshape(owners, STAT, LANES)).reshape(-1, LANES)
    totals = exchange(total_stats(table, home_stats, tokens))
    payload, shares = prepare(table, home_stats, (out_first, out_second), tokens)
    payload = backward(
        table,
        next_table,
        totals,
        (head_query, head_value, head_cotangent),
        tail,
        tail_cotangent,
        prior_tail,
        (next_query, next_cotangent),
        payload,
    )
    return tuple(combine(table, shares, sent(payload), tokens))


def solution(mesh):
    in_specs = (
        P("seq", "head"),
        P("seq", "head"),
        P("seq", "head"),
        P(None, "seq"),
        P(None, "seq"),
        P(None, "seq"),
    )
    out_specs = (P("seq", "head"), P("seq", "head"), P("seq", "head"))
    return jax.shard_map(
        per_device, mesh=mesh, in_specs=in_specs, out_specs=out_specs, check_vma=False
    )
```

```python
import functools

import jax
import jax.numpy as jnp
from jax import lax
from jax.experimental import pallas as pl
from jax.experimental.pallas import tpu as pltpu
from jax.sharding import PartitionSpec as P

DH = 128
GROUP = 256
NEG_SELF = -100000.0
EPS_KEY = 1e-06
LANES = 128
STAT = 8
PIECES = 3
MIB = 1 << 20


def dot(left, right, left_axis=1, right_axis=0):
    return lax.dot_general(
        left,
        right,
        (((left_axis,), (right_axis,)), ((), ())),
        preferred_element_type=jnp.float32,
    )


def params(mib=62):
    return pltpu.CompilerParams(vmem_limit_bytes=mib * MIB)


def cost(flops, moved, exps=0):
    return pl.CostEstimate(flops=int(flops), bytes_accessed=int(moved), transcendentals=int(exps))


def routed(block, route_of):
    owners, halves = lax.axis_size("seq"), lax.axis_size("head")
    route = [
        (i * halves + half, route_of(i, half, owners) * halves + half)
        for i in range(owners)
        for half in range(halves)
    ]
    return lax.ppermute(block, ("seq", "head"), route)


def to_next(block):
    return routed(block, lambda i, half, n: (i + (1 if half == 0 else -1)) % n)


def to_prior(block):
    return routed(block, lambda i, half, n: (i - (1 if half == 0 else -1)) % n)


def to_place_prior(block):
    return routed(block, lambda i, half, n: (i - 1) % n if half == 0 else n - 1 - (i - 1) % n)


def to_place(block):
    return routed(block, lambda i, half, n: i if half == 0 else n - 1 - i)


def exchange(block):
    return lax.all_to_all(block, "seq", split_axis=0, concat_axis=0, tiled=True)


def match(left, right):
    return jnp.where(left == right, 1.0, 0.0).astype(jnp.bfloat16)


ARRIVAL3, PLACE, ARRIVAL, SEND, SEND3, HALF, FIRST16, LAST16, SEND_CODE = 0, 12, 20, 32, 44, 56, 57, 65, 73
SLOT_ROWS, PLACE_ROWS, PART_ROWS = 12, 8, 8
SHARED_ROWS = 24


def table_row(table_ref, start, count):
    return jnp.concatenate([table_ref[start + i : start + i + 1, :] for i in range(count)], axis=1)


def table_cols(table_ref, start, count):
    turned = table_ref[...].T
    return [turned[:, start + i : start + i + 1] for i in range(count)]


def match_cols(cols, row):
    return jnp.concatenate([match(col, row) for col in cols])


def anywhere(count):
    return [pl.BlockSpec(memory_space=pl.ANY) for _ in range(count)]


def table_spec():
    return pl.BlockSpec((LANES, LANES), lambda *_: (0, 0))


def started(sources, targets, sems, first=0):
    copies = [
        pltpu.make_async_copy(source, target, sems.at[first + i])
        for i, (source, target) in enumerate(zip(sources, targets))
    ]
    for copy in copies:
        copy.start()
    return copies


def iota(shape, axis):
    return lax.broadcasted_iota(jnp.int32, shape, axis)


def pieces_of(wide):
    first = wide.astype(jnp.bfloat16)
    rest = wide - first.astype(jnp.float32)
    second = rest.astype(jnp.bfloat16)
    third = (rest - second.astype(jnp.float32)).astype(jnp.bfloat16)
    return first, second, third


def unit_rows(raw_rows):
    wide = raw_rows.astype(jnp.float32)
    inverse = lax.rsqrt(jnp.sum(wide * wide, -1, keepdims=True) + EPS_KEY)
    return wide * inverse, inverse


def pack_body(index_ref, *refs):
    sources, out_ref, held, staged, chosen, load, store = refs[:3], *refs[3:]
    tokens, width = sources[0].shape
    arriving = started(sources, [held.at[i] for i in range(3)], load)
    spare = jnp.zeros((LANES - SLOT_ROWS, LANES), jnp.int32)
    turned = jnp.concatenate([index_ref[...], spare]).T
    chosen[...] = match_cols(
        [turned[:, i : i + 1] for i in range(SLOT_ROWS)], iota((LANES, tokens), 1)
    )
    steps = 4
    block = chosen.shape[0] // steps
    leaving = []
    for step in range(steps):
        rows = slice(step * block, (step + 1) * block)
        for place in range(3):
            if step == 0:
                arriving[place].wait()
            staged[rows, place * width : (place + 1) * width] = dot(
                chosen[rows], held[place]
            ).astype(jnp.bfloat16)
        leaving += started(
            [staged.at[pl.ds(step * block, block)]],
            [out_ref.at[pl.ds(step * block, block)]],
            store,
            step,
        )
    for copy in leaving:
        copy.wait()


def pack(index, *sources):
    slots = SLOT_ROWS * LANES
    tokens, width = sources[0].shape
    total = width * len(sources)
    return pl.pallas_call(
        pack_body,
        in_specs=[pl.BlockSpec(index.shape, lambda *_: (0, 0))] + anywhere(3),
        out_specs=anywhere(1)[0],
        out_shape=jax.ShapeDtypeStruct((slots, total), jnp.bfloat16),
        scratch_shapes=[
            pltpu.VMEM((3, tokens, width), jnp.bfloat16),
            pltpu.VMEM((slots, total), jnp.bfloat16),
            pltpu.VMEM((slots, tokens), jnp.bfloat16),
            pltpu.SemaphoreType.DMA((3,)),
            pltpu.SemaphoreType.DMA((4,)),
        ],
        compiler_params=params(),
        cost_estimate=cost(2 * slots * tokens * total, 2 * (slots + tokens) * total),
        name="pack_rows",
    )(index, *sources)


def place_cols(table_ref, group):
    cols = table_cols(table_ref, PLACE, PLACE_ROWS)
    each = GROUP // LANES
    first, second = group * each, PLACE_ROWS // 2 + group * each
    return cols[first : first + each], cols[second : second + each]


def tail_body(table_ref, arrived_ref, tail_ref, held, staged, chosen, load, store):
    width = held.shape[1]
    arriving = started([arrived_ref.at[:, pl.ds(0, width)]], [held], load)
    first, second = place_cols(table_ref, 1)
    row = table_row(table_ref, ARRIVAL, SLOT_ROWS)
    for i, col in enumerate(first + second):
        chosen[i * LANES : (i + 1) * LANES] = match(col, row)
    arriving[0].wait()
    leaving = []
    for i in range(2):
        staged[i * GROUP : (i + 1) * GROUP] = dot(
            chosen[i * GROUP : (i + 1) * GROUP], held[...]
        ).astype(jnp.bfloat16)
        at = pl.ds(i * GROUP, GROUP)
        leaving += started([staged.at[at]], [tail_ref.at[at]], store, i)
    for copy in leaving:
        copy.wait()


def sort_tail(table, arrived, width):
    slots = arrived.shape[0]
    wide = width // 4
    return pl.pallas_call(
        tail_body,
        in_specs=[table_spec()] + anywhere(1),
        out_specs=anywhere(1)[0],
        out_shape=jax.ShapeDtypeStruct((2 * GROUP, width), jnp.bfloat16),
        scratch_shapes=[
            pltpu.VMEM((slots, width), jnp.bfloat16),
            pltpu.VMEM((2 * GROUP, width), jnp.bfloat16),
            pltpu.VMEM((2 * GROUP, slots), jnp.bfloat16),
            pltpu.SemaphoreType.DMA((4,)),
            pltpu.SemaphoreType.DMA((4,)),
        ],
        compiler_params=params(),
        cost_estimate=cost(4 * slots * GROUP * width, 2 * (slots + 2 * GROUP) * width),
        name="sort_tail",
    )(table, arrived)


def forward_tile(query, keys, values):
    scores = dot(query, keys, 1, 1)
    own = iota((GROUP, 2 * GROUP), 1) == iota((GROUP, 2 * GROUP), 0) + GROUP
    scores = jnp.where(own, NEG_SELF, scores)
    top = jnp.max(scores, -1, keepdims=True)
    raised = jnp.exp(scores - top)
    total = jnp.sum(raised, -1, keepdims=True)
    weights = (raised * (1.0 / total)).astype(jnp.bfloat16)
    return dot(weights, values), top + jnp.log(total)


def forward_pair(pair, query, raw, values, cotangent, out_ref):
    lane = iota((GROUP, LANES), 1) % STAT
    stat = jnp.zeros((GROUP, LANES), jnp.float32)
    for local in range(2):
        columns = slice(local * DH, (local + 1) * DH)
        keys = unit_rows(raw[:, columns])[0].astype(jnp.bfloat16)
        partial, lse = forward_tile(query[:, columns], keys, values[:, columns])
        out_ref[:, columns] = partial.astype(jnp.bfloat16)
        delta = jnp.sum(partial * cotangent[:, columns].astype(jnp.float32), -1, keepdims=True)
        head = pair * 2 + local
        stat = jnp.where(lane == head, lse, jnp.where(lane == head + 4, delta, stat))
    return stat


def own_body(
    table_ref,
    arrived_query_ref,
    arrived_value_ref,
    arrived_cotangent_ref,
    tail_query_ref,
    tail_value_ref,
    head_query_ref,
    head_value_ref,
    head_cotangent_ref,
    tail_cotangent_ref,
    out_ref,
    stat_ref,
    chosen,
):
    pair = pl.program_id(0)
    hash_round = pl.program_id(1)

    @pl.when((pair == 0) & (hash_round == 0))
    def _():
        row = table_row(table_ref, ARRIVAL, SLOT_ROWS)
        heads, tails = place_cols(table_ref, 0), place_cols(table_ref, 1)
        for each in range(2):
            chosen[each] = match_cols(heads[each] + tails[each], row)

    select_head = chosen[hash_round, :GROUP]
    query = dot(select_head, arrived_query_ref[...]).astype(jnp.bfloat16)
    value = dot(select_head, arrived_value_ref[...]).astype(jnp.bfloat16)
    cotangent = dot(chosen[hash_round], arrived_cotangent_ref[...]).astype(jnp.bfloat16)
    head_query_ref[...] = query
    head_value_ref[...] = value
    head_cotangent_ref[...] = cotangent[:GROUP]
    tail_cotangent_ref[...] = cotangent[GROUP:]
    stat_ref[...] = forward_pair(
        pair,
        tail_query_ref[...],
        jnp.concatenate([query, tail_query_ref[...]]),
        jnp.concatenate([value, tail_value_ref[...]]),
        cotangent[GROUP:],
        out_ref,
    )


def group_spec(offset=0):
    return pl.BlockSpec((GROUP, 2 * DH), lambda p, r: (r, p + offset))


def stat_spec():
    return pl.BlockSpec((GROUP, LANES), lambda p, r: (r, p))


def forward_own(table, arrived, tail):
    slots, width = arrived.shape
    wide = width // 6
    rows = 2 * GROUP
    array = jax.ShapeDtypeStruct((rows, width // 3), jnp.bfloat16)
    return pl.pallas_call(
        own_body,
        grid=(2, 2),
        in_specs=[pl.BlockSpec((LANES, LANES), lambda p, r: (0, 0))]
        + [pl.BlockSpec((slots, wide), lambda p, r, k=k: (0, p + 2 * k)) for k in range(3)]
        + [group_spec(), group_spec(2)],
        out_specs=[group_spec()] * 5 + [stat_spec()],
        out_shape=[array] * 4
        + [
            jax.ShapeDtypeStruct((rows, width // 3), jnp.bfloat16),
            jax.ShapeDtypeStruct((rows, 2 * LANES), jnp.float32),
        ],
        scratch_shapes=[pltpu.VMEM((2, 2 * GROUP, slots), jnp.bfloat16)],
        compiler_params=params(),
        cost_estimate=cost(5e9, 1e7, 8 * GROUP * 512),
        name="forward_own",
    )(table, arrived, arrived, arrived, tail, tail)


def edge_body(
    table_ref,
    query_ref,
    value_ref,
    cotangent_ref,
    prior_ref,
    second_stat_ref,
    out_ref,
    stats_ref,
    three,
    prior,
    second_stat,
    staged,
    both,
    load,
    store,
):
    each = [pl.ds(hash_round * GROUP, GROUP) for hash_round in range(2)]
    arriving = [
        started(
            [source.at[at] for source in (query_ref, prior_ref, value_ref, cotangent_ref)],
            [three.at[0, at], prior.at[at], three.at[1, at], three.at[2, at]],
            load,
            4 * hash_round,
        )
        for hash_round, at in enumerate(each)
    ]
    arriving[1] += started([second_stat_ref], [second_stat], load, 8)
    place_row = table_row(table_ref, PLACE, PLACE_ROWS)
    arrival_cols = table_cols(table_ref, ARRIVAL3, SLOT_ROWS)
    width = staged.shape[1]
    leaving = []
    for hash_round in range(2):
        kept = slice(hash_round * GROUP, (hash_round + 1) * GROUP)
        at = each[hash_round]
        for copy in arriving[hash_round]:
            copy.wait()
        stat = 0.0
        for pair in range(2):
            columns = slice(pair * 2 * DH, (pair + 1) * 2 * DH)
            values_at = slice(width + pair * 2 * DH, width + (pair + 1) * 2 * DH)
            query = three[0, kept, columns]
            stat = stat + forward_pair(
                pair,
                query,
                jnp.concatenate([prior[kept, columns], query]),
                jnp.concatenate([prior[kept, values_at], three[1, kept, columns]]),
                three[2, kept, columns],
                staged.at[at, pl.ds(pair * 2 * DH, 2 * DH)],
            )
        leaving += started([staged.at[at]], [out_ref.at[at]], store, hash_round)
        both[2 * hash_round * GROUP : (2 * hash_round + 1) * GROUP] = stat
    for hash_round in range(2):
        kept = slice(hash_round * GROUP, (hash_round + 1) * GROUP)
        both[(2 * hash_round + 1) * GROUP : (2 * hash_round + 2) * GROUP] = (
            second_stat[kept, :LANES] + second_stat[kept, LANES:]
        )
    rows = 4 * GROUP
    piece = iota((rows, LANES), 1) // (PIECES * STAT)
    first, second, third = pieces_of(both[...])
    nothing = jnp.zeros((rows, LANES), jnp.bfloat16)
    stats = jnp.where(
        piece == 0,
        first,
        jnp.where(piece == 1, second, jnp.where(piece == 2, third, nothing)),
    )
    third_slots = stats_ref.shape[0]
    lane_third = (iota((third_slots, LANES), 1) % (3 * STAT)) // STAT
    result = jnp.zeros((third_slots, LANES), jnp.float32)
    for third in range(3):
        span = slice((0, 0, rows // 2)[third], (rows // 2, rows, rows)[third])
        back = match_cols(arrival_cols[4 * third : 4 * third + 4], place_row[:, span])
        result = jnp.where(lane_third == third, dot(back, stats[span]), result)
    stats_ref[...] = result
    for copy in leaving:
        copy.wait()


def forward_edge(table, query, value, cotangent, prior_tail, second_stat):
    rows, width = query.shape
    third_slots = SLOT_ROWS * LANES // 3
    return pl.pallas_call(
        edge_body,
        in_specs=[table_spec()] + anywhere(5),
        out_specs=anywhere(1) + [pl.BlockSpec(memory_space=pltpu.VMEM)],
        out_shape=[
            jax.ShapeDtypeStruct((rows, width), jnp.bfloat16),
            jax.ShapeDtypeStruct((third_slots, LANES), jnp.float32),
        ],
        scratch_shapes=[
            pltpu.VMEM((3, rows, width), jnp.bfloat16),
            pltpu.VMEM((rows, 2 * width), jnp.bfloat16),
            pltpu.VMEM((rows, 2 * LANES), jnp.float32),
            pltpu.VMEM((rows, width), jnp.bfloat16),
            pltpu.VMEM((2 * rows, LANES), jnp.float32),
            pltpu.SemaphoreType.DMA((9,)),
            pltpu.SemaphoreType.DMA((2,)),
        ],
        compiler_params=params(59),
        cost_estimate=cost(2e9, 4e6, 8 * GROUP * 512),
        name="forward_edge",
    )(table, query, value, cotangent, prior_tail, second_stat)


def gather_stats(codes_row, slot_cols, stats):
    narrow = stats.astype(jnp.bfloat16)
    half = codes_row.shape[1] // 2
    sums = [0.0, 0.0]
    for third in range(3):
        for each in ((0,), (0, 1), (1,))[third]:
            codes = codes_row[:, each * half : (each + 1) * half]
            chosen = match_cols(slot_cols[4 * third : 4 * third + 4], codes)
            found = dot(narrow, chosen, 0, 0)
            for piece in range(PIECES):
                at = piece * PIECES * STAT + third * STAT
                sums[each] = sums[each] + found[at : at + STAT]
    return jnp.concatenate(sums, axis=1)


def found_at_tokens(tokens, table_ref, stats):
    slot_cols = table_cols(table_ref, SEND3, SLOT_ROWS)
    found = gather_stats(iota((1, 2 * tokens), 1), slot_cols, stats)
    lse_first, lse_second = found[:4, :tokens], found[:4, tokens:]
    top = jnp.maximum(lse_first, lse_second)
    total = top + jnp.log(jnp.exp(lse_first - top) + jnp.exp(lse_second - top))
    shares = jnp.exp(lse_first - total), jnp.exp(lse_second - total)
    delta = found[4:, :tokens] * shares[0] + found[4:, tokens:] * shares[1]
    return slot_cols, total, delta, shares


def total_body(tokens, table_ref, arrived_ref, out_ref):
    slot_cols, total, delta, _ = found_at_tokens(tokens, table_ref, arrived_ref[...])
    stat = jnp.concatenate([total, delta])
    first, second, third_piece = [member.astype(jnp.float32) for member in pieces_of(stat)]
    spare = jnp.zeros((LANES - 9 * STAT, tokens), jnp.float32)
    table = jnp.concatenate(
        [first] * 3 + [second] * 3 + [third_piece] * 3 + [spare]
    ).astype(jnp.bfloat16)
    third_slots = arrived_ref.shape[0]
    lane_third = (iota((third_slots, LANES), 1) % (3 * STAT)) // STAT
    result = jnp.zeros((third_slots, LANES), jnp.float32)
    for third in range(3):
        codes = slot_cols[4 * third : 4 * third + 4]
        cols = [jnp.where(code >= tokens, code - tokens, code) for code in codes]
        chosen = match_cols(cols, iota((LANES, tokens), 1))
        result = jnp.where(lane_third == third, dot(chosen, table, 1, 1), result)
    owners = third_slots // STAT
    by_owner = result.reshape(owners, STAT, LANES)
    out_ref[:, :STAT, :] = by_owner
    above = jnp.concatenate([by_owner[1:], by_owner[:1]])
    below = jnp.concatenate([by_owner[owners - 1 :], by_owner[: owners - 1]])
    half = table_ref[HALF : HALF + 1, :]
    out_ref[:, STAT:, :] = jnp.where(half[None] == 0, above, below)


def total_stats(table, arrived, tokens):
    owners = arrived.shape[0] // STAT
    return pl.pallas_call(
        functools.partial(total_body, tokens),
        out_shape=jax.ShapeDtypeStruct((owners, 2 * STAT, LANES), jnp.float32),
        compiler_params=params(24),
        cost_estimate=cost(2 * 1536 * 1536 * LANES, 1 << 20),
        name="total_stats",
    )(table, arrived)


def prepare_body(tokens, table_ref, arrived_ref, first_ref, second_ref, payload_ref, share_ref):
    @pl.when(pl.program_id(0) == 0)
    def _():
        shares = found_at_tokens(tokens, table_ref, arrived_ref[...])[3]
        spare = jnp.zeros((LANES - STAT, tokens), jnp.float32)
        share_ref[...] = jnp.concatenate([*shares, spare]).T

    back = match_cols(
        table_cols(table_ref, ARRIVAL, SLOT_ROWS), table_row(table_ref, PLACE, PLACE_ROWS)
    )
    rows = [first_ref[:GROUP], second_ref[:GROUP], first_ref[GROUP:], second_ref[GROUP:]]
    payload_ref[...] = dot(back, jnp.concatenate(rows)).astype(jnp.bfloat16)


def prepare(table, home_stats, outs, tokens):
    slots = SLOT_ROWS * LANES
    rows, width = outs[0].shape
    wide = width // 2
    return pl.pallas_call(
        functools.partial(prepare_body, tokens),
        grid=(2,),
        in_specs=[
            table_spec(),
            pl.BlockSpec(home_stats.shape, lambda i: (0, 0)),
            pl.BlockSpec((rows, wide), lambda i: (0, i)),
            pl.BlockSpec((rows, wide), lambda i: (0, i)),
        ],
        out_specs=[
            pl.BlockSpec((slots, wide), lambda i: (0, i)),
            pl.BlockSpec((tokens, LANES), lambda i: (0, 0)),
        ],
        out_shape=[
            jax.ShapeDtypeStruct((slots, 3 * width), jnp.bfloat16),
            jax.ShapeDtypeStruct((tokens, LANES), jnp.float32),
        ],
        compiler_params=params(62),
        cost_estimate=cost(2e9, 1e7),
        name="prepare_outputs",
    )(table, home_stats, *outs)


def backward_tile(query, upstream, keys, values, masked, total_row, delta_row):
    scores = dot(keys, query, 1, 1)
    if masked is not None:
        low, high = scores[:LANES], scores[LANES:]
        low = jnp.concatenate(
            [jnp.where(masked, NEG_SELF, low[:, :LANES]), low[:, LANES:]], axis=1
        )
        high = jnp.concatenate(
            [
                high[:, :LANES],
                jnp.where(masked, NEG_SELF, high[:, LANES : 2 * LANES]),
                high[:, 2 * LANES :],
            ],
            axis=1,
        )
        scores = jnp.concatenate([low, high])
    probs = jnp.exp(scores - total_row)
    dots = dot(values, upstream, 1, 1)
    slopes = (probs * (dots - delta_row)).astype(jnp.bfloat16)
    return probs.astype(jnp.bfloat16), slopes


def backward_heads(pair, stat, edge_stat, refs, hash_round, shaped):
    heads, tail, tail_cotangent, prior, nexts = refs
    kept = pl.ds(hash_round * GROUP, GROUP)
    own = iota((LANES, LANES), 0) == iota((LANES, LANES), 1)
    width = tail.shape[1] // 2
    for local in range(2):
        head = pair * 2 + local
        columns = pl.ds(head * DH, DH)
        values_at = pl.ds(width + head * DH, DH)
        total_row, delta_row = stat[head : head + 1], stat[head + 4 : head + 5]
        edge_total, edge_delta = edge_stat[head : head + 1], edge_stat[head + 4 : head + 5]
        raw = jnp.concatenate([heads[0][kept, columns], tail[kept, columns]])
        values = jnp.concatenate([heads[1][kept, columns], tail[kept, values_at]])
        upstream = jnp.concatenate([heads[2][kept, columns], tail_cotangent[kept, columns]])
        units, inverse = unit_rows(raw)
        keys = units.astype(jnp.bfloat16)
        prior_keys = unit_rows(prior[kept, columns])[0].astype(jnp.bfloat16)
        _, prior_slopes = backward_tile(
            raw[:GROUP],
            upstream[:GROUP],
            prior_keys,
            prior[kept, values_at],
            None,
            total_row[:, :GROUP],
            delta_row[:, :GROUP],
        )
        first_probs, first_slopes = backward_tile(
            raw, upstream, keys[:GROUP], values[:GROUP], own, total_row, delta_row
        )
        second_raw = jnp.concatenate([raw[GROUP:], nexts[0][kept, columns]])
        second_upstream = jnp.concatenate([upstream[GROUP:], nexts[1][kept, columns]])
        second_probs, second_slopes = backward_tile(
            second_raw,
            second_upstream,
            keys[GROUP:],
            values[GROUP:],
            own,
            jnp.concatenate([total_row[:, GROUP:], edge_total], axis=1),
            jnp.concatenate([delta_row[:, GROUP:], edge_delta], axis=1),
        )
        query_slope = jnp.concatenate(
            [
                dot(
                    jnp.concatenate([prior_keys, keys[:GROUP]]),
                    jnp.concatenate([prior_slopes, first_slopes[:, :GROUP]]),
                    0,
                    0,
                ).T,
                dot(
                    keys,
                    jnp.concatenate([first_slopes[:, GROUP:], second_slopes[:, :GROUP]]),
                    0,
                    0,
                ).T,
            ]
        )
        unit_slope = jnp.concatenate([dot(first_slopes, raw), dot(second_slopes, second_raw)])
        value_slope = jnp.concatenate(
            [dot(first_probs, upstream), dot(second_probs, second_upstream)]
        )
        key_slope = inverse * (
            unit_slope - units * jnp.sum(units * unit_slope, -1, keepdims=True)
        )
        shaped[hash_round, :, local * DH : (local + 1) * DH] = (query_slope + key_slope).astype(
            jnp.bfloat16
        )
        shaped[hash_round, :, (2 + local) * DH : (3 + local) * DH] = value_slope.astype(
            jnp.bfloat16
        )


def backward_body(
    table_ref,
    next_table_ref,
    stats_ref,
    head_query_ref,
    head_value_ref,
    head_cotangent_ref,
    tail_ref,
    tail_cotangent_ref,
    prior_ref,
    next_query_ref,
    next_cotangent_ref,
    _,
    payload_ref,
    stats,
    six,
    double,
    shaped,
    staged,
    load,
    store,
):
    rows = PLACE_ROWS * LANES
    per_round = rows // 2
    sources = [
        head_query_ref,
        head_value_ref,
        head_cotangent_ref,
        tail_cotangent_ref,
        next_query_ref,
        next_cotangent_ref,
        tail_ref,
        prior_ref,
    ]
    targets = [six.at[i] for i in range(6)] + [double.at[i] for i in range(2)]
    (stats_copy,) = started([stats_ref], [stats], load)
    arriving = []
    for each in range(2):
        at = pl.ds(each * GROUP, GROUP)
        arriving.append(
            started(
                [source.at[at] for source in sources],
                [target.at[at] for target in targets],
                load,
                1 + each * len(sources),
            )
        )
    place_row = table_row(table_ref, PLACE, PLACE_ROWS)
    next_places = table_row(next_table_ref, PLACE, PLACE_ROWS)
    next_row = jnp.concatenate(
        [next_places[:, each * per_round : each * per_round + GROUP] for each in range(2)], axis=1
    )
    back = [
        match_cols(
            table_cols(table_ref, (FIRST16, LAST16)[each], PART_ROWS),
            place_row[:, each * per_round : (each + 1) * per_round],
        )
        for each in range(2)
    ]
    stats_copy.wait()
    own_stats = stats[:, :STAT, :].reshape(-1, LANES)
    next_stats = stats[:, STAT:, :].reshape(-1, LANES)
    found = gather_stats(place_row, table_cols(table_ref, ARRIVAL3, SLOT_ROWS), own_stats)
    edge = gather_stats(next_row, table_cols(next_table_ref, ARRIVAL3, SLOT_ROWS), next_stats)
    refs = (
        (six.at[0], six.at[1], six.at[2]),
        double.at[0],
        six.at[3],
        double.at[1],
        (six.at[4], six.at[5]),
    )
    leaving = []
    width = shaped.shape[2]
    for pair in range(2):
        for hash_round in range(2):
            if pair == 0:
                for copy in arriving[hash_round]:
                    copy.wait()
            backward_heads(
                pair,
                found[:, hash_round * per_round : (hash_round + 1) * per_round],
                edge[:, hash_round * GROUP : (hash_round + 1) * GROUP],
                refs,
                hash_round,
                shaped,
            )
        chunks = 2
        for chunk in range(chunks):
            kept = slice(chunk * 1024 // chunks, (chunk + 1) * 1024 // chunks)
            first = dot(back[0][kept], shaped[0]).reshape(-1, 2, STAT, width)
            second = dot(back[1][kept], shaped[1]).reshape(-1, 2, STAT, width)
            whole = jnp.concatenate(
                [first[:, :1], first[:, 1:] + second[:, :1], second[:, 1:]], axis=1
            ).reshape(-1, width)
            count = whole.shape[0]
            at = pl.ds(chunk * count, count)
            staged[pair, at] = whole.astype(jnp.bfloat16)
            leaving += started(
                [staged.at[pair, at]],
                [payload_ref.at[at, pl.ds((pair + 1) * width, width)]],
                store,
                pair * chunks + chunk,
            )
    for copy in leaving:
        copy.wait()


def backward(table, next_table, stats, heads, tail, tail_cotangent, prior_tail, nexts, payload):
    slots = SLOT_ROWS * LANES
    rows, width = heads[0].shape
    return pl.pallas_call(
        backward_body,
        in_specs=[table_spec(), pl.BlockSpec(next_table.shape, lambda *_: (0, 0))] + anywhere(10),
        out_specs=anywhere(1)[0],
        out_shape=jax.ShapeDtypeStruct((slots, 3 * width), jnp.bfloat16),
        input_output_aliases={11: 0},
        scratch_shapes=[
            pltpu.VMEM(stats.shape, jnp.float32),
            pltpu.VMEM((6, rows, width), jnp.bfloat16),
            pltpu.VMEM((2, rows, 2 * width), jnp.bfloat16),
            pltpu.VMEM((2, 2 * GROUP, width), jnp.bfloat16),
            pltpu.VMEM((2, slots, width), jnp.bfloat16),
            pltpu.SemaphoreType.DMA((17,)),
            pltpu.SemaphoreType.DMA((4,)),
        ],
        compiler_params=params(57),
        cost_estimate=cost(8e9, 1.5e7, 3e6),
        name="backward",
    )(table, next_table, stats, *heads, tail, tail_cotangent, prior_tail, *nexts, payload)


def combine_body(
    table_ref,
    share_ref,
    arrived_ref,
    out_ref,
    first_ref,
    second_ref,
    staged,
    chosen,
    store,
):
    parts, tokens, wide = staged.shape
    token = iota((tokens, 1), 0)
    code = table_row(table_ref, SEND_CODE, SLOT_ROWS)
    chosen[0] = match(token, code)
    chosen[1] = match(token + tokens, code)
    chosen[2] = match(token, table_row(table_ref, SEND, SLOT_ROWS))
    width = parts * wide // 3
    leaving = []
    for half in range(2):
        kept = slice(half * tokens // 2, (half + 1) * tokens // 2)
        at = pl.ds(half * tokens // 2, tokens // 2)
        slopes = dot(chosen[2, kept], arrived_ref[:, width:]).astype(jnp.bfloat16)
        for place in range(4):
            staged[2 + place, kept] = slopes[:, place * wide : (place + 1) * wide]
            leaving += started(
                [staged.at[2 + place, at]],
                [(first_ref, second_ref)[place % 2].at[at, pl.ds((place // 2) * wide, wide)]],
                store,
                half * parts + 2 + place,
            )
        found = 0.0
        for each in range(2):
            share = jnp.concatenate(
                [
                    jnp.broadcast_to(
                        share_ref[kept, 4 * each + head : 4 * each + head + 1], (tokens // 2, DH)
                    )
                    for head in range(4)
                ],
                axis=1,
            )
            found = found + share * dot(chosen[each, kept], arrived_ref[:, :width])
        found = found.astype(jnp.bfloat16)
        for place in range(2):
            staged[place, kept] = found[:, place * wide : (place + 1) * wide]
            leaving += started(
                [staged.at[place, at]],
                [out_ref.at[at, pl.ds(place * wide, wide)]],
                store,
                half * parts + place,
            )
    for copy in leaving:
        copy.wait()


def combine(table, shares, arrived, tokens):
    slots, width = arrived.shape
    wide = width // 6
    return pl.pallas_call(
        combine_body,
        in_specs=[table_spec(), pl.BlockSpec(shares.shape, lambda *_: (0, 0))]
        + [pl.BlockSpec(memory_space=pltpu.VMEM)],
        out_specs=anywhere(3),
        out_shape=[jax.ShapeDtypeStruct((tokens, 2 * wide), jnp.bfloat16)] * 3,
        scratch_shapes=[
            pltpu.VMEM((6, tokens, wide), jnp.bfloat16),
            pltpu.VMEM((3, tokens, slots), jnp.bfloat16),
            pltpu.SemaphoreType.DMA((12,)),
        ],
        compiler_params=params(40),
        cost_estimate=cost(2 * slots * tokens * width, 2 * (slots + tokens) * width),
        name="combine_rows",
    )(table, shares, arrived)


def per_device(query_key, value, attended_cotangent, send_rows, arrival_count, receive_slot):
    tokens, row_width = query_key.shape
    rounds = send_rows.shape[0]
    owners = lax.axis_size("seq")
    capacity = send_rows.shape[1] // owners
    per_owner = rounds * capacity
    slots = owners * per_owner

    code = (tokens * jnp.arange(rounds, dtype=jnp.int32))[:, None]
    half = lax.axis_index("head")

    def by_owner(table):
        return table.reshape(rounds, owners, capacity).transpose(1, 0, 2).reshape(owners, per_owner)

    def by_third(codes):
        return codes.reshape(owners, 3, STAT).transpose(1, 0, 2)

    def sent(packed):
        return exchange(packed.reshape(owners, per_owner, -1)).reshape(slots, -1)

    blocks = send_rows.reshape(rounds, owners, capacity)
    send_rows = jnp.where(half == 0, blocks, blocks[:, ::-1]).reshape(rounds, -1)
    send = by_owner(send_rows)
    send_blocks = send.reshape(-1, LANES)
    packed = pack(send_blocks, query_key, value, attended_cotangent)

    within = jnp.arange(capacity, dtype=jnp.int32)

    def arrivals(counts):
        start = jnp.cumsum(counts, axis=1) - counts + code
        codes = jnp.where(within < counts[:, :, None], start[:, :, None] + within, -1)
        return by_owner(codes)

    tables = to_place(jnp.concatenate([arrival_count, receive_slot], axis=1))
    arrival = arrivals(tables[:, :owners])
    place = tables[:, owners:] + code

    def half_blocks(codes, first):
        return codes[:, first : first + 2 * STAT]

    members = [
        (ARRIVAL3, by_third(arrival)),
        (PLACE, place),
        (ARRIVAL, arrival),
        (SEND, send),
        (SEND3, by_third(by_owner(send_rows + code))),
        (HALF, jnp.full((1, LANES), half, jnp.int32)),
        (FIRST16, half_blocks(arrival, 0)),
        (LAST16, half_blocks(arrival, STAT)),
        (SEND_CODE, by_owner(send_rows + code)),
    ]
    rows = [codes.reshape(-1, LANES) for _, codes in members]
    assert [at for at, _ in members] == [sum(map(len, rows[:i])) for i in range(len(rows))]
    table = jnp.concatenate(rows)
    table = jnp.pad(table, ((0, LANES - len(table)), (0, 0)), constant_values=-1)

    arrived, table = lax.optimization_barrier((sent(packed), table))
    tail = sort_tail(table, arrived, 2 * row_width)
    prior_tail = to_next(tail)
    head_query, head_value, head_cotangent, tail_cotangent, out_second, stat_second = forward_own(
        table, arrived, tail
    )
    out_first, stats = forward_edge(
        table, head_query, head_value, head_cotangent, prior_tail, stat_second
    )
    shared, stats = lax.optimization_barrier((table[:SHARED_ROWS], stats))
    next_table = to_prior(shared)
    next_query = to_prior(head_query)
    next_cotangent = to_prior(head_cotangent)
    home_stats = exchange(stats.reshape(owners, STAT, LANES)).reshape(-1, LANES)
    totals = exchange(total_stats(table, home_stats, tokens))
    payload, shares = prepare(table, home_stats, (out_first, out_second), tokens)
    payload = backward(
        table,
        next_table,
        totals,
        (head_query, head_value, head_cotangent),
        tail,
        tail_cotangent,
        prior_tail,
        (next_query, next_cotangent),
        payload,
    )
    return tuple(combine(table, shares, sent(payload), tokens))


def solution(mesh):
    in_specs = (
        P("seq", "head"),
        P("seq", "head"),
        P("seq", "head"),
        P(None, "seq"),
        P(None, "seq"),
        P(None, "seq"),
    )
    out_specs = (P("seq", "head"), P("seq", "head"), P("seq", "head"))
    return jax.shard_map(
        per_device, mesh=mesh, in_specs=in_specs, out_specs=out_specs, check_vma=False
    )
```

```python
import functools

import jax
import jax.numpy as jnp
from jax import lax
from jax.experimental import pallas as pl
from jax.experimental.pallas import tpu as pltpu
from jax.sharding import PartitionSpec as P

DH = 128
GROUP = 256
NEG_SELF = -100000.0
EPS_KEY = 1e-06
LANES = 128
STAT = 8
PIECES = 3
MIB = 1 << 20


def dot(left, right, left_axis=1, right_axis=0):
    return lax.dot_general(
        left,
        right,
        (((left_axis,), (right_axis,)), ((), ())),
        preferred_element_type=jnp.float32,
    )


def params(mib=62):
    return pltpu.CompilerParams(vmem_limit_bytes=mib * MIB)


def cost(flops, moved, exps=0):
    return pl.CostEstimate(flops=int(flops), bytes_accessed=int(moved), transcendentals=int(exps))


def routed(block, route_of):
    owners, halves = lax.axis_size("seq"), lax.axis_size("head")
    route = [
        (i * halves + half, route_of(i, half, owners) * halves + half)
        for i in range(owners)
        for half in range(halves)
    ]
    return lax.ppermute(block, ("seq", "head"), route)


def to_next(block):
    return routed(block, lambda i, half, n: (i + (1 if half == 0 else -1)) % n)


def to_prior(block):
    return routed(block, lambda i, half, n: (i - (1 if half == 0 else -1)) % n)


def to_place_prior(block):
    return routed(block, lambda i, half, n: (i - 1) % n if half == 0 else n - 1 - (i - 1) % n)


def to_place(block):
    return routed(block, lambda i, half, n: i if half == 0 else n - 1 - i)


def exchange(block):
    return lax.all_to_all(block, "seq", split_axis=0, concat_axis=0, tiled=True)


def match(left, right):
    return jnp.where(left == right, 1.0, 0.0).astype(jnp.bfloat16)


ARRIVAL3, PLACE, ARRIVAL, SEND, SEND3, HALF, FIRST16, LAST16, SEND_CODE = 0, 12, 20, 32, 44, 56, 57, 65, 73
SLOT_ROWS, PLACE_ROWS, PART_ROWS = 12, 8, 8
SHARED_ROWS = 24


def table_row(table_ref, start, count):
    return jnp.concatenate([table_ref[start + i : start + i + 1, :] for i in range(count)], axis=1)


def table_cols(table_ref, start, count):
    turned = table_ref[...].T
    return [turned[:, start + i : start + i + 1] for i in range(count)]


def match_cols(cols, row):
    return jnp.concatenate([match(col, row) for col in cols])


def anywhere(count):
    return [pl.BlockSpec(memory_space=pl.ANY) for _ in range(count)]


def table_spec():
    return pl.BlockSpec((LANES, LANES), lambda *_: (0, 0))


def started(sources, targets, sems, first=0):
    copies = [
        pltpu.make_async_copy(source, target, sems.at[first + i])
        for i, (source, target) in enumerate(zip(sources, targets))
    ]
    for copy in copies:
        copy.start()
    return copies


def iota(shape, axis):
    return lax.broadcasted_iota(jnp.int32, shape, axis)


def pieces_of(wide):
    first = wide.astype(jnp.bfloat16)
    rest = wide - first.astype(jnp.float32)
    second = rest.astype(jnp.bfloat16)
    third = (rest - second.astype(jnp.float32)).astype(jnp.bfloat16)
    return first, second, third


def unit_rows(raw_rows):
    wide = raw_rows.astype(jnp.float32)
    inverse = lax.rsqrt(jnp.sum(wide * wide, -1, keepdims=True) + EPS_KEY)
    return wide * inverse, inverse


def pack_body(index_ref, *refs):
    sources, out_ref, held, staged, chosen, load, store = refs[:3], *refs[3:]
    tokens, width = sources[0].shape
    arriving = started(sources, [held.at[i] for i in range(3)], load)
    spare = jnp.zeros((LANES - SLOT_ROWS, LANES), jnp.int32)
    turned = jnp.concatenate([index_ref[...], spare]).T
    chosen[...] = match_cols(
        [turned[:, i : i + 1] for i in range(SLOT_ROWS)], iota((LANES, tokens), 1)
    )
    steps = 4
    block = chosen.shape[0] // steps
    leaving = []
    for step in range(steps):
        rows = slice(step * block, (step + 1) * block)
        for place in range(3):
            if step == 0:
                arriving[place].wait()
            staged[rows, place * width : (place + 1) * width] = dot(
                chosen[rows], held[place]
            ).astype(jnp.bfloat16)
        leaving += started(
            [staged.at[pl.ds(step * block, block)]],
            [out_ref.at[pl.ds(step * block, block)]],
            store,
            step,
        )
    for copy in leaving:
        copy.wait()


def pack(index, *sources):
    slots = SLOT_ROWS * LANES
    tokens, width = sources[0].shape
    total = width * len(sources)
    return pl.pallas_call(
        pack_body,
        in_specs=[pl.BlockSpec(index.shape, lambda *_: (0, 0))] + anywhere(3),
        out_specs=anywhere(1)[0],
        out_shape=jax.ShapeDtypeStruct((slots, total), jnp.bfloat16),
        scratch_shapes=[
            pltpu.VMEM((3, tokens, width), jnp.bfloat16),
            pltpu.VMEM((slots, total), jnp.bfloat16),
            pltpu.VMEM((slots, tokens), jnp.bfloat16),
            pltpu.SemaphoreType.DMA((3,)),
            pltpu.SemaphoreType.DMA((4,)),
        ],
        compiler_params=params(),
        cost_estimate=cost(2 * slots * tokens * total, 2 * (slots + tokens) * total),
        name="pack_rows",
    )(index, *sources)


def place_cols(table_ref, group):
    cols = table_cols(table_ref, PLACE, PLACE_ROWS)
    each = GROUP // LANES
    first, second = group * each, PLACE_ROWS // 2 + group * each
    return cols[first : first + each], cols[second : second + each]


def tail_body(table_ref, arrived_ref, tail_ref, held, staged, chosen, load, store):
    width = held.shape[1]
    arriving = started([arrived_ref.at[:, pl.ds(0, width)]], [held], load)
    first, second = place_cols(table_ref, 1)
    row = table_row(table_ref, ARRIVAL, SLOT_ROWS)
    for i, col in enumerate(first + second):
        chosen[i * LANES : (i + 1) * LANES] = match(col, row)
    arriving[0].wait()
    leaving = []
    for i in range(2):
        staged[i * GROUP : (i + 1) * GROUP] = dot(
            chosen[i * GROUP : (i + 1) * GROUP], held[...]
        ).astype(jnp.bfloat16)
        at = pl.ds(i * GROUP, GROUP)
        leaving += started([staged.at[at]], [tail_ref.at[at]], store, i)
    for copy in leaving:
        copy.wait()


def sort_tail(table, arrived, width):
    slots = arrived.shape[0]
    wide = width // 4
    return pl.pallas_call(
        tail_body,
        in_specs=[table_spec()] + anywhere(1),
        out_specs=anywhere(1)[0],
        out_shape=jax.ShapeDtypeStruct((2 * GROUP, width), jnp.bfloat16),
        scratch_shapes=[
            pltpu.VMEM((slots, width), jnp.bfloat16),
            pltpu.VMEM((2 * GROUP, width), jnp.bfloat16),
            pltpu.VMEM((2 * GROUP, slots), jnp.bfloat16),
            pltpu.SemaphoreType.DMA((4,)),
            pltpu.SemaphoreType.DMA((4,)),
        ],
        compiler_params=params(),
        cost_estimate=cost(4 * slots * GROUP * width, 2 * (slots + 2 * GROUP) * width),
        name="sort_tail",
    )(table, arrived)


def forward_tile(query, keys, values):
    scores = dot(query, keys, 1, 1)
    own = iota((GROUP, 2 * GROUP), 1) == iota((GROUP, 2 * GROUP), 0) + GROUP
    scores = jnp.where(own, NEG_SELF, scores)
    top = jnp.max(scores, -1, keepdims=True)
    raised = jnp.exp(scores - top)
    total = jnp.sum(raised, -1, keepdims=True)
    weights = (raised * (1.0 / total)).astype(jnp.bfloat16)
    return dot(weights, values), top + jnp.log(total)


def forward_pair(pair, query, raw, values, cotangent, out_ref):
    lane = iota((GROUP, LANES), 1) % STAT
    stat = jnp.zeros((GROUP, LANES), jnp.float32)
    for local in range(2):
        columns = slice(local * DH, (local + 1) * DH)
        keys = unit_rows(raw[:, columns])[0].astype(jnp.bfloat16)
        partial, lse = forward_tile(query[:, columns], keys, values[:, columns])
        out_ref[:, columns] = partial.astype(jnp.bfloat16)
        delta = jnp.sum(partial * cotangent[:, columns].astype(jnp.float32), -1, keepdims=True)
        head = pair * 2 + local
        stat = jnp.where(lane == head, lse, jnp.where(lane == head + 4, delta, stat))
    return stat


def own_body(
    table_ref,
    arrived_query_ref,
    arrived_value_ref,
    arrived_cotangent_ref,
    tail_query_ref,
    tail_value_ref,
    head_query_ref,
    head_value_ref,
    head_cotangent_ref,
    tail_cotangent_ref,
    out_ref,
    stat_ref,
    chosen,
):
    pair = pl.program_id(0)
    hash_round = pl.program_id(1)

    @pl.when((pair == 0) & (hash_round == 0))
    def _():
        row = table_row(table_ref, ARRIVAL, SLOT_ROWS)
        heads, tails = place_cols(table_ref, 0), place_cols(table_ref, 1)
        for each in range(2):
            chosen[each] = match_cols(heads[each] + tails[each], row)

    select_head = chosen[hash_round, :GROUP]
    query = dot(select_head, arrived_query_ref[...]).astype(jnp.bfloat16)
    value = dot(select_head, arrived_value_ref[...]).astype(jnp.bfloat16)
    cotangent = dot(chosen[hash_round], arrived_cotangent_ref[...]).astype(jnp.bfloat16)
    head_query_ref[...] = query
    head_value_ref[...] = value
    head_cotangent_ref[...] = cotangent[:GROUP]
    tail_cotangent_ref[...] = cotangent[GROUP:]
    stat_ref[...] = forward_pair(
        pair,
        tail_query_ref[...],
        jnp.concatenate([query, tail_query_ref[...]]),
        jnp.concatenate([value, tail_value_ref[...]]),
        cotangent[GROUP:],
        out_ref,
    )


def group_spec(offset=0):
    return pl.BlockSpec((GROUP, 2 * DH), lambda p, r: (r, p + offset))


def stat_spec():
    return pl.BlockSpec((GROUP, LANES), lambda p, r: (r, p))


def forward_own(table, arrived, tail):
    slots, width = arrived.shape
    wide = width // 6
    rows = 2 * GROUP
    array = jax.ShapeDtypeStruct((rows, width // 3), jnp.bfloat16)
    return pl.pallas_call(
        own_body,
        grid=(2, 2),
        in_specs=[pl.BlockSpec((LANES, LANES), lambda p, r: (0, 0))]
        + [pl.BlockSpec((slots, wide), lambda p, r, k=k: (0, p + 2 * k)) for k in range(3)]
        + [group_spec(), group_spec(2)],
        out_specs=[group_spec()] * 5 + [stat_spec()],
        out_shape=[array] * 4
        + [
            jax.ShapeDtypeStruct((rows, width // 3), jnp.bfloat16),
            jax.ShapeDtypeStruct((rows, 2 * LANES), jnp.float32),
        ],
        scratch_shapes=[pltpu.VMEM((2, 2 * GROUP, slots), jnp.bfloat16)],
        compiler_params=params(),
        cost_estimate=cost(5e9, 1e7, 8 * GROUP * 512),
        name="forward_own",
    )(table, arrived, arrived, arrived, tail, tail)


def edge_body(
    table_ref,
    query_ref,
    value_ref,
    cotangent_ref,
    prior_ref,
    second_stat_ref,
    out_ref,
    stats_ref,
    three,
    prior,
    second_stat,
    staged,
    both,
    load,
    store,
):
    each = [pl.ds(hash_round * GROUP, GROUP) for hash_round in range(2)]
    arriving = [
        started(
            [source.at[at] for source in (query_ref, prior_ref, value_ref, cotangent_ref)],
            [three.at[0, at], prior.at[at], three.at[1, at], three.at[2, at]],
            load,
            4 * hash_round,
        )
        for hash_round, at in enumerate(each)
    ]
    arriving[1] += started([second_stat_ref], [second_stat], load, 8)
    place_row = table_row(table_ref, PLACE, PLACE_ROWS)
    arrival_cols = table_cols(table_ref, ARRIVAL3, SLOT_ROWS)
    width = staged.shape[1]
    leaving = []
    for hash_round in range(2):
        kept = slice(hash_round * GROUP, (hash_round + 1) * GROUP)
        at = each[hash_round]
        for copy in arriving[hash_round]:
            copy.wait()
        stat = 0.0
        for pair in range(2):
            columns = slice(pair * 2 * DH, (pair + 1) * 2 * DH)
            values_at = slice(width + pair * 2 * DH, width + (pair + 1) * 2 * DH)
            query = three[0, kept, columns]
            stat = stat + forward_pair(
                pair,
                query,
                jnp.concatenate([prior[kept, columns], query]),
                jnp.concatenate([prior[kept, values_at], three[1, kept, columns]]),
                three[2, kept, columns],
                staged.at[at, pl.ds(pair * 2 * DH, 2 * DH)],
            )
        leaving += started([staged.at[at]], [out_ref.at[at]], store, hash_round)
        both[2 * hash_round * GROUP : (2 * hash_round + 1) * GROUP] = stat
    for hash_round in range(2):
        kept = slice(hash_round * GROUP, (hash_round + 1) * GROUP)
        both[(2 * hash_round + 1) * GROUP : (2 * hash_round + 2) * GROUP] = (
            second_stat[kept, :LANES] + second_stat[kept, LANES:]
        )
    rows = 4 * GROUP
    piece = iota((rows, LANES), 1) // (PIECES * STAT)
    first, second, third = pieces_of(both[...])
    nothing = jnp.zeros((rows, LANES), jnp.bfloat16)
    stats = jnp.where(
        piece == 0,
        first,
        jnp.where(piece == 1, second, jnp.where(piece == 2, third, nothing)),
    )
    third_slots = stats_ref.shape[0]
    lane_third = (iota((third_slots, LANES), 1) % (3 * STAT)) // STAT
    result = jnp.zeros((third_slots, LANES), jnp.float32)
    for third in range(3):
        span = slice((0, 0, rows // 2)[third], (rows // 2, rows, rows)[third])
        back = match_cols(arrival_cols[4 * third : 4 * third + 4], place_row[:, span])
        result = jnp.where(lane_third == third, dot(back, stats[span]), result)
    stats_ref[...] = result
    for copy in leaving:
        copy.wait()


def forward_edge(table, query, value, cotangent, prior_tail, second_stat):
    rows, width = query.shape
    third_slots = SLOT_ROWS * LANES // 3
    return pl.pallas_call(
        edge_body,
        in_specs=[table_spec()] + anywhere(5),
        out_specs=anywhere(1) + [pl.BlockSpec(memory_space=pltpu.VMEM)],
        out_shape=[
            jax.ShapeDtypeStruct((rows, width), jnp.bfloat16),
            jax.ShapeDtypeStruct((third_slots, LANES), jnp.float32),
        ],
        scratch_shapes=[
            pltpu.VMEM((3, rows, width), jnp.bfloat16),
            pltpu.VMEM((rows, 2 * width), jnp.bfloat16),
            pltpu.VMEM((rows, 2 * LANES), jnp.float32),
            pltpu.VMEM((rows, width), jnp.bfloat16),
            pltpu.VMEM((2 * rows, LANES), jnp.float32),
            pltpu.SemaphoreType.DMA((9,)),
            pltpu.SemaphoreType.DMA((2,)),
        ],
        compiler_params=params(59),
        cost_estimate=cost(2e9, 4e6, 8 * GROUP * 512),
        name="forward_edge",
    )(table, query, value, cotangent, prior_tail, second_stat)


def gather_stats(codes_row, slot_cols, stats):
    narrow = stats.astype(jnp.bfloat16)
    half = codes_row.shape[1] // 2
    sums = [0.0, 0.0]
    for third in range(3):
        for each in ((0,), (0, 1), (1,))[third]:
            codes = codes_row[:, each * half : (each + 1) * half]
            chosen = match_cols(slot_cols[4 * third : 4 * third + 4], codes)
            found = dot(narrow, chosen, 0, 0)
            for piece in range(PIECES):
                at = piece * PIECES * STAT + third * STAT
                sums[each] = sums[each] + found[at : at + STAT]
    return jnp.concatenate(sums, axis=1)


def found_at_tokens(tokens, table_ref, stats):
    slot_cols = table_cols(table_ref, SEND3, SLOT_ROWS)
    found = gather_stats(iota((1, 2 * tokens), 1), slot_cols, stats)
    lse_first, lse_second = found[:4, :tokens], found[:4, tokens:]
    top = jnp.maximum(lse_first, lse_second)
    total = top + jnp.log(jnp.exp(lse_first - top) + jnp.exp(lse_second - top))
    shares = jnp.exp(lse_first - total), jnp.exp(lse_second - total)
    delta = found[4:, :tokens] * shares[0] + found[4:, tokens:] * shares[1]
    return slot_cols, total, delta, shares


def total_body(tokens, table_ref, arrived_ref, out_ref):
    slot_cols, total, delta, _ = found_at_tokens(tokens, table_ref, arrived_ref[...])
    stat = jnp.concatenate([total, delta])
    first, second, third_piece = [member.astype(jnp.float32) for member in pieces_of(stat)]
    spare = jnp.zeros((LANES - 9 * STAT, tokens), jnp.float32)
    table = jnp.concatenate(
        [first] * 3 + [second] * 3 + [third_piece] * 3 + [spare]
    ).astype(jnp.bfloat16)
    third_slots = arrived_ref.shape[0]
    lane_third = (iota((third_slots, LANES), 1) % (3 * STAT)) // STAT
    result = jnp.zeros((third_slots, LANES), jnp.float32)
    for third in range(3):
        codes = slot_cols[4 * third : 4 * third + 4]
        cols = [jnp.where(code >= tokens, code - tokens, code) for code in codes]
        chosen = match_cols(cols, iota((LANES, tokens), 1))
        result = jnp.where(lane_third == third, dot(chosen, table, 1, 1), result)
    owners = third_slots // STAT
    by_owner = result.reshape(owners, STAT, LANES)
    out_ref[:, :STAT, :] = by_owner
    above = jnp.concatenate([by_owner[1:], by_owner[:1]])
    below = jnp.concatenate([by_owner[owners - 1 :], by_owner[: owners - 1]])
    half = table_ref[HALF : HALF + 1, :]
    out_ref[:, STAT:, :] = jnp.where(half[None] == 0, above, below)


def total_stats(table, arrived, tokens):
    owners = arrived.shape[0] // STAT
    return pl.pallas_call(
        functools.partial(total_body, tokens),
        out_shape=jax.ShapeDtypeStruct((owners, 2 * STAT, LANES), jnp.float32),
        compiler_params=params(24),
        cost_estimate=cost(2 * 1536 * 1536 * LANES, 1 << 20),
        name="total_stats",
    )(table, arrived)


def prepare_body(tokens, table_ref, arrived_ref, first_ref, second_ref, payload_ref, share_ref):
    @pl.when(pl.program_id(0) == 0)
    def _():
        shares = found_at_tokens(tokens, table_ref, arrived_ref[...])[3]
        spare = jnp.zeros((LANES - STAT, tokens), jnp.float32)
        share_ref[...] = jnp.concatenate([*shares, spare]).T

    back = match_cols(
        table_cols(table_ref, ARRIVAL, SLOT_ROWS), table_row(table_ref, PLACE, PLACE_ROWS)
    )
    rows = [first_ref[:GROUP], second_ref[:GROUP], first_ref[GROUP:], second_ref[GROUP:]]
    payload_ref[...] = dot(back, jnp.concatenate(rows)).astype(jnp.bfloat16)


def prepare(table, home_stats, outs, tokens):
    slots = SLOT_ROWS * LANES
    rows, width = outs[0].shape
    wide = width // 2
    return pl.pallas_call(
        functools.partial(prepare_body, tokens),
        grid=(2,),
        in_specs=[
            table_spec(),
            pl.BlockSpec(home_stats.shape, lambda i: (0, 0)),
            pl.BlockSpec((rows, wide), lambda i: (0, i)),
            pl.BlockSpec((rows, wide), lambda i: (0, i)),
        ],
        out_specs=[
            pl.BlockSpec((slots, wide), lambda i: (0, i)),
            pl.BlockSpec((tokens, LANES), lambda i: (0, 0)),
        ],
        out_shape=[
            jax.ShapeDtypeStruct((slots, 3 * width), jnp.bfloat16),
            jax.ShapeDtypeStruct((tokens, LANES), jnp.float32),
        ],
        compiler_params=params(62),
        cost_estimate=cost(2e9, 1e7),
        name="prepare_outputs",
    )(table, home_stats, *outs)


def backward_tile(query, upstream, keys, values, masked, total_row, delta_row):
    scores = dot(keys, query, 1, 1)
    if masked is not None:
        low, high = scores[:LANES], scores[LANES:]
        low = jnp.concatenate(
            [jnp.where(masked, NEG_SELF, low[:, :LANES]), low[:, LANES:]], axis=1
        )
        high = jnp.concatenate(
            [
                high[:, :LANES],
                jnp.where(masked, NEG_SELF, high[:, LANES : 2 * LANES]),
                high[:, 2 * LANES :],
            ],
            axis=1,
        )
        scores = jnp.concatenate([low, high])
    probs = jnp.exp(scores - total_row)
    dots = dot(values, upstream, 1, 1)
    slopes = (probs * (dots - delta_row)).astype(jnp.bfloat16)
    return probs.astype(jnp.bfloat16), slopes


def backward_heads(pair, stat, edge_stat, refs, hash_round, shaped):
    heads, tail, tail_cotangent, prior, nexts = refs
    kept = pl.ds(hash_round * GROUP, GROUP)
    own = iota((LANES, LANES), 0) == iota((LANES, LANES), 1)
    width = tail.shape[1] // 2
    for local in range(2):
        head = pair * 2 + local
        columns = pl.ds(head * DH, DH)
        values_at = pl.ds(width + head * DH, DH)
        total_row, delta_row = stat[head : head + 1], stat[head + 4 : head + 5]
        edge_total, edge_delta = edge_stat[head : head + 1], edge_stat[head + 4 : head + 5]
        raw = jnp.concatenate([heads[0][kept, columns], tail[kept, columns]])
        values = jnp.concatenate([heads[1][kept, columns], tail[kept, values_at]])
        upstream = jnp.concatenate([heads[2][kept, columns], tail_cotangent[kept, columns]])
        units, inverse = unit_rows(raw)
        keys = units.astype(jnp.bfloat16)
        prior_keys = unit_rows(prior[kept, columns])[0].astype(jnp.bfloat16)
        _, prior_slopes = backward_tile(
            raw[:GROUP],
            upstream[:GROUP],
            prior_keys,
            prior[kept, values_at],
            None,
            total_row[:, :GROUP],
            delta_row[:, :GROUP],
        )
        first_probs, first_slopes = backward_tile(
            raw, upstream, keys[:GROUP], values[:GROUP], own, total_row, delta_row
        )
        second_raw = jnp.concatenate([raw[GROUP:], nexts[0][kept, columns]])
        second_upstream = jnp.concatenate([upstream[GROUP:], nexts[1][kept, columns]])
        second_probs, second_slopes = backward_tile(
            second_raw,
            second_upstream,
            keys[GROUP:],
            values[GROUP:],
            own,
            jnp.concatenate([total_row[:, GROUP:], edge_total], axis=1),
            jnp.concatenate([delta_row[:, GROUP:], edge_delta], axis=1),
        )
        query_slope = jnp.concatenate(
            [
                dot(
                    jnp.concatenate([prior_keys, keys[:GROUP]]),
                    jnp.concatenate([prior_slopes, first_slopes[:, :GROUP]]),
                    0,
                    0,
                ).T,
                dot(
                    keys,
                    jnp.concatenate([first_slopes[:, GROUP:], second_slopes[:, :GROUP]]),
                    0,
                    0,
                ).T,
            ]
        )
        unit_slope = jnp.concatenate([dot(first_slopes, raw), dot(second_slopes, second_raw)])
        value_slope = jnp.concatenate(
            [dot(first_probs, upstream), dot(second_probs, second_upstream)]
        )
        key_slope = inverse * (
            unit_slope - units * jnp.sum(units * unit_slope, -1, keepdims=True)
        )
        shaped[hash_round, :, local * DH : (local + 1) * DH] = (query_slope + key_slope).astype(
            jnp.bfloat16
        )
        shaped[hash_round, :, (2 + local) * DH : (3 + local) * DH] = value_slope.astype(
            jnp.bfloat16
        )


def backward_body(
    table_ref,
    next_table_ref,
    stats_ref,
    head_query_ref,
    head_value_ref,
    head_cotangent_ref,
    tail_ref,
    tail_cotangent_ref,
    prior_ref,
    next_query_ref,
    next_cotangent_ref,
    _,
    payload_ref,
    stats,
    six,
    double,
    shaped,
    staged,
    load,
    store,
):
    rows = PLACE_ROWS * LANES
    per_round = rows // 2
    sources = [
        head_query_ref,
        head_value_ref,
        head_cotangent_ref,
        tail_cotangent_ref,
        next_query_ref,
        next_cotangent_ref,
        tail_ref,
        prior_ref,
    ]
    targets = [six.at[i] for i in range(6)] + [double.at[i] for i in range(2)]
    (stats_copy,) = started([stats_ref], [stats], load)
    arriving = []
    for each in range(2):
        at = pl.ds(each * GROUP, GROUP)
        arriving.append(
            started(
                [source.at[at] for source in sources],
                [target.at[at] for target in targets],
                load,
                1 + each * len(sources),
            )
        )
    place_row = table_row(table_ref, PLACE, PLACE_ROWS)
    next_places = table_row(next_table_ref, PLACE, PLACE_ROWS)
    next_row = jnp.concatenate(
        [next_places[:, each * per_round : each * per_round + GROUP] for each in range(2)], axis=1
    )
    back = [
        match_cols(
            table_cols(table_ref, (FIRST16, LAST16)[each], PART_ROWS),
            place_row[:, each * per_round : (each + 1) * per_round],
        )
        for each in range(2)
    ]
    stats_copy.wait()
    own_stats = stats[:, :STAT, :].reshape(-1, LANES)
    next_stats = stats[:, STAT:, :].reshape(-1, LANES)
    found = gather_stats(place_row, table_cols(table_ref, ARRIVAL3, SLOT_ROWS), own_stats)
    edge = gather_stats(next_row, table_cols(next_table_ref, ARRIVAL3, SLOT_ROWS), next_stats)
    refs = (
        (six.at[0], six.at[1], six.at[2]),
        double.at[0],
        six.at[3],
        double.at[1],
        (six.at[4], six.at[5]),
    )
    leaving = []
    width = shaped.shape[2]
    for pair in range(2):
        for hash_round in range(2):
            if pair == 0:
                for copy in arriving[hash_round]:
                    copy.wait()
            backward_heads(
                pair,
                found[:, hash_round * per_round : (hash_round + 1) * per_round],
                edge[:, hash_round * GROUP : (hash_round + 1) * GROUP],
                refs,
                hash_round,
                shaped,
            )
        chunks = 2
        for chunk in range(chunks):
            kept = slice(chunk * 1024 // chunks, (chunk + 1) * 1024 // chunks)
            first = dot(back[0][kept], shaped[0]).reshape(-1, 2, STAT, width)
            second = dot(back[1][kept], shaped[1]).reshape(-1, 2, STAT, width)
            whole = jnp.concatenate(
                [first[:, :1], first[:, 1:] + second[:, :1], second[:, 1:]], axis=1
            ).reshape(-1, width)
            count = whole.shape[0]
            at = pl.ds(chunk * count, count)
            staged[pair, at] = whole.astype(jnp.bfloat16)
            leaving += started(
                [staged.at[pair, at]],
                [payload_ref.at[at, pl.ds((pair + 1) * width, width)]],
                store,
                pair * chunks + chunk,
            )
    for copy in leaving:
        copy.wait()


def backward(table, next_table, stats, heads, tail, tail_cotangent, prior_tail, nexts, payload):
    slots = SLOT_ROWS * LANES
    rows, width = heads[0].shape
    return pl.pallas_call(
        backward_body,
        in_specs=[table_spec(), pl.BlockSpec(next_table.shape, lambda *_: (0, 0))] + anywhere(10),
        out_specs=anywhere(1)[0],
        out_shape=jax.ShapeDtypeStruct((slots, 3 * width), jnp.bfloat16),
        input_output_aliases={11: 0},
        scratch_shapes=[
            pltpu.VMEM(stats.shape, jnp.float32),
            pltpu.VMEM((6, rows, width), jnp.bfloat16),
            pltpu.VMEM((2, rows, 2 * width), jnp.bfloat16),
            pltpu.VMEM((2, 2 * GROUP, width), jnp.bfloat16),
            pltpu.VMEM((2, slots, width), jnp.bfloat16),
            pltpu.SemaphoreType.DMA((17,)),
            pltpu.SemaphoreType.DMA((4,)),
        ],
        compiler_params=params(57),
        cost_estimate=cost(8e9, 1.5e7, 3e6),
        name="backward",
    )(table, next_table, stats, *heads, tail, tail_cotangent, prior_tail, *nexts, payload)


def combine_body(
    table_ref,
    share_ref,
    arrived_ref,
    out_ref,
    first_ref,
    second_ref,
    staged,
    chosen,
    store,
):
    parts, tokens, wide = staged.shape
    token = iota((tokens, 1), 0)
    code = table_row(table_ref, SEND_CODE, SLOT_ROWS)
    chosen[0] = match(token, code)
    chosen[1] = match(token + tokens, code)
    chosen[2] = match(token, table_row(table_ref, SEND, SLOT_ROWS))
    width = parts * wide // 3
    leaving = []
    for half in range(2):
        kept = slice(half * tokens // 2, (half + 1) * tokens // 2)
        at = pl.ds(half * tokens // 2, tokens // 2)
        slopes = dot(chosen[2, kept], arrived_ref[:, width:]).astype(jnp.bfloat16)
        for place in range(4):
            staged[2 + place, kept] = slopes[:, place * wide : (place + 1) * wide]
            leaving += started(
                [staged.at[2 + place, at]],
                [(first_ref, second_ref)[place % 2].at[at, pl.ds((place // 2) * wide, wide)]],
                store,
                half * parts + 2 + place,
            )
        found = 0.0
        for each in range(2):
            share = jnp.concatenate(
                [
                    jnp.broadcast_to(
                        share_ref[kept, 4 * each + head : 4 * each + head + 1], (tokens // 2, DH)
                    )
                    for head in range(4)
                ],
                axis=1,
            )
            found = found + share * dot(chosen[each, kept], arrived_ref[:, :width])
        found = found.astype(jnp.bfloat16)
        for place in range(2):
            staged[place, kept] = found[:, place * wide : (place + 1) * wide]
            leaving += started(
                [staged.at[place, at]],
                [out_ref.at[at, pl.ds(place * wide, wide)]],
                store,
                half * parts + place,
            )
    for copy in leaving:
        copy.wait()


def combine(table, shares, arrived, tokens):
    slots, width = arrived.shape
    wide = width // 6
    return pl.pallas_call(
        combine_body,
        in_specs=[table_spec(), pl.BlockSpec(shares.shape, lambda *_: (0, 0))]
        + [pl.BlockSpec(memory_space=pltpu.VMEM)],
        out_specs=anywhere(3),
        out_shape=[jax.ShapeDtypeStruct((tokens, 2 * wide), jnp.bfloat16)] * 3,
        scratch_shapes=[
            pltpu.VMEM((6, tokens, wide), jnp.bfloat16),
            pltpu.VMEM((3, tokens, slots), jnp.bfloat16),
            pltpu.SemaphoreType.DMA((12,)),
        ],
        compiler_params=params(40),
        cost_estimate=cost(2 * slots * tokens * width, 2 * (slots + tokens) * width),
        name="combine_rows",
    )(table, shares, arrived)


def per_device(query_key, value, attended_cotangent, send_rows, arrival_count, receive_slot):
    tokens, row_width = query_key.shape
    rounds = send_rows.shape[0]
    owners = lax.axis_size("seq")
    capacity = send_rows.shape[1] // owners
    per_owner = rounds * capacity
    slots = owners * per_owner

    code = (tokens * jnp.arange(rounds, dtype=jnp.int32))[:, None]
    half = lax.axis_index("head")

    def by_owner(table):
        return table.reshape(rounds, owners, capacity).transpose(1, 0, 2).reshape(owners, per_owner)

    def by_third(codes):
        return codes.reshape(owners, 3, STAT).transpose(1, 0, 2)

    def sent(packed):
        return exchange(packed.reshape(owners, per_owner, -1)).reshape(slots, -1)

    blocks = send_rows.reshape(rounds, owners, capacity)
    send_rows = jnp.where(half == 0, blocks, blocks[:, ::-1]).reshape(rounds, -1)
    send = by_owner(send_rows)
    send_blocks = send.reshape(-1, LANES)
    packed = pack(send_blocks, query_key, value, attended_cotangent)

    within = jnp.arange(capacity, dtype=jnp.int32)

    def arrivals(counts):
        start = jnp.cumsum(counts, axis=1) - counts + code
        codes = jnp.where(within < counts[:, :, None], start[:, :, None] + within, -1)
        return by_owner(codes)

    tables = to_place(jnp.concatenate([arrival_count, receive_slot], axis=1))
    arrival = arrivals(tables[:, :owners])
    place = tables[:, owners:] + code

    def half_blocks(codes, first):
        return codes[:, first : first + 2 * STAT]

    members = [
        (ARRIVAL3, by_third(arrival)),
        (PLACE, place),
        (ARRIVAL, arrival),
        (SEND, send),
        (SEND3, by_third(by_owner(send_rows + code))),
        (HALF, jnp.full((1, LANES), half, jnp.int32)),
        (FIRST16, half_blocks(arrival, 0)),
        (LAST16, half_blocks(arrival, STAT)),
        (SEND_CODE, by_owner(send_rows + code)),
    ]
    rows = [codes.reshape(-1, LANES) for _, codes in members]
    assert [at for at, _ in members] == [sum(map(len, rows[:i])) for i in range(len(rows))]
    table = jnp.concatenate(rows)
    table = jnp.pad(table, ((0, LANES - len(table)), (0, 0)), constant_values=-1)

    arrived, table = lax.optimization_barrier((sent(packed), table))
    tail = sort_tail(table, arrived, 2 * row_width)
    prior_tail = to_next(tail)
    head_query, head_value, head_cotangent, tail_cotangent, out_second, stat_second = forward_own(
        table, arrived, tail
    )
    out_first, stats = forward_edge(
        table, head_query, head_value, head_cotangent, prior_tail, stat_second
    )
    shared, stats = lax.optimization_barrier((table[:SHARED_ROWS], stats))
    next_table = to_prior(shared)
    home_stats = exchange(stats.reshape(owners, STAT, LANES)).reshape(-1, LANES)
    home_stats, for_query, for_cotangent = lax.optimization_barrier(
        (home_stats, head_query, head_cotangent)
    )
    next_query = to_prior(for_query)
    next_cotangent = to_prior(for_cotangent)
    totals = exchange(total_stats(table, home_stats, tokens))
    payload, shares = prepare(table, home_stats, (out_first, out_second), tokens)
    payload = backward(
        table,
        next_table,
        totals,
        (head_query, head_value, head_cotangent),
        tail,
        tail_cotangent,
        prior_tail,
        (next_query, next_cotangent),
        payload,
    )
    return tuple(combine(table, shares, sent(payload), tokens))


def solution(mesh):
    in_specs = (
        P("seq", "head"),
        P("seq", "head"),
        P("seq", "head"),
        P(None, "seq"),
        P(None, "seq"),
        P(None, "seq"),
    )
    out_specs = (P("seq", "head"), P("seq", "head"), P("seq", "head"))
    return jax.shard_map(
        per_device, mesh=mesh, in_specs=in_specs, out_specs=out_specs, check_vma=False
    )
```
